128 devices in a mesh: seq: 16 (over z, y), head: 8 (over x, core).
Axes of the slice: x: 4, y: 4, z: 4, core: 2. Of those that a mesh axis runs over, the one named last changes fastest.
Arguments:
- video_query: bfloat16 [4096, 3072], P(('seq', 'head')), may hold values from -5 to 5
- video_key: bfloat16 [4096, 3072], P(('seq', 'head')), may hold values from -5 to 5
- video_value: bfloat16 [4096, 3072], P(('seq', 'head')), may hold values from -6 to 6
- video_grad: bfloat16 [4096, 3072], P(('seq', 'head')), may hold values from -6 to 6
- text_query: bfloat16 [2048, 3072], P('seq', 'head'), may hold values from -5 to 5
- text_key: bfloat16 [2048, 3072], P('seq', 'head'), may hold values from -5 to 5
- text_value: bfloat16 [2048, 3072], P('seq', 'head'), may hold values from -6 to 6
- text_grad: bfloat16 [2048, 3072], P('seq', 'head'), may hold values from -6 to 6
- shot_length: int32 [8], replicated, may hold values from 1 to 2048, 4096 in all
- caption_length: int32 [8], replicated, may hold values from 64 to 256, as said below
Outputs:
- video_query_grad: bfloat16 [4096, 3072], P(('seq', 'head'))
- video_key_grad: bfloat16 [4096, 3072], P(('seq', 'head'))
- video_value_grad: bfloat16 [4096, 3072], P(('seq', 'head'))
- text_query_grad: bfloat16 [2048, 3072], P('seq', 'head')
- text_key_grad: bfloat16 [2048, 3072], P('seq', 'head')
- text_value_grad: bfloat16 [2048, 3072], P('seq', 'head')
The draws below stay inside these ranges and needn't reach their ends.
Inputs may be any that keep to these rules, and one draw needn't show every extreme that they name: `shot_length`: the shots cover the video in order; exactly one length equals 2048. `caption_length`: some shot has all 256 caption tokens live.
All inputs are finite; a program needn't handle non-finite values.
Results may differ from the reference program's by a relative error of at most 0.012.
The reference program's roundings to bfloat16 on the way count: a program that leaves them out, or rounds other values in their place, can miss the bound.
Values may be sent and summed in bfloat16 or wider, within the bound.
No kernel may reach another device: no remote copies, remote signals or barrier semaphores. Data moves between devices by JAX's collectives and lax.ppermute only.
A program may use at most 128 MiB of HBM per device.

```python
import math
import jax
import jax.numpy as jnp
import numpy as np
from jax import lax

HEADS = 24
HDIM = 128
NSHOT = 8
CAP = 256
WIDTH = 3072
VIDEO = 4096
TEXT = 2048


def drawn_rows(key, count):
    return jnp.clip(jax.random.normal(key, (count, WIDTH), jnp.float32), -5.0, 5.0)


def draw_video_query(key, part):
    key = jax.random.fold_in(key, 1)
    return drawn_rows(key, VIDEO).astype(jnp.bfloat16)


def draw_video_key(key, part):
    key = jax.random.fold_in(key, 2)
    return drawn_rows(key, VIDEO).astype(jnp.bfloat16)


def draw_text_query(key, part):
    key = jax.random.fold_in(key, 3)
    return drawn_rows(key, TEXT).astype(jnp.bfloat16)


def draw_text_key(key, part):
    key = jax.random.fold_in(key, 4)
    return drawn_rows(key, TEXT).astype(jnp.bfloat16)


def draw_caption_length(key, part):
    key = jax.random.fold_in(key, 5)
    lengths = jax.random.randint(key, (NSHOT,), CAP // 4, CAP + 1)
    chosen = jax.random.randint(jax.random.fold_in(key, 1), (), 0, NSHOT)
    return jnp.where(jnp.arange(NSHOT) == chosen, CAP, lengths).astype(jnp.int32)


def block_scale(stream_key, dims, shards, least, largest):
    factor_of, own = 1.0, jax.random.fold_in(stream_key, 6)
    for axis_at, shards_of in shards:
        steps = jnp.exp(jax.random.uniform(jax.random.fold_in(own, axis_at), (shards_of,), jnp.float32, least / len(shards), largest / len(shards)))
        factor_of = factor_of * jnp.repeat(steps, dims[axis_at] // shards_of).reshape([-1 if axis == axis_at else 1 for axis in range(len(dims))])
    return factor_of


def profile(count, total, bound, lean):
    portions = [(1 << 20) // math.isqrt(rank ** lean) + 1 for rank in range(2, count + 1)]
    surplus, given = total - bound - (count - 1), [1] * (count - 1)
    while surplus > 0:
        candidates = [i for i in range(count - 1) if given[i] < bound]
        mass, budget = sum([portions[i] for i in candidates]), surplus
        for i in candidates:
            more = min(bound - given[i], max(1, budget * portions[i] // mass), surplus)
            given[i] = given[i] + more
            surplus = surplus - more
    return np.array([bound] + given)


def ragged_sizes(rng, amount, total, most, lean):
    if amount == 2:
        one = jax.random.randint(rng, (), max(1, total - most), min(most, total - 1) + 1)
        return jnp.stack([one, total - one])
    sizes = jnp.asarray(profile(amount, total, most, lean), jnp.int32)
    couples = (amount - 1) // 2
    source_of, sink = sizes[1:1 + 2 * couples:2], sizes[2:2 + 2 * couples:2]
    slack = jnp.minimum(source_of - 1, most - sink)
    moved = jax.random.randint(jax.random.fold_in(rng, 1), (couples,), 0, 1 << 20) % (slack + 1)
    sizes = sizes.at[1:1 + 2 * couples:2].set(source_of - moved).at[2:2 + 2 * couples:2].set(sink + moved)
    return sizes[jax.random.permutation(jax.random.fold_in(rng, 2), amount)]


def noise(own_key, dims, spread, reach, cuts=(), kind=jnp.bfloat16):
    entries = spread * jax.random.normal(own_key, dims, jnp.float32)
    if cuts:
        entries = entries * block_scale(own_key, dims, cuts, -0.22, 0.18)
    return jnp.clip(entries, -reach, reach).astype(kind)


def setup_inputs(seed: int = 0) -> dict:
    splits = jax.random.split(jax.random.key(seed), 11)
    video_query = draw_video_query(jax.random.fold_in(splits[10], 71), 0)
    video_key = draw_video_key(jax.random.fold_in(splits[10], 71), 0)
    video_value = noise(splits[2], (VIDEO, WIDTH), 1.0, 6.0, ((0, 128),))
    video_grad = noise(splits[3], (VIDEO, WIDTH), 1.0, 6.0, ((0, 128),))
    text_query = draw_text_query(jax.random.fold_in(splits[10], 71), 0)
    text_key = draw_text_key(jax.random.fold_in(splits[10], 71), 0)
    text_value = noise(splits[6], (TEXT, WIDTH), 1.0, 6.0, ((0, 16), (1, 8)))
    text_grad = noise(splits[7], (TEXT, WIDTH), 1.0, 6.0, ((0, 16), (1, 8)))
    shot_length = ragged_sizes(splits[8], NSHOT, VIDEO, VIDEO // 2, 2).astype(jnp.int32)
    caption_length = draw_caption_length(jax.random.fold_in(splits[10], 71), 0)
    return {"video_query": video_query, "video_key": video_key, "video_value": video_value, "video_grad": video_grad, "text_query": text_query, "text_key": text_key, "text_value": text_value, "text_grad": text_grad, "shot_length": shot_length, "caption_length": caption_length}


def reference(video_query, video_key, video_value, video_grad, text_query, text_key, text_value, text_grad, shot_length, caption_length):
    ends = jnp.cumsum(shot_length).astype(jnp.int32)
    video_rows = jnp.arange(VIDEO, dtype=jnp.int32)
    video_shot = jnp.sum((video_rows[:, None] >= ends[None, :]).astype(jnp.int32), axis=1).astype(jnp.int32)
    text_rows = jnp.arange(TEXT, dtype=jnp.int32)
    text_shot = (text_rows // CAP).astype(jnp.int32)
    text_live = (text_rows % CAP) < caption_length[text_shot]
    shot_id = jnp.concatenate([video_shot, text_shot])
    is_text = jnp.concatenate([jnp.zeros((VIDEO,), bool), jnp.ones((TEXT,), bool)])
    is_live = jnp.concatenate([jnp.ones((VIDEO,), bool), text_live])
    both_video = jnp.logical_and(jnp.logical_not(is_text)[:, None], jnp.logical_not(is_text)[None, :])
    same_shot = shot_id[:, None] == shot_id[None, :]
    allowed = jnp.logical_and(is_live[None, :], jnp.logical_or(both_video, same_shot))
    grads_text = jnp.where(text_live[:, None], text_grad, jnp.zeros_like(text_grad))
    queries = jnp.concatenate([video_query, text_query], 0)
    keys = jnp.concatenate([video_key, text_key], 0)
    values = jnp.concatenate([video_value, text_value], 0)
    grads = jnp.concatenate([video_grad, grads_text], 0)
    scale = HDIM ** -0.5

    def one_head(index):
        start = index * HDIM
        head_queries = lax.dynamic_slice_in_dim(queries, start, HDIM, 1)
        head_keys = lax.dynamic_slice_in_dim(keys, start, HDIM, 1)
        head_values = lax.dynamic_slice_in_dim(values, start, HDIM, 1)
        head_grads = lax.dynamic_slice_in_dim(grads, start, HDIM, 1)
        scores = jnp.dot(head_queries, head_keys.T, preferred_element_type=jnp.float32) * scale
        scores = jnp.where(allowed, scores, -jnp.inf)
        row_max = jnp.max(scores, axis=1, keepdims=True)
        log_total = row_max + jnp.log(jnp.sum(jnp.exp(scores - row_max), axis=1, keepdims=True))
        probs = jnp.exp(scores - log_total)
        probs_low = probs.astype(jnp.bfloat16)
        output = jnp.dot(probs_low, head_values, preferred_element_type=jnp.float32)
        delta = jnp.sum(head_grads.astype(jnp.float32) * output, axis=1, keepdims=True)
        dprob = jnp.dot(head_grads, head_values.T, preferred_element_type=jnp.float32)
        dscore = (probs * (dprob - delta)).astype(jnp.bfloat16)
        query_grad = jnp.dot(dscore, head_keys, preferred_element_type=jnp.float32) * scale
        key_grad = jnp.dot(dscore.T, head_queries, preferred_element_type=jnp.float32) * scale
        value_grad = jnp.dot(probs_low.T, head_grads, preferred_element_type=jnp.float32)
        return jnp.stack([query_grad, key_grad, value_grad]).astype(jnp.bfloat16)

    per_head = lax.map(one_head, jnp.arange(HEADS, dtype=jnp.int32))
    merged = jnp.transpose(per_head, (1, 2, 0, 3)).reshape(3, VIDEO + TEXT, HEADS * HDIM)
    return (merged[0, :VIDEO], merged[1, :VIDEO], merged[2, :VIDEO],
            merged[0, VIDEO:], merged[1, VIDEO:], merged[2, VIDEO:])
```

```python
import functools

import jax
import jax.numpy as jnp
from jax import lax
from jax.experimental import pallas as pl
from jax.experimental.pallas import tpu as pltpu
from jax.sharding import PartitionSpec as P

HDIM = 128
CAP = 256
NSHOT = 8
HEADS_LOCAL = 3
WIDTH = HEADS_LOCAL * HDIM
GROUP = 8
SIDE = 4
OWN = 32
BLOCK = GROUP * OWN
HALF = 128
VIDEO_ROWS = SIDE * BLOCK
TEXT_ROWS = SIDE * HALF
ROWS = VIDEO_ROWS + TEXT_ROWS
SCALE = HDIM ** (-0.5)
LOG2E = 1.4426950408889634
TO_LOG2 = SCALE * LOG2E
LOW = -1e30
F32 = jnp.float32
BF16 = jnp.bfloat16
VMEM_LIMIT = 24 * 1024 * 1024


def dot_nt(a, b):
    return lax.dot_general(a, b, (((1,), (1,)), ((), ())), preferred_element_type=F32)


def dot_nn(a, b):
    return lax.dot_general(a, b, (((1,), (0,)), ((), ())), preferred_element_type=F32)


def pack_kernel(q_ref, k_ref, v_ref, g_ref, tq_ref, tg_ref, out_ref, text_qg_ref):
    for d in range(GROUP):
        cols = slice(d * WIDTH, (d + 1) * WIDTH)
        for n, ref in enumerate((q_ref, g_ref, k_ref, v_ref)):
            out_ref[d, n] = ref[:, cols]
    text_qg_ref[0] = tq_ref[...]
    text_qg_ref[1] = tg_ref[...]


def pack(*arrays):
    video = jax.ShapeDtypeStruct((GROUP, 4, OWN, WIDTH), BF16)
    text = jax.ShapeDtypeStruct((2, HALF, WIDTH), BF16)
    return pl.pallas_call(pack_kernel, out_shape=(video, text), name="pack_inputs")(*arrays)


def assemble_kernel(in_ref, tk_ref, tv_ref, qg_ref, kv_ref):
    for n in range(2):
        qg_ref[n] = in_ref[:, n].reshape(BLOCK, WIDTH)
        kv_ref[n, :BLOCK] = in_ref[:, 2 + n].reshape(BLOCK, WIDTH)
    kv_ref[0, BLOCK:] = tk_ref[...]
    kv_ref[1, BLOCK:] = tv_ref[...]


def assemble(arrived, text_key, text_value):
    return pl.pallas_call(
        assemble_kernel,
        out_shape=(QUERY_MESSAGE, KEY_MESSAGE),
        name="assemble_blocks",
    )(*placed([arrived]), text_key, text_value)


def unpack_kernel(in_ref, q_ref, k_ref, v_ref):
    for d in range(GROUP):
        cols = slice(d * WIDTH, (d + 1) * WIDTH)
        q_ref[:, cols] = in_ref[d, 0]
        k_ref[:, cols] = in_ref[d, 1]
        v_ref[:, cols] = in_ref[d, 2]


def unpack(arrived):
    shape = jax.ShapeDtypeStruct((OWN, GROUP * WIDTH), BF16)
    return pl.pallas_call(unpack_kernel, out_shape=(shape, shape, shape), name="unpack_video")(*placed([arrived]))


def head_cols(h):
    return slice(h * HDIM, (h + 1) * HDIM)


def sum_kernel(*refs):
    dq, dkv = refs[:SIDE], refs[SIDE : 2 * SIDE]
    out, *text_out = refs[2 * SIDE :]
    for h in range(HEADS_LOCAL):
        total = jnp.transpose(sum(r[h].astype(F32) for r in dq).astype(BF16))
        out[:, 0, :, head_cols(h)] = total[:BLOCK].reshape(GROUP, OWN, HDIM)
        text_out[0][:, head_cols(h)] = total[BLOCK:]
    for n in range(2):
        total = sum(r[n].astype(F32) for r in dkv).astype(BF16)
        out[:, 1 + n] = total[:BLOCK].reshape(GROUP, OWN, WIDTH)
        text_out[1 + n][...] = total[BLOCK:]


def sum_terms(dq, dkv):
    return pl.pallas_call(
        sum_kernel,
        out_shape=[jax.ShapeDtypeStruct((GROUP, 3, OWN, WIDTH), BF16)]
        + [jax.ShapeDtypeStruct((HALF, WIDTH), BF16)] * 3,
        name="sum_terms",
    )(*placed([*dq, *dkv]))


class Labels:
    def __init__(self, length_ref, caption_ref, place_ref):
        place = place_ref[0]
        self.z = place // SIDE
        self.y = place % SIDE
        self.caption_ref = caption_ref
        starts = [jnp.int32(0)]
        for s in range(NSHOT):
            starts.append(starts[-1] + length_ref[s])
        self.starts = starts

    def span(self, shot):
        begin = jnp.int32(0)
        end = jnp.int32(0)
        for s in range(NSHOT):
            begin = jnp.where(shot == s, self.starts[s], begin)
            end = jnp.where(shot == s, self.starts[s + 1], end)
        return begin, end

    def query_base(self, j):
        return (self.z * SIDE + (self.y ^ j)) * BLOCK

    def key_base(self, i):
        return ((self.z ^ i) * SIDE + self.y) * BLOCK

    def query_shot(self, p):
        return self.z * 2 + (self.y ^ (2 * p)) // 2

    def key_shot(self, t):
        return (self.z ^ t) * 2 + self.y // 2

    def live(self, shot, half):
        row = half * HALF + lax.broadcasted_iota(jnp.int32, (HALF, 1), 0)
        return row < self.caption_ref[shot]


def stage_queries(labels, qg, text_qg, q_all, g_all):
    for j in range(SIDE):
        q_all[j] = qg[j][0]
        g_all[j] = qg[j][1]
    for u in range(SIDE):
        p, rows = u // 2, slice(u % 2 * HALF, (u % 2 + 1) * HALF)
        q_all[SIDE + p, rows] = text_qg[u][0]
        live = labels.live(labels.query_shot(p), (labels.y ^ u) % 2)
        g_all[SIDE + p, rows] = jnp.where(live, text_qg[u][1], jnp.zeros((HALF, WIDTH), BF16))


def stage_keys(kv, k_all, v_all, tk_all, tv_all):
    for i, ref in enumerate(kv):
        k_all[i] = ref[0, :BLOCK]
        v_all[i] = ref[1, :BLOCK]
        tk_all[i] = ref[0, BLOCK:]
        tv_all[i] = ref[1, BLOCK:]


def loop(count, step):
    lax.fori_loop(0, count, lambda n, c: (step(n), c)[1], 0)


def text_keys(labels, first, count, visit):
    def step(n):
        t, j = first + n // SIDE, n % SIDE
        shot, base = labels.key_shot(t), labels.query_base(j)
        begin, end = labels.span(shot)

        @pl.when(jnp.logical_and(begin < base + BLOCK, end > base))
        def _():
            row = base + lax.broadcasted_iota(jnp.int32, (1, BLOCK), 1)
            same = jnp.logical_and(row >= begin, row < end)
            visit(t - first, j, jnp.logical_and(labels.live(shot, labels.y % 2), same))

    loop(count * SIDE, step)
    if first == 0:
        live = labels.live(labels.key_shot(0), labels.y % 2)
        visit(0, SIDE, jnp.broadcast_to(live, (HALF, BLOCK)))


def text_queries(labels, first, count, visit):
    def step(n):
        i, p = first + n // 2, n % 2
        base = labels.key_base(i)
        begin, end = labels.span(labels.query_shot(p))

        @pl.when(jnp.logical_and(begin < base + BLOCK, end > base))
        def _():
            row = base + lax.broadcasted_iota(jnp.int32, (BLOCK, 1), 0)
            same = jnp.logical_and(row >= begin, row < end)
            visit(i - first, p, jnp.broadcast_to(same, (BLOCK, BLOCK)))

    loop(2 * count, step)


def head_ds(h):
    return pl.ds(pl.multiple_of(h * HDIM, HDIM), HDIM)


def rows_ds(j):
    return pl.ds(pl.multiple_of(j * BLOCK, BLOCK), BLOCK)


def query_cols(j):
    return slice(j * BLOCK, (j + 1) * BLOCK)


def stats_kernel(first, length_ref, caption_ref, place_ref, *refs):
    acc_in, refs = (refs[:1], refs[1:]) if first else ((), refs)
    qg, kv, text_qg = refs[:SIDE], refs[SIDE : SIDE + 2], refs[SIDE + 2 : 2 * SIDE + 2]
    out_ref, q_all, g_all, k_all, v_all, tk_all, tv_all, *scratch = refs[2 * SIDE + 2 :]
    labels = Labels(length_ref, caption_ref, place_ref)
    stage_queries(labels, qg, text_qg, q_all, g_all)
    stage_keys(kv, k_all, v_all, tk_all, tv_all)
    if first:
        acc = scratch[0]
        acc[...] = acc_in[0][...]
    else:
        acc = out_ref
        acc[0] = jnp.full((HEADS_LOCAL, ROWS), LOW, F32)
        acc[1:3] = jnp.zeros((2, HEADS_LOCAL, ROWS), F32)

    def head(h):
        c, row = head_ds(h), pl.ds(h, 1)
        keys = k_all[:, :, c].reshape(2 * BLOCK, HDIM)
        values = v_all[:, :, c].reshape(2 * BLOCK, HDIM)
        for j in range(SIDE):
            cols = query_cols(j)
            scores = dot_nt(keys, q_all[j, :, c])
            dprob = dot_nt(values, g_all[j, :, c])
            top = jnp.max(scores, axis=0, keepdims=True) * TO_LOG2
            if first:
                before = acc[0, row, cols]
                top = jnp.maximum(before, top)
                shrink = jnp.exp2(before - top)
            weight = jnp.exp2(scores * TO_LOG2 - top)
            total = jnp.sum(weight, axis=0, keepdims=True)
            weighted = jnp.sum(weight * dprob, axis=0, keepdims=True)
            if first:
                total += acc[1, row, cols] * shrink
                weighted += acc[2, row, cols] * shrink
            acc[0, row, cols] = top
            acc[1, row, cols] = total
            acc[2, row, cols] = weighted

    loop(HEADS_LOCAL, head)

    def visit(keys_ref, values_ref, n, j, mask):
        cols = rows_ds(j)
        results = []
        for h in range(HEADS_LOCAL):
            c = head_cols(h)
            scores = jnp.where(mask, dot_nt(keys_ref[n, :, c], q_all[j, :, c]) * TO_LOG2, LOW)
            dprob = dot_nt(values_ref[n, :, c], g_all[j, :, c])
            before = acc[0, h : h + 1, cols]
            top = jnp.maximum(before, jnp.max(scores, axis=0, keepdims=True))
            weight = jnp.where(mask, jnp.exp2(scores - top), 0.0)
            shrink = jnp.exp2(before - top)
            results.append(
                (
                    top,
                    acc[1, h : h + 1, cols] * shrink + jnp.sum(weight, axis=0, keepdims=True),
                    acc[2, h : h + 1, cols] * shrink + jnp.sum(weight * dprob, axis=0, keepdims=True),
                )
            )
        for h in range(HEADS_LOCAL):
            for n in range(3):
                acc[n, h : h + 1, cols] = results[h][n]

    text_keys(labels, first, 2, lambda t, j, mask: visit(tk_all, tv_all, t, j, mask))
    text_queries(labels, first, 2, lambda i, p, mask: visit(k_all, v_all, i, SIDE + p, mask))
    if first:
        total = acc[1]
        some = total > 0.0
        total = jnp.where(some, total, 1.0)
        out_ref[0] = jnp.where(some, acc[0] + jnp.log2(total), LOW)
        out_ref[1] = acc[2] / total


def normalize(stats, norm):
    for j in range(SIDE + 2):
        parts = []
        for e in range(SIDE):
            if j < SIDE:
                parts.append([stats[e][n, :, query_cols(j ^ e)] for n in range(2)])
            else:
                halves = []
                for u in (2 * (j - SIDE), 2 * (j - SIDE) + 1):
                    at = VIDEO_ROWS + (u ^ e) * HALF
                    halves.append([stats[e][n, :, at : at + HALF] for n in range(2)])
                parts.append([jnp.concatenate([halves[0][n], halves[1][n]], 1) for n in range(2)])
        top = functools.reduce(jnp.maximum, [p[0] for p in parts])
        share = [jnp.exp2(p[0] - top) for p in parts]
        total = sum(share)
        delta = sum(p[1] * s for p, s in zip(parts, share)) / total
        norm[0, :, query_cols(j)] = top + jnp.log2(total)
        norm[1, :, query_cols(j)] = delta


def key_grads(labels, first, count, kv, dkv_out, norm, dq_t, scratch):
    q_all, g_all, k_all, v_all, tk_all, tv_all, dk, dv, text_dk, text_dv, p_all, ds_all = scratch
    stage_keys(kv, k_all, v_all, tk_all, tv_all)
    text_dk[...] = jnp.zeros((count, HEADS_LOCAL, HALF, HDIM), F32)
    text_dv[...] = jnp.zeros((count, HEADS_LOCAL, HALF, HDIM), F32)
    rows = count * BLOCK

    def head(h):
        c, row = head_ds(h), pl.ds(h, 1)
        keys = k_all[:, :, c].reshape(rows, HDIM)
        values = v_all[:, :, c].reshape(rows, HDIM)
        keys_t = jnp.transpose(keys)
        for j in range(SIDE):
            cols = query_cols(j)
            scores = dot_nt(keys, q_all[j, :, c])
            dprob = dot_nt(values, g_all[j, :, c])
            probs = jnp.exp2(scores * TO_LOG2 - norm[0, row, cols])
            dscore = (probs * (dprob - norm[1, row, cols])).astype(BF16)
            p_all[:, cols] = probs.astype(BF16)
            ds_all[:, cols] = dscore
            part = dot_nn(keys_t, dscore)
            if first:
                dq_t[h, :, cols] = part
            else:
                dq_t[h, :, cols] += part
        dv[h] = dot_nn(p_all[...], g_all[:SIDE, :, c].reshape(VIDEO_ROWS, HDIM))
        dk[h] = dot_nn(ds_all[...], q_all[:SIDE, :, c].reshape(VIDEO_ROWS, HDIM))

    loop(HEADS_LOCAL, head)

    def visit(keys_ref, values_ref, n, j, mask, add):
        cols = rows_ds(j)
        results = []
        for h in range(HEADS_LOCAL):
            c = head_cols(h)
            keys, queries, grads = keys_ref[n, :, c], q_all[j, :, c], g_all[j, :, c]
            scores = dot_nt(keys, queries) * TO_LOG2
            dprob = dot_nt(values_ref[n, :, c], grads)
            probs = jnp.where(mask, jnp.exp2(jnp.where(mask, scores, LOW) - norm[0, h : h + 1, cols]), 0.0)
            low = probs.astype(BF16)
            dscore = (probs * (dprob - norm[1, h : h + 1, cols])).astype(BF16)
            results.append((dot_nn(dscore, queries), dot_nn(low, grads), dot_nn(jnp.transpose(keys), dscore)))
        for h in range(HEADS_LOCAL):
            add(n, h, results[h][0], results[h][1])
            dq_t[h, :, cols] += results[h][2]

    def add_text(n, h, key_part, value_part):
        text_dk[n, h] += key_part
        text_dv[n, h] += value_part

    def add_video(n, h, key_part, value_part):
        dk[h, rows_ds(n)] += key_part
        dv[h, rows_ds(n)] += value_part

    text_keys(labels, first, count, lambda t, j, mask: visit(tk_all, tv_all, t, j, mask, add_text))
    text_queries(labels, first, count, lambda i, p, mask: visit(k_all, v_all, i, SIDE + p, mask, add_video))

    for i in range(count):
        for h in range(HEADS_LOCAL):
            c = head_cols(h)
            dkv_out[i][0, :BLOCK, c] = (dk[h, query_cols(i)] * SCALE).astype(BF16)
            dkv_out[i][1, :BLOCK, c] = dv[h, query_cols(i)].astype(BF16)
            dkv_out[i][0, BLOCK:, c] = (text_dk[i, h] * SCALE).astype(BF16)
            dkv_out[i][1, BLOCK:, c] = text_dv[i, h].astype(BF16)


def others_kernel(length_ref, caption_ref, place_ref, *refs):
    qg, kv, stats = refs[:SIDE], refs[SIDE : 2 * SIDE - 1], refs[2 * SIDE - 1 : 3 * SIDE - 1]
    text_qg, refs = refs[3 * SIDE - 1 : 4 * SIDE - 1], refs[4 * SIDE - 1 :]
    dkv_out, (dq_t, norm, *scratch) = refs[: SIDE - 1], refs[SIDE - 1 :]
    labels = Labels(length_ref, caption_ref, place_ref)
    stage_queries(labels, qg, text_qg, scratch[0], scratch[1])
    normalize(stats, norm)
    dq_t[:, :, VIDEO_ROWS:] = jnp.zeros((HEADS_LOCAL, HDIM, TEXT_ROWS), F32)
    key_grads(labels, 1, SIDE - 1, kv, dkv_out, norm, dq_t, scratch)


def own_kernel(length_ref, caption_ref, place_ref, *refs):
    norm, dq_in, qg, kv = refs[0], refs[1], refs[2 : SIDE + 2], refs[SIDE + 2 : SIDE + 3]
    text_qg, refs = refs[SIDE + 3 : 2 * SIDE + 3], refs[2 * SIDE + 3 :]
    dq_out, dkv_out, (dq_t, *scratch) = refs[:SIDE], refs[SIDE : SIDE + 1], refs[SIDE + 1 :]
    labels = Labels(length_ref, caption_ref, place_ref)
    stage_queries(labels, qg, text_qg, scratch[0], scratch[1])
    dq_t[...] = dq_in[...]
    key_grads(labels, 0, 1, kv, dkv_out, norm, dq_t, scratch)
    for n in range(SIDE):
        dq_out[n][:, :, :BLOCK] = (dq_t[:, :, query_cols(n)] * SCALE).astype(BF16)
        dq_out[n][:, :, BLOCK:] = (dq_t[:, :, VIDEO_ROWS + n * HALF : VIDEO_ROWS + (n + 1) * HALF] * SCALE).astype(BF16)


SMEM_SPEC = pl.BlockSpec(memory_space=pltpu.SMEM)
VMEM_SPEC = pl.BlockSpec(memory_space=pltpu.VMEM)
PARAMS = pltpu.CompilerParams(vmem_limit_bytes=VMEM_LIMIT)
DQ_T = (HEADS_LOCAL, HDIM, ROWS)
STATS = (3, HEADS_LOCAL, ROWS)
QUERY_MESSAGE = jax.ShapeDtypeStruct((2, BLOCK, WIDTH), BF16)
KEY_MESSAGE = jax.ShapeDtypeStruct((2, BLOCK + HALF, WIDTH), BF16)


def staged(count):
    return (
        [pltpu.VMEM((SIDE + 2, BLOCK, WIDTH), BF16)] * 2
        + [pltpu.VMEM((count, BLOCK, WIDTH), BF16)] * 2
        + [pltpu.VMEM((count, HALF, WIDTH), BF16)] * 2
    )


def grads_scratch(count):
    return (
        staged(count)
        + [pltpu.VMEM((HEADS_LOCAL, count * BLOCK, HDIM), F32)] * 2
        + [pltpu.VMEM((count, HEADS_LOCAL, HALF, HDIM), F32)] * 2
        + [pltpu.VMEM((count * BLOCK, VIDEO_ROWS), BF16)] * 2
    )


def placed(arrays, space=pltpu.VMEM):
    return [pltpu.with_memory_space_constraint(a, space) for a in arrays]


def cost(blocks, matmuls):
    pairs = HEADS_LOCAL * VIDEO_ROWS * BLOCK * blocks
    return pl.CostEstimate(flops=2 * HDIM * matmuls * pairs, bytes_accessed=8 * 1024 * 1024, transcendentals=pairs)


def stats_call(first, scalars, acc, qg, kv, text_qg):
    return pl.pallas_call(
        functools.partial(stats_kernel, first),
        in_specs=[SMEM_SPEC] * 3 + [VMEM_SPEC] * (len(acc) + 2 * SIDE + 2),
        out_specs=VMEM_SPEC,
        out_shape=jax.ShapeDtypeStruct((2, HEADS_LOCAL, ROWS) if first else STATS, F32),
        scratch_shapes=staged(2) + ([pltpu.VMEM(STATS, F32)] if first else []),
        compiler_params=PARAMS,
        cost_estimate=cost(2, 2),
        name="stats_last" if first else "stats_first",
    )(*scalars, *placed([*acc, *qg, *kv[first : first + 2]]), *placed(text_qg, pltpu.HBM))


def others_call(scalars, qg, kv, text_qg, stats):
    *dkv, dq_t, norm = pl.pallas_call(
        others_kernel,
        in_specs=[SMEM_SPEC] * 3 + [VMEM_SPEC] * (4 * SIDE - 1),
        out_specs=[VMEM_SPEC] * (SIDE + 1),
        out_shape=[KEY_MESSAGE] * (SIDE - 1)
        + [jax.ShapeDtypeStruct(DQ_T, F32), jax.ShapeDtypeStruct((2, HEADS_LOCAL, ROWS), F32)],
        scratch_shapes=grads_scratch(SIDE - 1),
        compiler_params=PARAMS,
        cost_estimate=cost(SIDE - 1, 5),
        name="grads_others",
    )(*scalars, *placed([*qg, *kv[1:], *stats]), *placed(text_qg, pltpu.HBM))
    return dkv, dq_t, norm


def own_call(scalars, qg, kv, text_qg, dq_t, norm):
    *dq, dkv = pl.pallas_call(
        own_kernel,
        in_specs=[SMEM_SPEC] * 3 + [VMEM_SPEC] * (2 * SIDE + 3),
        out_specs=[VMEM_SPEC] * (SIDE + 1),
        out_shape=[jax.ShapeDtypeStruct((HEADS_LOCAL, HDIM, BLOCK + HALF), BF16)] * SIDE + [KEY_MESSAGE],
        scratch_shapes=[pltpu.VMEM(DQ_T, F32)] + grads_scratch(1),
        compiler_params=PARAMS,
        cost_estimate=cost(1, 5),
        name="grads_own",
    )(*scalars, *placed([norm]), dq_t, *placed(qg, pltpu.HBM), *placed(kv[:1]), *placed(text_qg, pltpu.HBM))
    return dq, dkv


def swap(array, axis, step):
    shift = step if axis == "y" else step * SIDE
    return lax.ppermute(array, "seq", [(i, i ^ shift) for i in range(SIDE * SIDE)])


def gathered(array, axis):
    return [array] + [swap(array, axis, step) for step in range(1, SIDE)]


def on_device(
    video_query,
    video_key,
    video_value,
    video_grad,
    text_query,
    text_key,
    text_value,
    text_grad,
    shot_length,
    caption_length,
):
    place = lax.axis_index("seq").astype(jnp.int32)
    scalars = (shot_length, caption_length, place.reshape(1))
    packed, text_qg = pack(video_query, video_key, video_value, video_grad, text_query, text_grad)
    text_qg = gathered(text_qg, "y")
    arrived = lax.all_to_all(packed, "head", split_axis=0, concat_axis=0)
    arrived, text_qg = lax.optimization_barrier((arrived, text_qg))
    qg, kv = assemble(arrived, text_key, text_value)
    qg, kv = gathered(qg, "y"), gathered(kv, "z")

    acc = stats_call(0, scalars, [], qg, kv, text_qg)
    stats = gathered(stats_call(2, scalars, [acc], qg, kv, text_qg), "y")
    dkv, dq_t, norm = others_call(scalars, qg, kv, text_qg, stats)
    dq, dkv_own = own_call(scalars, qg, kv, text_qg, dq_t, norm)

    first = swap(dkv[0], "z", 1)
    dq, first = lax.optimization_barrier((dq, first))
    dkv = [dkv_own, first, swap(dkv[1], "z", 2), swap(dkv[2], "z", 3)]
    dq = [dq[0]] + [swap(dq[step], "y", step) for step in range(1, SIDE)]
    video, *text = sum_terms(dq, dkv)
    video_back = unpack(lax.all_to_all(video, "head", split_axis=0, concat_axis=0))
    return (*video_back, *text)


def solution(mesh):
    video = P(("seq", "head"), None)
    text = P("seq", "head")
    return jax.shard_map(
        on_device,
        mesh=mesh,
        in_specs=(video,) * 4 + (text,) * 4 + (P(), P()),
        out_specs=(video,) * 3 + (text,) * 3,
        check_vma=False,
    )
```

```python
import functools

import jax
import jax.numpy as jnp
from jax import lax
from jax.experimental import pallas as pl
from jax.experimental.pallas import tpu as pltpu
from jax.sharding import PartitionSpec as P

HDIM = 128
CAP = 256
NSHOT = 8
HEADS_LOCAL = 3
WIDTH = HEADS_LOCAL * HDIM
GROUP = 8
SIDE = 4
OWN = 32
BLOCK = GROUP * OWN
HALF = 128
VIDEO_ROWS = SIDE * BLOCK
TEXT_ROWS = SIDE * HALF
ROWS = VIDEO_ROWS + TEXT_ROWS
SCALE = HDIM ** (-0.5)
LOG2E = 1.4426950408889634
TO_LOG2 = SCALE * LOG2E
LOW = -1e30
F32 = jnp.float32
BF16 = jnp.bfloat16
VMEM_LIMIT = 24 * 1024 * 1024


def dot_nt(a, b):
    return lax.dot_general(a, b, (((1,), (1,)), ((), ())), preferred_element_type=F32)


def dot_nn(a, b):
    return lax.dot_general(a, b, (((1,), (0,)), ((), ())), preferred_element_type=F32)


def pack_kernel(q_ref, k_ref, v_ref, g_ref, tq_ref, tg_ref, out_ref, text_qg_ref):
    for d in range(GROUP):
        cols = slice(d * WIDTH, (d + 1) * WIDTH)
        for n, ref in enumerate((q_ref, g_ref, k_ref, v_ref)):
            out_ref[d, n] = ref[:, cols]
    text_qg_ref[0] = tq_ref[...]
    text_qg_ref[1] = tg_ref[...]


def pack(*arrays):
    video = jax.ShapeDtypeStruct((GROUP, 4, OWN, WIDTH), BF16)
    text = jax.ShapeDtypeStruct((2, HALF, WIDTH), BF16)
    return pl.pallas_call(pack_kernel, out_shape=(video, text), name="pack_inputs")(*arrays)


def assemble_kernel(in_ref, tk_ref, tv_ref, qg_ref, kv_ref):
    for n in range(2):
        qg_ref[n] = in_ref[:, n].reshape(BLOCK, WIDTH)
        kv_ref[n, :BLOCK] = in_ref[:, 2 + n].reshape(BLOCK, WIDTH)
    kv_ref[0, BLOCK:] = tk_ref[...]
    kv_ref[1, BLOCK:] = tv_ref[...]


def assemble(arrived, text_key, text_value):
    return pl.pallas_call(
        assemble_kernel,
        out_shape=(QUERY_MESSAGE, KEY_MESSAGE),
        compiler_params=SMALL,
        name="assemble_blocks",
    )(*placed([arrived]), text_key, text_value)


def unpack_kernel(in_ref, q_ref, k_ref, v_ref):
    for d in range(GROUP):
        cols = slice(d * WIDTH, (d + 1) * WIDTH)
        q_ref[:, cols] = in_ref[d, 0]
        k_ref[:, cols] = in_ref[d, 1]
        v_ref[:, cols] = in_ref[d, 2]


def unpack(arrived):
    shape = jax.ShapeDtypeStruct((OWN, GROUP * WIDTH), BF16)
    return pl.pallas_call(unpack_kernel, out_shape=(shape, shape, shape), compiler_params=SMALL, name="unpack_video")(*placed([arrived]))


def head_cols(h):
    return slice(h * HDIM, (h + 1) * HDIM)


def sum_kernel(*refs):
    dq, dkv = refs[:SIDE], refs[SIDE : 2 * SIDE]
    out, *text_out = refs[2 * SIDE :]
    for h in range(HEADS_LOCAL):
        total = jnp.transpose(sum(r[h].astype(F32) for r in dq).astype(BF16))
        out[:, 0, :, head_cols(h)] = total[:BLOCK].reshape(GROUP, OWN, HDIM)
        text_out[0][:, head_cols(h)] = total[BLOCK:]
    for n in range(2):
        total = sum(r[n].astype(F32) for r in dkv).astype(BF16)
        out[:, 1 + n] = total[:BLOCK].reshape(GROUP, OWN, WIDTH)
        text_out[1 + n][...] = total[BLOCK:]


def sum_terms(dq, dkv):
    return pl.pallas_call(
        sum_kernel,
        out_shape=[jax.ShapeDtypeStruct((GROUP, 3, OWN, WIDTH), BF16)]
        + [jax.ShapeDtypeStruct((HALF, WIDTH), BF16)] * 3,
        compiler_params=SMALL,
        name="sum_terms",
    )(*placed([*dq, *dkv]))


class Labels:
    def __init__(self, length_ref, caption_ref, place_ref):
        place = place_ref[0]
        self.z = place // SIDE
        self.y = place % SIDE
        self.caption_ref = caption_ref
        starts = [jnp.int32(0)]
        for s in range(NSHOT):
            starts.append(starts[-1] + length_ref[s])
        self.starts = starts

    def span(self, shot):
        begin = jnp.int32(0)
        end = jnp.int32(0)
        for s in range(NSHOT):
            begin = jnp.where(shot == s, self.starts[s], begin)
            end = jnp.where(shot == s, self.starts[s + 1], end)
        return begin, end

    def query_base(self, j):
        return (self.z * SIDE + (self.y ^ j)) * BLOCK

    def key_base(self, i):
        return ((self.z ^ i) * SIDE + self.y) * BLOCK

    def query_shot(self, p):
        return self.z * 2 + (self.y ^ (2 * p)) // 2

    def key_shot(self, t):
        return (self.z ^ t) * 2 + self.y // 2

    def live(self, shot, half):
        row = half * HALF + lax.broadcasted_iota(jnp.int32, (HALF, 1), 0)
        return row < self.caption_ref[shot]


def stage_queries(labels, qg, text_qg, q_all, g_all):
    for j in range(SIDE):
        q_all[j] = qg[j][0]
        g_all[j] = qg[j][1]
    for u in range(SIDE):
        p, rows = u // 2, slice(u % 2 * HALF, (u % 2 + 1) * HALF)
        q_all[SIDE + p, rows] = text_qg[u][0]
        live = labels.live(labels.query_shot(p), (labels.y ^ u) % 2)
        g_all[SIDE + p, rows] = jnp.where(live, text_qg[u][1], jnp.zeros((HALF, WIDTH), BF16))


def stage_keys(kv, k_all, v_all, tk_all, tv_all):
    for i, ref in enumerate(kv):
        k_all[i] = ref[0, :BLOCK]
        v_all[i] = ref[1, :BLOCK]
        tk_all[i] = ref[0, BLOCK:]
        tv_all[i] = ref[1, BLOCK:]


def loop(count, step):
    lax.fori_loop(0, count, lambda n, c: (step(n), c)[1], 0)


def chosen(blocks, n):
    return sum(jnp.where(n == m, block, 0) for m, block in enumerate(blocks))


def text_keys(labels, blocks, visit):
    def step(n):
        t, j = n // SIDE, n % SIDE
        shot, base = labels.key_shot(chosen(blocks, t)), labels.query_base(j)
        begin, end = labels.span(shot)

        @pl.when(jnp.logical_and(begin < base + BLOCK, end > base))
        def _():
            row = base + lax.broadcasted_iota(jnp.int32, (1, BLOCK), 1)
            same = jnp.logical_and(row >= begin, row < end)
            visit(t, j, jnp.logical_and(labels.live(shot, labels.y % 2), same))

    loop(len(blocks) * SIDE, step)
    if 0 in blocks:
        live = labels.live(labels.key_shot(0), labels.y % 2)
        visit(blocks.index(0), SIDE, jnp.broadcast_to(live, (HALF, BLOCK)))


def text_queries(labels, blocks, visit):
    def step(n):
        i, p = n // 2, n % 2
        base = labels.key_base(chosen(blocks, i))
        begin, end = labels.span(labels.query_shot(p))

        @pl.when(jnp.logical_and(begin < base + BLOCK, end > base))
        def _():
            row = base + lax.broadcasted_iota(jnp.int32, (BLOCK, 1), 0)
            same = jnp.logical_and(row >= begin, row < end)
            visit(i, p, jnp.broadcast_to(same, (BLOCK, BLOCK)))

    loop(2 * len(blocks), step)


def head_ds(h):
    return pl.ds(pl.multiple_of(h * HDIM, HDIM), HDIM)


def rows_ds(j):
    return pl.ds(pl.multiple_of(j * BLOCK, BLOCK), BLOCK)


def query_cols(j):
    return slice(j * BLOCK, (j + 1) * BLOCK)


def stats_kernel(blocks, last, length_ref, caption_ref, place_ref, *refs):
    count = len(blocks)
    acc_in, refs = (refs[:1], refs[1:]) if last else ((), refs)
    qg, kv, text_qg = refs[:SIDE], refs[SIDE : SIDE + count], refs[SIDE + count : 2 * SIDE + count]
    out_ref, q_all, g_all, k_all, v_all, tk_all, tv_all, *scratch = refs[2 * SIDE + count :]
    labels = Labels(length_ref, caption_ref, place_ref)
    stage_queries(labels, qg, text_qg, q_all, g_all)
    stage_keys(kv, k_all, v_all, tk_all, tv_all)
    if last:
        acc = scratch[0]
        acc[...] = acc_in[0][...]
    else:
        acc = out_ref
        acc[0] = jnp.full((HEADS_LOCAL, ROWS), LOW, F32)
        acc[1:3] = jnp.zeros((2, HEADS_LOCAL, ROWS), F32)

    def head(h):
        c, row = head_ds(h), pl.ds(h, 1)
        keys = k_all[:, :, c].reshape(count * BLOCK, HDIM)
        values = v_all[:, :, c].reshape(count * BLOCK, HDIM)
        for j in range(SIDE):
            cols = query_cols(j)
            scores = dot_nt(keys, q_all[j, :, c])
            dprob = dot_nt(values, g_all[j, :, c])
            top = jnp.max(scores, axis=0, keepdims=True) * TO_LOG2
            if last:
                before = acc[0, row, cols]
                top = jnp.maximum(before, top)
                shrink = jnp.exp2(before - top)
            weight = jnp.exp2(scores * TO_LOG2 - top)
            total = jnp.sum(weight, axis=0, keepdims=True)
            weighted = jnp.sum(weight * dprob, axis=0, keepdims=True)
            if last:
                total += acc[1, row, cols] * shrink
                weighted += acc[2, row, cols] * shrink
            acc[0, row, cols] = top
            acc[1, row, cols] = total
            acc[2, row, cols] = weighted

    loop(HEADS_LOCAL, head)

    def visit(keys_ref, values_ref, n, j, mask):
        cols = rows_ds(j)
        results = []
        for h in range(HEADS_LOCAL):
            c = head_cols(h)
            scores = jnp.where(mask, dot_nt(keys_ref[n, :, c], q_all[j, :, c]) * TO_LOG2, LOW)
            dprob = dot_nt(values_ref[n, :, c], g_all[j, :, c])
            before = acc[0, h : h + 1, cols]
            top = jnp.maximum(before, jnp.max(scores, axis=0, keepdims=True))
            weight = jnp.where(mask, jnp.exp2(scores - top), 0.0)
            shrink = jnp.exp2(before - top)
            results.append(
                (
                    top,
                    acc[1, h : h + 1, cols] * shrink + jnp.sum(weight, axis=0, keepdims=True),
                    acc[2, h : h + 1, cols] * shrink + jnp.sum(weight * dprob, axis=0, keepdims=True),
                )
            )
        for h in range(HEADS_LOCAL):
            for n in range(3):
                acc[n, h : h + 1, cols] = results[h][n]

    text_keys(labels, blocks, lambda t, j, mask: visit(tk_all, tv_all, t, j, mask))
    text_queries(labels, blocks, lambda i, p, mask: visit(k_all, v_all, i, SIDE + p, mask))
    if last:
        total = acc[1]
        some = total > 0.0
        total = jnp.where(some, total, 1.0)
        out_ref[0] = jnp.where(some, acc[0] + jnp.log2(total), LOW)
        out_ref[1] = acc[2] / total


def normalize(stats, norm):
    for j in range(SIDE + 2):
        parts = []
        for e in range(SIDE):
            if j < SIDE:
                parts.append([stats[e][n, :, query_cols(j ^ e)] for n in range(2)])
            else:
                halves = []
                for u in (2 * (j - SIDE), 2 * (j - SIDE) + 1):
                    at = VIDEO_ROWS + (u ^ e) * HALF
                    halves.append([stats[e][n, :, at : at + HALF] for n in range(2)])
                parts.append([jnp.concatenate([halves[0][n], halves[1][n]], 1) for n in range(2)])
        top = functools.reduce(jnp.maximum, [p[0] for p in parts])
        share = [jnp.exp2(p[0] - top) for p in parts]
        total = sum(share)
        delta = sum(p[1] * s for p, s in zip(parts, share)) / total
        norm[0, :, query_cols(j)] = top + jnp.log2(total)
        norm[1, :, query_cols(j)] = delta


def key_grads(labels, blocks, fresh, kv, dkv_out, norm, dq_t, scratch):
    count = len(blocks)
    q_all, g_all, k_all, v_all, tk_all, tv_all, dk, dv, text_dk, text_dv, p_all, ds_all = scratch
    stage_keys(kv, k_all, v_all, tk_all, tv_all)
    text_dk[...] = jnp.zeros((count, HEADS_LOCAL, HALF, HDIM), F32)
    text_dv[...] = jnp.zeros((count, HEADS_LOCAL, HALF, HDIM), F32)
    rows = count * BLOCK

    def head(h):
        c, row = head_ds(h), pl.ds(h, 1)
        keys = k_all[:, :, c].reshape(rows, HDIM)
        values = v_all[:, :, c].reshape(rows, HDIM)
        keys_t = jnp.transpose(keys)
        for j in range(SIDE):
            cols = query_cols(j)
            scores = dot_nt(keys, q_all[j, :, c])
            dprob = dot_nt(values, g_all[j, :, c])
            probs = jnp.exp2(scores * TO_LOG2 - norm[0, row, cols])
            dscore = (probs * (dprob - norm[1, row, cols])).astype(BF16)
            p_all[:, cols] = probs.astype(BF16)
            ds_all[:, cols] = dscore
            part = dot_nn(keys_t, dscore)
            if fresh:
                dq_t[h, :, cols] = part
            else:
                dq_t[h, :, cols] += part
        dv[h] = dot_nn(p_all[...], g_all[:SIDE, :, c].reshape(VIDEO_ROWS, HDIM))
        dk[h] = dot_nn(ds_all[...], q_all[:SIDE, :, c].reshape(VIDEO_ROWS, HDIM))

    loop(HEADS_LOCAL, head)

    def visit(keys_ref, values_ref, n, j, mask, add):
        cols = rows_ds(j)
        results = []
        for h in range(HEADS_LOCAL):
            c = head_cols(h)
            keys, queries, grads = keys_ref[n, :, c], q_all[j, :, c], g_all[j, :, c]
            scores = dot_nt(keys, queries) * TO_LOG2
            dprob = dot_nt(values_ref[n, :, c], grads)
            probs = jnp.where(mask, jnp.exp2(jnp.where(mask, scores, LOW) - norm[0, h : h + 1, cols]), 0.0)
            low = probs.astype(BF16)
            dscore = (probs * (dprob - norm[1, h : h + 1, cols])).astype(BF16)
            results.append((dot_nn(dscore, queries), dot_nn(low, grads), dot_nn(jnp.transpose(keys), dscore)))
        for h in range(HEADS_LOCAL):
            add(n, h, results[h][0], results[h][1])
            dq_t[h, :, cols] += results[h][2]

    def add_text(n, h, key_part, value_part):
        text_dk[n, h] += key_part
        text_dv[n, h] += value_part

    def add_video(n, h, key_part, value_part):
        dk[h, rows_ds(n)] += key_part
        dv[h, rows_ds(n)] += value_part

    text_keys(labels, blocks, lambda t, j, mask: visit(tk_all, tv_all, t, j, mask, add_text))
    text_queries(labels, blocks, lambda i, p, mask: visit(k_all, v_all, i, SIDE + p, mask, add_video))

    for i in range(count):
        for h in range(HEADS_LOCAL):
            c = head_cols(h)
            dkv_out[i][0, :BLOCK, c] = (dk[h, query_cols(i)] * SCALE).astype(BF16)
            dkv_out[i][1, :BLOCK, c] = dv[h, query_cols(i)].astype(BF16)
            dkv_out[i][0, BLOCK:, c] = (text_dk[i, h] * SCALE).astype(BF16)
            dkv_out[i][1, BLOCK:, c] = text_dv[i, h].astype(BF16)


def grads_first_kernel(blocks, length_ref, caption_ref, place_ref, *refs):
    count = len(blocks)
    qg, kv, refs = refs[:SIDE], refs[SIDE : SIDE + count], refs[SIDE + count :]
    stats, text_qg, refs = refs[:SIDE], refs[SIDE : 2 * SIDE], refs[2 * SIDE :]
    dkv_out, (dq_t, norm, *scratch) = refs[:count], refs[count:]
    labels = Labels(length_ref, caption_ref, place_ref)
    stage_queries(labels, qg, text_qg, scratch[0], scratch[1])
    normalize(stats, norm)
    dq_t[:, :, VIDEO_ROWS:] = jnp.zeros((HEADS_LOCAL, HDIM, TEXT_ROWS), F32)
    key_grads(labels, blocks, True, kv, dkv_out, norm, dq_t, scratch)


def grads_last_kernel(blocks, length_ref, caption_ref, place_ref, *refs):
    count = len(blocks)
    norm, dq_in, qg, refs = refs[0], refs[1], refs[2 : SIDE + 2], refs[SIDE + 2 :]
    kv, text_qg, refs = refs[:count], refs[count : SIDE + count], refs[SIDE + count :]
    dq_out, dkv_out, (dq_t, *scratch) = refs[:SIDE], refs[SIDE : SIDE + count], refs[SIDE + count :]
    labels = Labels(length_ref, caption_ref, place_ref)
    stage_queries(labels, qg, text_qg, scratch[0], scratch[1])
    dq_t[...] = dq_in[...]
    key_grads(labels, blocks, False, kv, dkv_out, norm, dq_t, scratch)
    for n in range(SIDE):
        dq_out[n][:, :, :BLOCK] = (dq_t[:, :, query_cols(n)] * SCALE).astype(BF16)
        dq_out[n][:, :, BLOCK:] = (dq_t[:, :, VIDEO_ROWS + n * HALF : VIDEO_ROWS + (n + 1) * HALF] * SCALE).astype(BF16)


SMEM_SPEC = pl.BlockSpec(memory_space=pltpu.SMEM)
VMEM_SPEC = pl.BlockSpec(memory_space=pltpu.VMEM)
PARAMS = pltpu.CompilerParams(vmem_limit_bytes=VMEM_LIMIT)
SMALL = pltpu.CompilerParams(vmem_limit_bytes=8 * 1024 * 1024)
DQ_T = (HEADS_LOCAL, HDIM, ROWS)
STATS = (3, HEADS_LOCAL, ROWS)
QUERY_MESSAGE = jax.ShapeDtypeStruct((2, BLOCK, WIDTH), BF16)
KEY_MESSAGE = jax.ShapeDtypeStruct((2, BLOCK + HALF, WIDTH), BF16)


def staged(count):
    return (
        [pltpu.VMEM((SIDE + 2, BLOCK, WIDTH), BF16)] * 2
        + [pltpu.VMEM((count, BLOCK, WIDTH), BF16)] * 2
        + [pltpu.VMEM((count, HALF, WIDTH), BF16)] * 2
    )


def grads_scratch(count):
    return (
        staged(count)
        + [pltpu.VMEM((HEADS_LOCAL, count * BLOCK, HDIM), F32)] * 2
        + [pltpu.VMEM((count, HEADS_LOCAL, HALF, HDIM), F32)] * 2
        + [pltpu.VMEM((count * BLOCK, VIDEO_ROWS), BF16)] * 2
    )


def placed(arrays, space=pltpu.VMEM):
    return [pltpu.with_memory_space_constraint(a, space) for a in arrays]


def cost(blocks, matmuls):
    pairs = HEADS_LOCAL * VIDEO_ROWS * BLOCK * blocks
    return pl.CostEstimate(flops=2 * HDIM * matmuls * pairs, bytes_accessed=8 * 1024 * 1024, transcendentals=pairs)


def stats_call(blocks, scalars, acc, qg, kv, text_qg):
    last = len(acc)
    return pl.pallas_call(
        functools.partial(stats_kernel, blocks, last),
        in_specs=[SMEM_SPEC] * 3 + [VMEM_SPEC] * (last + 2 * SIDE + len(blocks)),
        out_specs=VMEM_SPEC,
        out_shape=jax.ShapeDtypeStruct((2, HEADS_LOCAL, ROWS) if last else STATS, F32),
        scratch_shapes=staged(len(blocks)) + [pltpu.VMEM(STATS, F32)] * last,
        compiler_params=PARAMS,
        cost_estimate=cost(len(blocks), 2),
        name="stats_last" if last else "stats_first",
    )(*scalars, *placed([*acc, *qg, *[kv[i] for i in blocks]]), *placed(text_qg, pltpu.HBM))


def grads_first_call(blocks, scalars, qg, kv, text_qg, stats):
    count = len(blocks)
    *dkv, dq_t, norm = pl.pallas_call(
        functools.partial(grads_first_kernel, blocks),
        in_specs=[SMEM_SPEC] * 3 + [VMEM_SPEC] * (3 * SIDE + count),
        out_specs=[VMEM_SPEC] * (count + 2),
        out_shape=[KEY_MESSAGE] * count
        + [jax.ShapeDtypeStruct(DQ_T, F32), jax.ShapeDtypeStruct((2, HEADS_LOCAL, ROWS), F32)],
        scratch_shapes=grads_scratch(count),
        compiler_params=PARAMS,
        cost_estimate=cost(count, 5),
        name="grads_first",
    )(*scalars, *placed([*qg, *[kv[i] for i in blocks], *stats]), *placed(text_qg, pltpu.HBM))
    return dkv, dq_t, norm


def grads_last_call(blocks, scalars, qg, kv, text_qg, dq_t, norm):
    count = len(blocks)
    out = pl.pallas_call(
        functools.partial(grads_last_kernel, blocks),
        in_specs=[SMEM_SPEC] * 3 + [VMEM_SPEC] * (2 * SIDE + count + 2),
        out_specs=[VMEM_SPEC] * (SIDE + count),
        out_shape=[jax.ShapeDtypeStruct((HEADS_LOCAL, HDIM, BLOCK + HALF), BF16)] * SIDE + [KEY_MESSAGE] * count,
        scratch_shapes=[pltpu.VMEM(DQ_T, F32)] + grads_scratch(count),
        compiler_params=PARAMS,
        cost_estimate=cost(count, 5),
        name="grads_last",
    )(*scalars, *placed([norm]), dq_t, *placed(qg, pltpu.HBM), *placed([kv[i] for i in blocks]), *placed(text_qg, pltpu.HBM))
    return out[:SIDE], out[SIDE:]


def swap(array, axis, step):
    shift = step if axis == "y" else step * SIDE
    return lax.ppermute(array, "seq", [(i, i ^ shift) for i in range(SIDE * SIDE)])


def gathered(array, axis):
    return [array] + [swap(array, axis, step) for step in range(1, SIDE)]


def on_device(
    video_query,
    video_key,
    video_value,
    video_grad,
    text_query,
    text_key,
    text_value,
    text_grad,
    shot_length,
    caption_length,
):
    place = lax.axis_index("seq").astype(jnp.int32)
    scalars = (shot_length, caption_length, place.reshape(1))
    packed, text_qg = pack(video_query, video_key, video_value, video_grad, text_query, text_grad)
    text_qg = gathered(text_qg, "y")
    arrived = lax.all_to_all(packed, "head", split_axis=0, concat_axis=0)
    arrived, text_qg = lax.optimization_barrier((arrived, text_qg))
    qg, kv = assemble(arrived, text_key, text_value)
    qg = gathered(qg, "y")
    kv1, kv3 = swap(kv, "z", 1), swap(kv, "z", 3)
    later, qg = lax.optimization_barrier((kv, qg))
    kv = [kv, kv1, swap(later, "z", 2), kv3]

    acc = stats_call((0, 1, 3), scalars, [], qg, kv, text_qg)
    stats = gathered(stats_call((2,), scalars, [acc], qg, kv, text_qg), "y")
    (dkv1, dkv3), dq_t, norm = grads_first_call((1, 3), scalars, qg, kv, text_qg, stats)
    dq, (dkv2, dkv0) = grads_last_call((2, 0), scalars, qg, kv, text_qg, dq_t, norm)

    dkv1, dkv3 = swap(dkv1, "z", 1), swap(dkv3, "z", 3)
    dq, dkv1, dkv2 = lax.optimization_barrier((dq, dkv1, dkv2))
    dq = [dq[0]] + [swap(dq[step], "y", step) for step in range(1, SIDE)]
    dkv = [dkv0, dkv1, swap(dkv2, "z", 2), dkv3]
    video, *text = sum_terms(dq, dkv)
    video_back = unpack(lax.all_to_all(video, "head", split_axis=0, concat_axis=0))
    return (*video_back, *text)


def solution(mesh):
    video = P(("seq", "head"), None)
    text = P("seq", "head")
    return jax.shard_map(
        on_device,
        mesh=mesh,
        in_specs=(video,) * 4 + (text,) * 4 + (P(), P()),
        out_specs=(video,) * 3 + (text,) * 3,
        check_vma=False,
    )
```

```python
import functools

import jax
import jax.numpy as jnp
from jax import lax
from jax.experimental import pallas as pl
from jax.experimental.pallas import tpu as pltpu
from jax.sharding import PartitionSpec as P

HDIM = 128
CAP = 256
NSHOT = 8
HEADS_LOCAL = 3
WIDTH = HEADS_LOCAL * HDIM
GROUP = 8
SIDE = 4
OWN = 32
BLOCK = GROUP * OWN
HALF = 128
VIDEO_ROWS = SIDE * BLOCK
TEXT_ROWS = SIDE * HALF
ROWS = VIDEO_ROWS + TEXT_ROWS
SCALE = HDIM ** (-0.5)
LOG2E = 1.4426950408889634
TO_LOG2 = SCALE * LOG2E
LOW = -1e30
F32 = jnp.float32
BF16 = jnp.bfloat16
VMEM_LIMIT = 24 * 1024 * 1024


def dot_nt(a, b):
    return lax.dot_general(a, b, (((1,), (1,)), ((), ())), preferred_element_type=F32)


def dot_nn(a, b):
    return lax.dot_general(a, b, (((1,), (0,)), ((), ())), preferred_element_type=F32)


def pack_kernel(q_ref, k_ref, v_ref, g_ref, tq_ref, tg_ref, out_ref, text_qg_ref):
    for d in range(GROUP):
        cols = slice(d * WIDTH, (d + 1) * WIDTH)
        for n, ref in enumerate((q_ref, g_ref, k_ref, v_ref)):
            out_ref[d, n] = ref[:, cols]
    text_qg_ref[0] = tq_ref[...]
    text_qg_ref[1] = tg_ref[...]


def pack(*arrays):
    video = jax.ShapeDtypeStruct((GROUP, 4, OWN, WIDTH), BF16)
    text = jax.ShapeDtypeStruct((2, HALF, WIDTH), BF16)
    call = pl.pallas_call(pack_kernel, out_shape=(video, text), compiler_params=SMALL, name="pack_inputs")
    return call(*placed(arrays, pltpu.HBM))


def assemble_kernel(in_ref, tk_ref, tv_ref, qg_ref, kv_ref):
    for n in range(2):
        qg_ref[n] = in_ref[:, n].reshape(BLOCK, WIDTH)
        kv_ref[n, :BLOCK] = in_ref[:, 2 + n].reshape(BLOCK, WIDTH)
    kv_ref[0, BLOCK:] = tk_ref[...]
    kv_ref[1, BLOCK:] = tv_ref[...]


def assemble(arrived, text_key, text_value):
    return pl.pallas_call(
        assemble_kernel,
        out_shape=(QUERY_MESSAGE, KEY_MESSAGE),
        compiler_params=SMALL,
        name="assemble_blocks",
    )(*placed([arrived]), text_key, text_value)


def unpack_kernel(in_ref, q_ref, k_ref, v_ref):
    for d in range(GROUP):
        cols = slice(d * WIDTH, (d + 1) * WIDTH)
        q_ref[:, cols] = in_ref[d, 0]
        k_ref[:, cols] = in_ref[d, 1]
        v_ref[:, cols] = in_ref[d, 2]


def unpack(arrived):
    shape = jax.ShapeDtypeStruct((OWN, GROUP * WIDTH), BF16)
    return pl.pallas_call(unpack_kernel, out_shape=(shape, shape, shape), compiler_params=SMALL, name="unpack_video")(*placed([arrived]))


def head_cols(h):
    return slice(h * HDIM, (h + 1) * HDIM)


def sum_kernel(*refs):
    dq, dkv = refs[:SIDE], refs[SIDE : 2 * SIDE]
    out, *text_out = refs[2 * SIDE :]
    for h in range(HEADS_LOCAL):
        total = jnp.transpose(sum(r[h].astype(F32) for r in dq).astype(BF16))
        out[:, 0, :, head_cols(h)] = total[:BLOCK].reshape(GROUP, OWN, HDIM)
        text_out[0][:, head_cols(h)] = total[BLOCK:]
    for n in range(2):
        total = sum(r[n].astype(F32) for r in dkv).astype(BF16)
        out[:, 1 + n] = total[:BLOCK].reshape(GROUP, OWN, WIDTH)
        text_out[1 + n][...] = total[BLOCK:]


def sum_terms(dq, dkv):
    return pl.pallas_call(
        sum_kernel,
        out_shape=[jax.ShapeDtypeStruct((GROUP, 3, OWN, WIDTH), BF16)]
        + [jax.ShapeDtypeStruct((HALF, WIDTH), BF16)] * 3,
        compiler_params=SMALL,
        name="sum_terms",
    )(*placed([*dq, *dkv]))


class Labels:
    def __init__(self, length_ref, caption_ref, place_ref):
        place = place_ref[0]
        self.z = place // SIDE
        self.y = place % SIDE
        self.caption_ref = caption_ref
        starts = [jnp.int32(0)]
        for s in range(NSHOT):
            starts.append(starts[-1] + length_ref[s])
        self.starts = starts

    def span(self, shot):
        begin = jnp.int32(0)
        end = jnp.int32(0)
        for s in range(NSHOT):
            begin = jnp.where(shot == s, self.starts[s], begin)
            end = jnp.where(shot == s, self.starts[s + 1], end)
        return begin, end

    def query_base(self, j):
        return (self.z * SIDE + (self.y ^ j)) * BLOCK

    def key_base(self, i):
        return ((self.z ^ i) * SIDE + self.y) * BLOCK

    def query_shot(self, p):
        return self.z * 2 + (self.y ^ (2 * p)) // 2

    def key_shot(self, t):
        return (self.z ^ t) * 2 + self.y // 2

    def live(self, shot, half):
        row = half * HALF + lax.broadcasted_iota(jnp.int32, (HALF, 1), 0)
        return row < self.caption_ref[shot]


def stage_queries(labels, qg, text_qg, q_all, g_all):
    for j in range(SIDE):
        q_all[j] = qg[j][0]
        g_all[j] = qg[j][1]
    for u in range(SIDE):
        p, rows = u // 2, slice(u % 2 * HALF, (u % 2 + 1) * HALF)
        q_all[SIDE + p, rows] = text_qg[u][0]
        live = labels.live(labels.query_shot(p), (labels.y ^ u) % 2)
        g_all[SIDE + p, rows] = jnp.where(live, text_qg[u][1], jnp.zeros((HALF, WIDTH), BF16))


def stage_keys(kv, k_all, v_all, tk_all, tv_all):
    for i, ref in enumerate(kv):
        k_all[i] = ref[0, :BLOCK]
        v_all[i] = ref[1, :BLOCK]
        tk_all[i] = ref[0, BLOCK:]
        tv_all[i] = ref[1, BLOCK:]


def loop(count, step):
    lax.fori_loop(0, count, lambda n, c: (step(n), c)[1], 0)


def chosen(blocks, n):
    return sum(jnp.where(n == m, block, 0) for m, block in enumerate(blocks))


def text_keys(labels, blocks, visit):
    def step(n):
        t, j = n // SIDE, n % SIDE
        shot, base = labels.key_shot(chosen(blocks, t)), labels.query_base(j)
        begin, end = labels.span(shot)

        @pl.when(jnp.logical_and(begin < base + BLOCK, end > base))
        def _():
            row = base + lax.broadcasted_iota(jnp.int32, (1, BLOCK), 1)
            same = jnp.logical_and(row >= begin, row < end)
            visit(t, j, jnp.logical_and(labels.live(shot, labels.y % 2), same))

    loop(len(blocks) * SIDE, step)
    if 0 in blocks:
        live = labels.live(labels.key_shot(0), labels.y % 2)
        visit(blocks.index(0), SIDE, jnp.broadcast_to(live, (HALF, BLOCK)))


def text_queries(labels, blocks, visit):
    def step(n):
        i, p = n // 2, n % 2
        base = labels.key_base(chosen(blocks, i))
        begin, end = labels.span(labels.query_shot(p))

        @pl.when(jnp.logical_and(begin < base + BLOCK, end > base))
        def _():
            row = base + lax.broadcasted_iota(jnp.int32, (BLOCK, 1), 0)
            same = jnp.logical_and(row >= begin, row < end)
            visit(i, p, jnp.broadcast_to(same, (BLOCK, BLOCK)))

    loop(2 * len(blocks), step)


def head_ds(h):
    return pl.ds(pl.multiple_of(h * HDIM, HDIM), HDIM)


def rows_ds(j):
    return pl.ds(pl.multiple_of(j * BLOCK, BLOCK), BLOCK)


def query_cols(j):
    return slice(j * BLOCK, (j + 1) * BLOCK)


def stats_kernel(blocks, last, length_ref, caption_ref, place_ref, *refs):
    kv, refs = refs[: len(blocks)], refs[len(blocks) :]
    labels = Labels(length_ref, caption_ref, place_ref)
    if last:
        acc_in, q_all, g_all, out_ref, k_all, v_all, tk_all, tv_all, *scratch = refs
    else:
        qg, text_qg = refs[:SIDE], refs[SIDE : 2 * SIDE]
        out_ref, q_all, g_all, k_all, v_all, tk_all, tv_all, *scratch = refs[2 * SIDE :]
        stage_queries(labels, qg, text_qg, q_all, g_all)
    stage_keys(kv, k_all, v_all, tk_all, tv_all)
    if last:
        acc = scratch[0]
        acc[...] = acc_in[...]
    else:
        acc = out_ref
        acc[0] = jnp.full((HEADS_LOCAL, ROWS), LOW, F32)
        acc[1:3] = jnp.zeros((2, HEADS_LOCAL, ROWS), F32)

    def head(h):
        c, row = head_ds(h), pl.ds(h, 1)
        keys = k_all[:, :, c].reshape(len(blocks) * BLOCK, HDIM)
        values = v_all[:, :, c].reshape(len(blocks) * BLOCK, HDIM)
        for j in range(SIDE):
            cols = query_cols(j)
            scores = dot_nt(keys, q_all[j, :, c])
            dprob = dot_nt(values, g_all[j, :, c])
            top = jnp.max(scores, axis=0, keepdims=True) * TO_LOG2
            if last:
                before = acc[0, row, cols]
                top = jnp.maximum(before, top)
                shrink = jnp.exp2(before - top)
            weight = jnp.exp2(scores * TO_LOG2 - top)
            total = jnp.sum(weight, axis=0, keepdims=True)
            weighted = jnp.sum(weight * dprob, axis=0, keepdims=True)
            if last:
                total += acc[1, row, cols] * shrink
                weighted += acc[2, row, cols] * shrink
            acc[0, row, cols] = top
            acc[1, row, cols] = total
            acc[2, row, cols] = weighted

    loop(HEADS_LOCAL, head)

    def visit(keys_ref, values_ref, n, j, mask):
        cols = rows_ds(j)
        results = []
        for h in range(HEADS_LOCAL):
            c = head_cols(h)
            scores = jnp.where(mask, dot_nt(keys_ref[n, :, c], q_all[j, :, c]) * TO_LOG2, LOW)
            dprob = dot_nt(values_ref[n, :, c], g_all[j, :, c])
            before = acc[0, h : h + 1, cols]
            top = jnp.maximum(before, jnp.max(scores, axis=0, keepdims=True))
            weight = jnp.where(mask, jnp.exp2(scores - top), 0.0)
            shrink = jnp.exp2(before - top)
            results.append(
                (
                    top,
                    acc[1, h : h + 1, cols] * shrink + jnp.sum(weight, axis=0, keepdims=True),
                    acc[2, h : h + 1, cols] * shrink + jnp.sum(weight * dprob, axis=0, keepdims=True),
                )
            )
        for h in range(HEADS_LOCAL):
            for n in range(3):
                acc[n, h : h + 1, cols] = results[h][n]

    text_keys(labels, blocks, lambda t, j, mask: visit(tk_all, tv_all, t, j, mask))
    text_queries(labels, blocks, lambda i, p, mask: visit(k_all, v_all, i, SIDE + p, mask))
    if last:
        total = acc[1]
        some = total > 0.0
        total = jnp.where(some, total, 1.0)
        out_ref[0] = jnp.where(some, acc[0] + jnp.log2(total), LOW)
        out_ref[1] = acc[2] / total


def normalize(stats, norm):
    for j in range(SIDE + 2):
        parts = []
        for e in range(SIDE):
            if j < SIDE:
                parts.append([stats[e][n, :, query_cols(j ^ e)] for n in range(2)])
            else:
                halves = []
                for u in (2 * (j - SIDE), 2 * (j - SIDE) + 1):
                    at = VIDEO_ROWS + (u ^ e) * HALF
                    halves.append([stats[e][n, :, at : at + HALF] for n in range(2)])
                parts.append([jnp.concatenate([halves[0][n], halves[1][n]], 1) for n in range(2)])
        top = functools.reduce(jnp.maximum, [p[0] for p in parts])
        share = [jnp.exp2(p[0] - top) for p in parts]
        total = sum(share)
        delta = sum(p[1] * s for p, s in zip(parts, share)) / total
        norm[0, :, query_cols(j)] = top + jnp.log2(total)
        norm[1, :, query_cols(j)] = delta


def key_grads(labels, blocks, fresh, q_all, g_all, kv, dkv_out, norm, dq_t, scratch):
    count = len(blocks)
    k_all, v_all, tk_all, tv_all, dk, dv, text_dk, text_dv, p_all, ds_all = scratch
    stage_keys(kv, k_all, v_all, tk_all, tv_all)
    text_dk[...] = jnp.zeros((count, HEADS_LOCAL, HALF, HDIM), F32)
    text_dv[...] = jnp.zeros((count, HEADS_LOCAL, HALF, HDIM), F32)
    rows = count * BLOCK

    def head(h):
        c, row = head_ds(h), pl.ds(h, 1)
        keys = k_all[:, :, c].reshape(rows, HDIM)
        values = v_all[:, :, c].reshape(rows, HDIM)
        keys_t = jnp.transpose(keys)
        for j in range(SIDE):
            cols = query_cols(j)
            scores = dot_nt(keys, q_all[j, :, c])
            dprob = dot_nt(values, g_all[j, :, c])
            probs = jnp.exp2(scores * TO_LOG2 - norm[0, row, cols])
            dscore = (probs * (dprob - norm[1, row, cols])).astype(BF16)
            p_all[:, cols] = probs.astype(BF16)
            ds_all[:, cols] = dscore
            part = dot_nn(keys_t, dscore)
            if fresh:
                dq_t[h, :, cols] = part
            else:
                dq_t[h, :, cols] += part
        dv[h] = dot_nn(p_all[...], g_all[:SIDE, :, c].reshape(VIDEO_ROWS, HDIM))
        dk[h] = dot_nn(ds_all[...], q_all[:SIDE, :, c].reshape(VIDEO_ROWS, HDIM))

    loop(HEADS_LOCAL, head)

    def visit(keys_ref, values_ref, n, j, mask, add):
        cols = rows_ds(j)
        results = []
        for h in range(HEADS_LOCAL):
            c = head_cols(h)
            keys, queries, grads = keys_ref[n, :, c], q_all[j, :, c], g_all[j, :, c]
            scores = dot_nt(keys, queries) * TO_LOG2
            dprob = dot_nt(values_ref[n, :, c], grads)
            probs = jnp.where(mask, jnp.exp2(jnp.where(mask, scores, LOW) - norm[0, h : h + 1, cols]), 0.0)
            low = probs.astype(BF16)
            dscore = (probs * (dprob - norm[1, h : h + 1, cols])).astype(BF16)
            results.append((dot_nn(dscore, queries), dot_nn(low, grads), dot_nn(jnp.transpose(keys), dscore)))
        for h in range(HEADS_LOCAL):
            add(n, h, results[h][0], results[h][1])
            dq_t[h, :, cols] += results[h][2]

    def add_text(n, h, key_part, value_part):
        text_dk[n, h] += key_part
        text_dv[n, h] += value_part

    def add_video(n, h, key_part, value_part):
        dk[h, rows_ds(n)] += key_part
        dv[h, rows_ds(n)] += value_part

    text_keys(labels, blocks, lambda t, j, mask: visit(tk_all, tv_all, t, j, mask, add_text))
    text_queries(labels, blocks, lambda i, p, mask: visit(k_all, v_all, i, SIDE + p, mask, add_video))

    for i in range(count):
        for h in range(HEADS_LOCAL):
            c = head_cols(h)
            dkv_out[i][0, :BLOCK, c] = (dk[h, query_cols(i)] * SCALE).astype(BF16)
            dkv_out[i][1, :BLOCK, c] = dv[h, query_cols(i)].astype(BF16)
            dkv_out[i][0, BLOCK:, c] = (text_dk[i, h] * SCALE).astype(BF16)
            dkv_out[i][1, BLOCK:, c] = text_dv[i, h].astype(BF16)


def grads_first_kernel(blocks, length_ref, caption_ref, place_ref, *refs):
    count = len(blocks)
    q_all, g_all, kv, refs = refs[0], refs[1], refs[2 : 2 + count], refs[2 + count :]
    stats, dkv_out, (dq_t, norm, *scratch) = refs[:SIDE], refs[SIDE : SIDE + count], refs[SIDE + count :]
    labels = Labels(length_ref, caption_ref, place_ref)
    normalize(stats, norm)
    dq_t[:, :, VIDEO_ROWS:] = jnp.zeros((HEADS_LOCAL, HDIM, TEXT_ROWS), F32)
    key_grads(labels, blocks, True, q_all, g_all, kv, dkv_out, norm, dq_t, scratch)


def grads_last_kernel(blocks, length_ref, caption_ref, place_ref, *refs):
    count = len(blocks)
    norm, dq_in, q_all, g_all, kv, refs = *refs[:4], refs[4 : 4 + count], refs[4 + count :]
    dq_out, dkv_out, (dq_t, *scratch) = refs[:SIDE], refs[SIDE : SIDE + count], refs[SIDE + count :]
    labels = Labels(length_ref, caption_ref, place_ref)
    dq_t[...] = dq_in[...]
    key_grads(labels, blocks, False, q_all, g_all, kv, dkv_out, norm, dq_t, scratch)
    for n in range(SIDE):
        dq_out[n][:, :, :BLOCK] = (dq_t[:, :, query_cols(n)] * SCALE).astype(BF16)
        dq_out[n][:, :, BLOCK:] = (dq_t[:, :, VIDEO_ROWS + n * HALF : VIDEO_ROWS + (n + 1) * HALF] * SCALE).astype(BF16)


SMEM_SPEC = pl.BlockSpec(memory_space=pltpu.SMEM)
VMEM_SPEC = pl.BlockSpec(memory_space=pltpu.VMEM)
PARAMS = pltpu.CompilerParams(vmem_limit_bytes=VMEM_LIMIT)
SMALL = pltpu.CompilerParams(vmem_limit_bytes=8 * 1024 * 1024)
DQ_T = (HEADS_LOCAL, HDIM, ROWS)
STATS = (3, HEADS_LOCAL, ROWS)
STAGED_QUERIES = jax.ShapeDtypeStruct((SIDE + 2, BLOCK, WIDTH), BF16)
QUERY_MESSAGE = jax.ShapeDtypeStruct((2, BLOCK, WIDTH), BF16)
KEY_MESSAGE = jax.ShapeDtypeStruct((2, BLOCK + HALF, WIDTH), BF16)


def staged(count):
    return [pltpu.VMEM((count, BLOCK, WIDTH), BF16)] * 2 + [pltpu.VMEM((count, HALF, WIDTH), BF16)] * 2


def grads_scratch(count):
    return (
        staged(count)
        + [pltpu.VMEM((HEADS_LOCAL, count * BLOCK, HDIM), F32)] * 2
        + [pltpu.VMEM((count, HEADS_LOCAL, HALF, HDIM), F32)] * 2
        + [pltpu.VMEM((count * BLOCK, VIDEO_ROWS), BF16)] * 2
    )


def placed(arrays, space=pltpu.VMEM):
    return [pltpu.with_memory_space_constraint(a, space) for a in arrays]


def cost(blocks, matmuls):
    pairs = HEADS_LOCAL * VIDEO_ROWS * BLOCK * blocks
    return pl.CostEstimate(flops=2 * HDIM * matmuls * pairs, bytes_accessed=8 * 1024 * 1024, transcendentals=pairs)


def stats_first_call(blocks, scalars, qg, kv, text_qg):
    return pl.pallas_call(
        functools.partial(stats_kernel, blocks, False),
        in_specs=[SMEM_SPEC] * 3 + [VMEM_SPEC] * (2 * SIDE + len(blocks)),
        out_specs=[VMEM_SPEC] * 3,
        out_shape=[jax.ShapeDtypeStruct(STATS, F32), STAGED_QUERIES, STAGED_QUERIES],
        scratch_shapes=staged(len(blocks)),
        compiler_params=PARAMS,
        cost_estimate=cost(len(blocks), 2),
        name="stats_first",
    )(*scalars, *placed([kv[i] for i in blocks] + qg), *placed(text_qg, pltpu.HBM))


def stats_last_call(blocks, scalars, acc, queries, kv):
    return pl.pallas_call(
        functools.partial(stats_kernel, blocks, True),
        in_specs=[SMEM_SPEC] * 3 + [VMEM_SPEC] * (3 + len(blocks)),
        out_specs=VMEM_SPEC,
        out_shape=jax.ShapeDtypeStruct((2, HEADS_LOCAL, ROWS), F32),
        scratch_shapes=staged(len(blocks)) + [pltpu.VMEM(STATS, F32)],
        compiler_params=PARAMS,
        cost_estimate=cost(len(blocks), 2),
        name="stats_last",
    )(*scalars, *placed([*[kv[i] for i in blocks], acc, *queries]))


def grads_first_call(blocks, scalars, queries, kv, stats):
    count = len(blocks)
    *dkv, dq_t, norm = pl.pallas_call(
        functools.partial(grads_first_kernel, blocks),
        in_specs=[SMEM_SPEC] * 3 + [VMEM_SPEC] * (2 + SIDE + count),
        out_specs=[VMEM_SPEC] * (count + 2),
        out_shape=[KEY_MESSAGE] * count
        + [jax.ShapeDtypeStruct(DQ_T, F32), jax.ShapeDtypeStruct((2, HEADS_LOCAL, ROWS), F32)],
        scratch_shapes=grads_scratch(count),
        compiler_params=PARAMS,
        cost_estimate=cost(count, 5),
        name="grads_first",
    )(*scalars, *placed([*queries, *[kv[i] for i in blocks], *stats]))
    return dkv, dq_t, norm


def grads_last_call(blocks, scalars, queries, kv, dq_t, norm):
    count = len(blocks)
    out = pl.pallas_call(
        functools.partial(grads_last_kernel, blocks),
        in_specs=[SMEM_SPEC] * 3 + [VMEM_SPEC] * (4 + count),
        out_specs=[VMEM_SPEC] * (SIDE + count),
        out_shape=[jax.ShapeDtypeStruct((HEADS_LOCAL, HDIM, BLOCK + HALF), BF16)] * SIDE + [KEY_MESSAGE] * count,
        scratch_shapes=[pltpu.VMEM(DQ_T, F32)] + grads_scratch(count),
        compiler_params=PARAMS,
        cost_estimate=cost(count, 5),
        name="grads_last",
    )(*scalars, *placed([norm]), dq_t, *placed([*queries, *[kv[i] for i in blocks]]))
    return out[:SIDE], out[SIDE:]


def swap(array, axis, step):
    shift = step if axis == "y" else step * SIDE
    return lax.ppermute(array, "seq", [(i, i ^ shift) for i in range(SIDE * SIDE)])


def gathered(array, axis):
    return [array] + [swap(array, axis, step) for step in range(1, SIDE)]


def on_device(
    video_query,
    video_key,
    video_value,
    video_grad,
    text_query,
    text_key,
    text_value,
    text_grad,
    shot_length,
    caption_length,
):
    place = lax.axis_index("seq").astype(jnp.int32)
    scalars = (shot_length, caption_length, place.reshape(1))
    packed, text_qg = pack(video_query, video_key, video_value, video_grad, text_query, text_grad)
    text_qg = gathered(text_qg, "y")
    arrived = lax.all_to_all(packed, "head", split_axis=0, concat_axis=0)
    arrived, text_qg = lax.optimization_barrier((arrived, text_qg))
    qg, kv = assemble(arrived, text_key, text_value)
    qg = gathered(qg, "y")
    kv1, kv3 = swap(kv, "z", 1), swap(kv, "z", 3)
    later, qg[1], qg[3] = lax.optimization_barrier((kv, qg[1], qg[3]))
    kv = [kv, kv1, swap(later, "z", 2), kv3]

    acc, *queries = stats_first_call((0, 1, 3), scalars, qg, kv, text_qg)
    stats = gathered(stats_last_call((2,), scalars, acc, queries, kv), "y")
    (dkv1, dkv3), dq_t, norm = grads_first_call((1, 3), scalars, queries, kv, stats)
    dq, (dkv2, dkv0) = grads_last_call((2, 0), scalars, queries, kv, dq_t, norm)

    dkv1, dkv3 = swap(dkv1, "z", 1), swap(dkv3, "z", 3)
    dq, dkv1, dkv2 = lax.optimization_barrier((dq, dkv1, dkv2))
    dq = [dq[0]] + [swap(dq[step], "y", step) for step in range(1, SIDE)]
    dkv = [dkv0, dkv1, swap(dkv2, "z", 2), dkv3]
    video, *text = sum_terms(dq, dkv)
    video_back = unpack(lax.all_to_all(video, "head", split_axis=0, concat_axis=0))
    return (*video_back, *text)


def solution(mesh):
    video = P(("seq", "head"), None)
    text = P("seq", "head")
    return jax.shard_map(
        on_device,
        mesh=mesh,
        in_specs=(video,) * 4 + (text,) * 4 + (P(), P()),
        out_specs=(video,) * 3 + (text,) * 3,
        check_vma=False,
    )
```

```python
import functools

import jax
import jax.numpy as jnp
from jax import lax
from jax.experimental import pallas as pl
from jax.experimental.pallas import tpu as pltpu
from jax.sharding import PartitionSpec as P

HDIM = 128
CAP = 256
NSHOT = 8
HEADS_LOCAL = 3
WIDTH = HEADS_LOCAL * HDIM
GROUP = 8
SIDE = 4
OWN = 32
BLOCK = GROUP * OWN
HALF = 128
VIDEO_ROWS = SIDE * BLOCK
TEXT_ROWS = SIDE * HALF
ROWS = VIDEO_ROWS + TEXT_ROWS
SCALE = HDIM ** (-0.5)
LOG2E = 1.4426950408889634
TO_LOG2 = SCALE * LOG2E
LOW = -1e30
F32 = jnp.float32
BF16 = jnp.bfloat16
VMEM_LIMIT = 16 * 1024 * 1024


def dot_nt(a, b):
    return lax.dot_general(a, b, (((1,), (1,)), ((), ())), preferred_element_type=F32)


def dot_nn(a, b):
    return lax.dot_general(a, b, (((1,), (0,)), ((), ())), preferred_element_type=F32)


def pack_kernel(q_ref, k_ref, v_ref, g_ref, tq_ref, tg_ref, out_ref, text_qg_ref):
    for d in range(GROUP):
        cols = slice(d * WIDTH, (d + 1) * WIDTH)
        for n, ref in enumerate((q_ref, g_ref, k_ref, v_ref)):
            out_ref[d, n] = ref[:, cols]
    text_qg_ref[0] = tq_ref[...]
    text_qg_ref[1] = tg_ref[...]


def pack(*arrays):
    video = jax.ShapeDtypeStruct((GROUP, 4, OWN, WIDTH), BF16)
    text = jax.ShapeDtypeStruct((2, HALF, WIDTH), BF16)
    call = pl.pallas_call(pack_kernel, out_shape=(video, text), compiler_params=SMALL, name="pack_inputs")
    return call(*placed(arrays, pltpu.HBM))


def assemble_kernel(in_ref, tk_ref, tv_ref, qg_ref, kv_ref):
    for n in range(2):
        qg_ref[n] = in_ref[:, n].reshape(BLOCK, WIDTH)
        kv_ref[n, :BLOCK] = in_ref[:, 2 + n].reshape(BLOCK, WIDTH)
    kv_ref[0, BLOCK:] = tk_ref[...]
    kv_ref[1, BLOCK:] = tv_ref[...]


def assemble(arrived, text_key, text_value):
    return pl.pallas_call(
        assemble_kernel,
        out_shape=(QUERY_MESSAGE, KEY_MESSAGE),
        compiler_params=SMALL,
        name="assemble_blocks",
    )(*placed([arrived]), text_key, text_value)


def unpack_kernel(in_ref, q_ref, k_ref, v_ref):
    for d in range(GROUP):
        cols = slice(d * WIDTH, (d + 1) * WIDTH)
        q_ref[:, cols] = in_ref[d, 0]
        k_ref[:, cols] = in_ref[d, 1]
        v_ref[:, cols] = in_ref[d, 2]


def unpack(arrived):
    shape = jax.ShapeDtypeStruct((OWN, GROUP * WIDTH), BF16)
    return pl.pallas_call(unpack_kernel, out_shape=(shape, shape, shape), compiler_params=SMALL, name="unpack_video")(*placed([arrived]))


def head_cols(h):
    return slice(h * HDIM, (h + 1) * HDIM)


def sum_kernel(*refs):
    dq, dkv = refs[:SIDE], refs[SIDE : 2 * SIDE]
    out, *text_out = refs[2 * SIDE :]
    for h in range(HEADS_LOCAL):
        total = jnp.transpose(sum(r[h].astype(F32) for r in dq).astype(BF16))
        out[:, 0, :, head_cols(h)] = total[:BLOCK].reshape(GROUP, OWN, HDIM)
        text_out[0][:, head_cols(h)] = total[BLOCK:]
    for n in range(2):
        total = sum(r[n].astype(F32) for r in dkv).astype(BF16)
        out[:, 1 + n] = total[:BLOCK].reshape(GROUP, OWN, WIDTH)
        text_out[1 + n][...] = total[BLOCK:]


def sum_terms(dq, dkv):
    return pl.pallas_call(
        sum_kernel,
        out_shape=[jax.ShapeDtypeStruct((GROUP, 3, OWN, WIDTH), BF16)]
        + [jax.ShapeDtypeStruct((HALF, WIDTH), BF16)] * 3,
        compiler_params=SMALL,
        name="sum_terms",
    )(*placed([*dq, *dkv]))


class Labels:
    def __init__(self, length_ref, caption_ref, place_ref):
        place = place_ref[0]
        self.z = place // SIDE
        self.y = place % SIDE
        self.caption_ref = caption_ref
        starts = [jnp.int32(0)]
        for s in range(NSHOT):
            starts.append(starts[-1] + length_ref[s])
        self.starts = starts

    def span(self, shot):
        begin = jnp.int32(0)
        end = jnp.int32(0)
        for s in range(NSHOT):
            begin = jnp.where(shot == s, self.starts[s], begin)
            end = jnp.where(shot == s, self.starts[s + 1], end)
        return begin, end

    def query_base(self, j):
        return (self.z * SIDE + (self.y ^ j)) * BLOCK

    def key_base(self, i):
        return ((self.z ^ i) * SIDE + self.y) * BLOCK

    def query_shot(self, p):
        return self.z * 2 + (self.y ^ (2 * p)) // 2

    def key_shot(self, t):
        return (self.z ^ t) * 2 + self.y // 2

    def live(self, shot, half):
        row = half * HALF + lax.broadcasted_iota(jnp.int32, (HALF, 1), 0)
        return row < self.caption_ref[shot]


def stage_text_queries(labels, text_qg, q_all, g_all):
    for u in range(SIDE):
        p, rows = u // 2, slice(u % 2 * HALF, (u % 2 + 1) * HALF)
        q_all[SIDE + p, rows] = text_qg[u][0]
        live = labels.live(labels.query_shot(p), (labels.y ^ u) % 2)
        g_all[SIDE + p, rows] = jnp.where(live, text_qg[u][1], jnp.zeros((HALF, WIDTH), BF16))


VIDEO_PART = slice(0, BLOCK)
TEXT_PART = slice(BLOCK, BLOCK + HALF)


def joined(kv, which, c):
    return jnp.concatenate([ref[which, VIDEO_PART, c] for ref in kv], 0)


def loop(count, step):
    lax.fori_loop(0, count, lambda n, c: (step(n), c)[1], 0)


def chosen(blocks, n):
    return sum(jnp.where(n == m, block, 0) for m, block in enumerate(blocks))


def text_keys(labels, blocks, queries, visit):
    for n, block in enumerate(blocks):
        shot = labels.key_shot(block)
        begin, end = labels.span(shot)

        def step(m, n=n, shot=shot, begin=begin, end=end):
            j = queries[0] if len(queries) == 1 else chosen(queries, m)
            base = labels.query_base(j)

            @pl.when(jnp.logical_and(begin < base + BLOCK, end > base))
            def _():
                row = base + lax.broadcasted_iota(jnp.int32, (1, BLOCK), 1)
                same = jnp.logical_and(row >= begin, row < end)
                visit(n, j, jnp.logical_and(labels.live(shot, labels.y % 2), same))

        loop(len(queries), step)


def own_text(labels, n, visit):
    live = labels.live(labels.key_shot(0), labels.y % 2)
    visit(n, SIDE, jnp.broadcast_to(live, (HALF, BLOCK)))


def text_queries(labels, blocks, visit):
    for n, block in enumerate(blocks):
        base = labels.key_base(block)

        def step(p, n=n, base=base):
            begin, end = labels.span(labels.query_shot(p))

            @pl.when(jnp.logical_and(begin < base + BLOCK, end > base))
            def _():
                row = base + lax.broadcasted_iota(jnp.int32, (BLOCK, 1), 0)
                same = jnp.logical_and(row >= begin, row < end)
                visit(n, SIDE + p, jnp.broadcast_to(same, (BLOCK, BLOCK)))

        loop(2, step)


def head_ds(h):
    return pl.ds(pl.multiple_of(h * HDIM, HDIM), HDIM)


def rows_ds(j):
    return pl.ds(pl.multiple_of(j * BLOCK, BLOCK), BLOCK)


def query_cols(j):
    return slice(j * BLOCK, (j + 1) * BLOCK)


def video_stats(acc, q_all, g_all, kv, queries, fresh):
    def head(h):
        c, row = head_ds(h), pl.ds(h, 1)
        keys, values = joined(kv, 0, c), joined(kv, 1, c)
        for j in queries:
            cols = query_cols(j)
            scores = dot_nt(keys, q_all[j, :, c])
            dprob = dot_nt(values, g_all[j, :, c])
            top = jnp.max(scores, axis=0, keepdims=True) * TO_LOG2
            if not fresh:
                before = acc[0, row, cols]
                top = jnp.maximum(before, top)
                shrink = jnp.exp2(before - top)
            weight = jnp.exp2(scores * TO_LOG2 - top)
            total = jnp.sum(weight, axis=0, keepdims=True)
            weighted = jnp.sum(weight * dprob, axis=0, keepdims=True)
            if not fresh:
                total += acc[1, row, cols] * shrink
                weighted += acc[2, row, cols] * shrink
            acc[0, row, cols] = top
            acc[1, row, cols] = total
            acc[2, row, cols] = weighted

    loop(HEADS_LOCAL, head)


def visit_stats(acc, q_all, g_all, kv, part, n, j, mask):
    cols = rows_ds(j)
    results = []
    for h in range(HEADS_LOCAL):
        c = head_cols(h)
        scores = jnp.where(mask, dot_nt(kv[n][0, part, c], q_all[j, :, c]) * TO_LOG2, LOW)
        dprob = dot_nt(kv[n][1, part, c], g_all[j, :, c])
        before = acc[0, h : h + 1, cols]
        top = jnp.maximum(before, jnp.max(scores, axis=0, keepdims=True))
        weight = jnp.where(mask, jnp.exp2(scores - top), 0.0)
        shrink = jnp.exp2(before - top)
        results.append(
            (
                top,
                acc[1, h : h + 1, cols] * shrink + jnp.sum(weight, axis=0, keepdims=True),
                acc[2, h : h + 1, cols] * shrink + jnp.sum(weight * dprob, axis=0, keepdims=True),
            )
        )
    for h in range(HEADS_LOCAL):
        for m in range(3):
            acc[m, h : h + 1, cols] = results[h][m]


NEAR = (0, 1, 3)
FAR = 2


def stats_first_kernel(length_ref, caption_ref, place_ref, *refs):
    kv, qg, text_qg, (acc, q_all, g_all) = refs[:3], refs[3:6], refs[6 : SIDE + 6], refs[SIDE + 6 :]
    labels = Labels(length_ref, caption_ref, place_ref)
    for j, ref in zip(NEAR, qg):
        q_all[j] = ref[0]
        g_all[j] = ref[1]
    stage_text_queries(labels, text_qg, q_all, g_all)
    acc[0] = jnp.full((HEADS_LOCAL, ROWS), LOW, F32)
    acc[1:3] = jnp.zeros((2, HEADS_LOCAL, ROWS), F32)
    video_stats(acc, q_all, g_all, kv, NEAR, True)
    visit = functools.partial(visit_stats, acc, q_all, g_all, kv)
    text_keys(labels, NEAR, NEAR, functools.partial(visit, TEXT_PART))
    own_text(labels, 0, functools.partial(visit, TEXT_PART))
    text_queries(labels, NEAR, functools.partial(visit, VIDEO_PART))


def stats_last_kernel(length_ref, caption_ref, place_ref, *refs):
    kv, far_kv, (acc_in, q_in, g_in, far_qg, out_ref, q_all, g_all, acc) = refs[:3], refs[3:4], refs[4:]
    labels = Labels(length_ref, caption_ref, place_ref)
    for j in range(SIDE + 2):
        q_all[j] = far_qg[0] if j == FAR else q_in[j]
        g_all[j] = far_qg[1] if j == FAR else g_in[j]
    acc[...] = acc_in[...]
    video_stats(acc, q_all, g_all, kv, (FAR,), True)
    video_stats(acc, q_all, g_all, far_kv, range(SIDE), False)
    visit = functools.partial(visit_stats, acc, q_all, g_all)
    text_keys(labels, NEAR, (FAR,), functools.partial(visit, kv, TEXT_PART))
    text_keys(labels, (FAR,), tuple(range(SIDE)), functools.partial(visit, far_kv, TEXT_PART))
    text_queries(labels, (FAR,), functools.partial(visit, far_kv, VIDEO_PART))
    total = acc[1]
    some = total > 0.0
    total = jnp.where(some, total, 1.0)
    out_ref[0] = jnp.where(some, acc[0] + jnp.log2(total), LOW)
    out_ref[1] = acc[2] / total


def normalize(stats, norm):
    for j in range(SIDE + 2):
        parts = []
        for e in range(SIDE):
            if j < SIDE:
                parts.append([stats[e][n, :, query_cols(j ^ e)] for n in range(2)])
            else:
                halves = []
                for u in (2 * (j - SIDE), 2 * (j - SIDE) + 1):
                    at = VIDEO_ROWS + (u ^ e) * HALF
                    halves.append([stats[e][n, :, at : at + HALF] for n in range(2)])
                parts.append([jnp.concatenate([halves[0][n], halves[1][n]], 1) for n in range(2)])
        top = functools.reduce(jnp.maximum, [p[0] for p in parts])
        share = [jnp.exp2(p[0] - top) for p in parts]
        total = sum(share)
        delta = sum(p[1] * s for p, s in zip(parts, share)) / total
        norm[0, :, query_cols(j)] = top + jnp.log2(total)
        norm[1, :, query_cols(j)] = delta


def key_grads(labels, blocks, fresh, q_all, g_all, kv, dkv_out, norm, dq_t, scratch):
    count = len(blocks)
    dk, dv, text_dk, text_dv, p_all, ds_all = scratch
    text_dk[...] = jnp.zeros((count, HEADS_LOCAL, HALF, HDIM), F32)
    text_dv[...] = jnp.zeros((count, HEADS_LOCAL, HALF, HDIM), F32)

    def head(h):
        c, row = head_ds(h), pl.ds(h, 1)
        keys, values = joined(kv, 0, c), joined(kv, 1, c)
        keys_t = jnp.transpose(keys)
        for j in range(SIDE):
            cols = query_cols(j)
            scores = dot_nt(keys, q_all[j, :, c])
            dprob = dot_nt(values, g_all[j, :, c])
            probs = jnp.exp2(scores * TO_LOG2 - norm[0, row, cols])
            dscore = (probs * (dprob - norm[1, row, cols])).astype(BF16)
            p_all[:, cols] = probs.astype(BF16)
            ds_all[:, cols] = dscore
            part = dot_nn(keys_t, dscore)
            if fresh:
                dq_t[h, :, cols] = part
            else:
                dq_t[h, :, cols] += part
        dv[h] = dot_nn(p_all[...], g_all[:SIDE, :, c].reshape(VIDEO_ROWS, HDIM))
        dk[h] = dot_nn(ds_all[...], q_all[:SIDE, :, c].reshape(VIDEO_ROWS, HDIM))

    loop(HEADS_LOCAL, head)

    def visit(part, add, n, j, mask):
        cols = rows_ds(j)
        results = []
        for h in range(HEADS_LOCAL):
            c = head_cols(h)
            keys, queries, grads = kv[n][0, part, c], q_all[j, :, c], g_all[j, :, c]
            scores = dot_nt(keys, queries) * TO_LOG2
            dprob = dot_nt(kv[n][1, part, c], grads)
            probs = jnp.where(mask, jnp.exp2(jnp.where(mask, scores, LOW) - norm[0, h : h + 1, cols]), 0.0)
            low = probs.astype(BF16)
            dscore = (probs * (dprob - norm[1, h : h + 1, cols])).astype(BF16)
            results.append((dot_nn(dscore, queries), dot_nn(low, grads), dot_nn(jnp.transpose(keys), dscore)))
        for h in range(HEADS_LOCAL):
            add(n, h, results[h][0], results[h][1])
            dq_t[h, :, cols] += results[h][2]

    def add_text(n, h, key_part, value_part):
        text_dk[n, h] += key_part
        text_dv[n, h] += value_part

    def add_video(n, h, key_part, value_part):
        dk[h, query_cols(n)] += key_part
        dv[h, query_cols(n)] += value_part

    visit_text = functools.partial(visit, TEXT_PART, add_text)
    text_keys(labels, blocks, tuple(range(SIDE)), visit_text)
    if 0 in blocks:
        own_text(labels, blocks.index(0), visit_text)
    text_queries(labels, blocks, functools.partial(visit, VIDEO_PART, add_video))

    for i in range(count):
        for h in range(HEADS_LOCAL):
            c = head_cols(h)
            dkv_out[i][0, :BLOCK, c] = (dk[h, query_cols(i)] * SCALE).astype(BF16)
            dkv_out[i][1, :BLOCK, c] = dv[h, query_cols(i)].astype(BF16)
            dkv_out[i][0, BLOCK:, c] = (text_dk[i, h] * SCALE).astype(BF16)
            dkv_out[i][1, BLOCK:, c] = text_dv[i, h].astype(BF16)


def grads_first_kernel(blocks, length_ref, caption_ref, place_ref, *refs):
    count = len(blocks)
    q_all, g_all, kv, refs = refs[0], refs[1], refs[2 : 2 + count], refs[2 + count :]
    stats, dkv_out, (dq_t, norm, *scratch) = refs[:SIDE], refs[SIDE : SIDE + count], refs[SIDE + count :]
    labels = Labels(length_ref, caption_ref, place_ref)
    normalize(stats, norm)
    dq_t[:, :, VIDEO_ROWS:] = jnp.zeros((HEADS_LOCAL, HDIM, TEXT_ROWS), F32)
    key_grads(labels, blocks, True, q_all, g_all, kv, dkv_out, norm, dq_t, scratch)


def grads_last_kernel(blocks, length_ref, caption_ref, place_ref, *refs):
    count = len(blocks)
    norm, dq_in, q_all, g_all, kv, refs = *refs[:4], refs[4 : 4 + count], refs[4 + count :]
    dq_out, dkv_out, (dq_t, *scratch) = refs[:SIDE], refs[SIDE : SIDE + count], refs[SIDE + count :]
    labels = Labels(length_ref, caption_ref, place_ref)
    dq_t[...] = dq_in[...]
    key_grads(labels, blocks, False, q_all, g_all, kv, dkv_out, norm, dq_t, scratch)
    for n in range(SIDE):
        dq_out[n][:, :, :BLOCK] = (dq_t[:, :, query_cols(n)] * SCALE).astype(BF16)
        dq_out[n][:, :, BLOCK:] = (dq_t[:, :, VIDEO_ROWS + n * HALF : VIDEO_ROWS + (n + 1) * HALF] * SCALE).astype(BF16)


SMEM_SPEC = pl.BlockSpec(memory_space=pltpu.SMEM)
VMEM_SPEC = pl.BlockSpec(memory_space=pltpu.VMEM)
PARAMS = pltpu.CompilerParams(vmem_limit_bytes=VMEM_LIMIT)
SMALL = pltpu.CompilerParams(vmem_limit_bytes=8 * 1024 * 1024)
DQ_T = (HEADS_LOCAL, HDIM, ROWS)
STATS = (3, HEADS_LOCAL, ROWS)
STAGED_QUERIES = jax.ShapeDtypeStruct((SIDE + 2, BLOCK, WIDTH), BF16)
QUERY_MESSAGE = jax.ShapeDtypeStruct((2, BLOCK, WIDTH), BF16)
KEY_MESSAGE = jax.ShapeDtypeStruct((2, BLOCK + HALF, WIDTH), BF16)


def grads_scratch(count):
    return (
        [pltpu.VMEM((HEADS_LOCAL, count * BLOCK, HDIM), F32)] * 2
        + [pltpu.VMEM((count, HEADS_LOCAL, HALF, HDIM), F32)] * 2
        + [pltpu.VMEM((count * BLOCK, VIDEO_ROWS), BF16)] * 2
    )


def placed(arrays, space=pltpu.VMEM):
    return [pltpu.with_memory_space_constraint(a, space) for a in arrays]


def cost(blocks, matmuls):
    pairs = HEADS_LOCAL * VIDEO_ROWS * BLOCK * blocks
    return pl.CostEstimate(flops=2 * HDIM * matmuls * pairs, bytes_accessed=8 * 1024 * 1024, transcendentals=pairs)


def stats_first_call(scalars, qg, kv, text_qg):
    near_kv, near_qg = [kv[i] for i in NEAR], [qg[j] for j in NEAR]
    return pl.pallas_call(
        stats_first_kernel,
        in_specs=[SMEM_SPEC] * 3 + [VMEM_SPEC] * (SIDE + 6),
        out_specs=[VMEM_SPEC] * 3,
        out_shape=[jax.ShapeDtypeStruct(STATS, F32), STAGED_QUERIES, STAGED_QUERIES],
        compiler_params=PARAMS,
        cost_estimate=cost(3, 2),
        name="stats_first",
    )(*scalars, *placed(near_kv), *placed([*near_qg, *text_qg], pltpu.HBM))


def stats_last_call(scalars, acc, queries, qg, kv):
    return pl.pallas_call(
        stats_last_kernel,
        in_specs=[SMEM_SPEC] * 3 + [VMEM_SPEC] * (SIDE + 4),
        out_specs=[VMEM_SPEC] * 3,
        out_shape=[jax.ShapeDtypeStruct((2, HEADS_LOCAL, ROWS), F32), STAGED_QUERIES, STAGED_QUERIES],
        scratch_shapes=[pltpu.VMEM(STATS, F32)],
        compiler_params=PARAMS,
        cost_estimate=cost(2, 2),
        name="stats_last",
    )(*scalars, *placed([*[kv[i] for i in NEAR], kv[FAR], acc, *queries, qg[FAR]]))


def grads_first_call(blocks, scalars, queries, kv, stats):
    count = len(blocks)
    *dkv, dq_t, norm = pl.pallas_call(
        functools.partial(grads_first_kernel, blocks),
        in_specs=[SMEM_SPEC] * 3 + [VMEM_SPEC] * (2 + SIDE + count),
        out_specs=[VMEM_SPEC] * (count + 2),
        out_shape=[KEY_MESSAGE] * count
        + [jax.ShapeDtypeStruct(DQ_T, F32), jax.ShapeDtypeStruct((2, HEADS_LOCAL, ROWS), F32)],
        scratch_shapes=grads_scratch(count),
        compiler_params=PARAMS,
        cost_estimate=cost(count, 5),
        name="grads_first",
    )(*scalars, *placed([*queries, *[kv[i] for i in blocks], *stats]))
    return dkv, dq_t, norm


def grads_last_call(blocks, scalars, queries, kv, dq_t, norm):
    count = len(blocks)
    out = pl.pallas_call(
        functools.partial(grads_last_kernel, blocks),
        in_specs=[SMEM_SPEC] * 3 + [VMEM_SPEC] * (4 + count),
        out_specs=[VMEM_SPEC] * (SIDE + count),
        out_shape=[jax.ShapeDtypeStruct((HEADS_LOCAL, HDIM, BLOCK + HALF), BF16)] * SIDE + [KEY_MESSAGE] * count,
        scratch_shapes=[pltpu.VMEM(DQ_T, F32)] + grads_scratch(count),
        compiler_params=PARAMS,
        cost_estimate=cost(count, 5),
        name="grads_last",
    )(*scalars, *placed([norm]), dq_t, *placed([*queries, *[kv[i] for i in blocks]]))
    return out[:SIDE], out[SIDE:]


def swap(array, axis, step):
    shift = step if axis == "y" else step * SIDE
    return lax.ppermute(array, "seq", [(i, i ^ shift) for i in range(SIDE * SIDE)])


def gathered(array, axis):
    return [array] + [swap(array, axis, step) for step in range(1, SIDE)]


def on_device(
    video_query,
    video_key,
    video_value,
    video_grad,
    text_query,
    text_key,
    text_value,
    text_grad,
    shot_length,
    caption_length,
):
    place = lax.axis_index("seq").astype(jnp.int32)
    scalars = (shot_length, caption_length, place.reshape(1))
    packed, text_qg = pack(video_query, video_key, video_value, video_grad, text_query, text_grad)
    text_qg = gathered(text_qg, "y")
    arrived = lax.all_to_all(packed, "head", split_axis=0, concat_axis=0)
    arrived, text_qg = lax.optimization_barrier((arrived, text_qg))
    qg, kv = assemble(arrived, text_key, text_value)
    qg1, qg3 = swap(qg, "y", 1), swap(qg, "y", 3)
    kv1, kv3 = swap(kv, "z", 1), swap(kv, "z", 3)
    qg2 = swap(qg, "y", FAR)
    far_kv, qg1, qg3 = lax.optimization_barrier((kv, qg1, qg3))
    qg = [qg, qg1, qg2, qg3]
    kv = [kv, kv1, swap(far_kv, "z", FAR), kv3]

    acc, *queries = stats_first_call(scalars, qg, kv, text_qg)
    stats, *queries = stats_last_call(scalars, acc, queries, qg, kv)
    stats = gathered(stats, "y")
    (dkv1, dkv3), dq_t, norm = grads_first_call((1, 3), scalars, queries, kv, stats)
    dq, (dkv2, dkv0) = grads_last_call((2, 0), scalars, queries, kv, dq_t, norm)

    dkv1, dkv3 = swap(dkv1, "z", 1), swap(dkv3, "z", 3)
    dq, dkv1, dkv2 = lax.optimization_barrier((dq, dkv1, dkv2))
    dq = [dq[0]] + [swap(dq[step], "y", step) for step in range(1, SIDE)]
    dkv = [dkv0, dkv1, swap(dkv2, "z", 2), dkv3]
    video, *text = sum_terms(dq, dkv)
    video_back = unpack(lax.all_to_all(video, "head", split_axis=0, concat_axis=0))
    return (*video_back, *text)


def solution(mesh):
    video = P(("seq", "head"), None)
    text = P("seq", "head")
    return jax.shard_map(
        on_device,
        mesh=mesh,
        in_specs=(video,) * 4 + (text,) * 4 + (P(), P()),
        out_specs=(video,) * 3 + (text,) * 3,
        check_vma=False,
    )
```

```python
import functools

import jax
import jax.numpy as jnp
from jax import lax
from jax.experimental import pallas as pl
from jax.experimental.pallas import tpu as pltpu
from jax.sharding import PartitionSpec as P

HDIM = 128
CAP = 256
NSHOT = 8
HEADS_LOCAL = 3
WIDTH = HEADS_LOCAL * HDIM
GROUP = 8
SIDE = 4
OWN = 32
BLOCK = GROUP * OWN
HALF = 128
VIDEO_ROWS = SIDE * BLOCK
TEXT_ROWS = SIDE * HALF
ROWS = VIDEO_ROWS + TEXT_ROWS
SCALE = HDIM ** (-0.5)
LOG2E = 1.4426950408889634
TO_LOG2 = SCALE * LOG2E
LOW = -1e30
F32 = jnp.float32
BF16 = jnp.bfloat16
VMEM_LIMIT = 16 * 1024 * 1024


def dot_nt(a, b):
    return lax.dot_general(a, b, (((1,), (1,)), ((), ())), preferred_element_type=F32)


def dot_nn(a, b):
    return lax.dot_general(a, b, (((1,), (0,)), ((), ())), preferred_element_type=F32)


def pack_kernel(q_ref, k_ref, v_ref, g_ref, tq_ref, tg_ref, tk_ref, tv_ref, out_ref, text_qg_ref, text_kv_ref):
    for d in range(GROUP):
        cols = slice(d * WIDTH, (d + 1) * WIDTH)
        for n, ref in enumerate((q_ref, g_ref, k_ref, v_ref)):
            out_ref[d, n] = ref[:, cols]
    text_qg_ref[0] = tq_ref[...]
    text_qg_ref[1] = tg_ref[...]
    text_kv_ref[0] = tk_ref[...]
    text_kv_ref[1] = tv_ref[...]


def pack(*arrays):
    video = jax.ShapeDtypeStruct((GROUP, 4, OWN, WIDTH), BF16)
    text = jax.ShapeDtypeStruct((2, HALF, WIDTH), BF16)
    call = pl.pallas_call(pack_kernel, out_shape=(video, text, text), compiler_params=SMALL, name="pack_inputs")
    return call(*placed(arrays, pltpu.HBM))


def assemble_kernel(in_ref, text_ref, qg_ref, kv_ref, far_ref):
    for n in range(2):
        qg_ref[n] = in_ref[:, n].reshape(BLOCK, WIDTH)
        rows = in_ref[:, 2 + n].reshape(BLOCK, WIDTH)
        kv_ref[n] = rows
        far_ref[n, :BLOCK] = rows
        far_ref[n, BLOCK:] = text_ref[n]


def assemble(arrived, text_kv):
    return pl.pallas_call(
        assemble_kernel,
        out_shape=(VIDEO_MESSAGE, VIDEO_MESSAGE, KEY_MESSAGE),
        compiler_params=SMALL,
        name="assemble_blocks",
    )(*placed([arrived]), *placed([text_kv], pltpu.HBM))


def unpack_kernel(in_ref, q_ref, k_ref, v_ref):
    for d in range(GROUP):
        cols = slice(d * WIDTH, (d + 1) * WIDTH)
        q_ref[:, cols] = in_ref[d, 0]
        k_ref[:, cols] = in_ref[d, 1]
        v_ref[:, cols] = in_ref[d, 2]


def unpack(arrived):
    shape = jax.ShapeDtypeStruct((OWN, GROUP * WIDTH), BF16)
    return pl.pallas_call(unpack_kernel, out_shape=(shape, shape, shape), compiler_params=SMALL, name="unpack_video")(*placed([arrived]))


def head_cols(h):
    return slice(h * HDIM, (h + 1) * HDIM)


def sum_kernel(*refs):
    dq, dkv = refs[:SIDE], refs[SIDE : 2 * SIDE]
    out, *text_out = refs[2 * SIDE :]
    for h in range(HEADS_LOCAL):
        total = jnp.transpose(sum(r[h].astype(F32) for r in dq).astype(BF16))
        out[:, 0, :, head_cols(h)] = total[:BLOCK].reshape(GROUP, OWN, HDIM)
        text_out[0][:, head_cols(h)] = total[BLOCK:]
    for n in range(2):
        total = sum(r[n].astype(F32) for r in dkv).astype(BF16)
        out[:, 1 + n] = total[:BLOCK].reshape(GROUP, OWN, WIDTH)
        text_out[1 + n][...] = total[BLOCK:]


def sum_terms(dq, dkv):
    return pl.pallas_call(
        sum_kernel,
        out_shape=[jax.ShapeDtypeStruct((GROUP, 3, OWN, WIDTH), BF16)]
        + [jax.ShapeDtypeStruct((HALF, WIDTH), BF16)] * 3,
        compiler_params=SMALL,
        name="sum_terms",
    )(*placed([*dq, *dkv]))


class Labels:
    def __init__(self, length_ref, caption_ref, place_ref):
        place = place_ref[0]
        self.z = place // SIDE
        self.y = place % SIDE
        self.caption_ref = caption_ref
        starts = [jnp.int32(0)]
        for s in range(NSHOT):
            starts.append(starts[-1] + length_ref[s])
        self.starts = starts

    def span(self, shot):
        begin = jnp.int32(0)
        end = jnp.int32(0)
        for s in range(NSHOT):
            begin = jnp.where(shot == s, self.starts[s], begin)
            end = jnp.where(shot == s, self.starts[s + 1], end)
        return begin, end

    def query_base(self, j):
        return (self.z * SIDE + (self.y ^ j)) * BLOCK

    def key_base(self, i):
        return ((self.z ^ i) * SIDE + self.y) * BLOCK

    def query_shot(self, p):
        return self.z * 2 + (self.y ^ (2 * p)) // 2

    def key_shot(self, t):
        return (self.z ^ t) * 2 + self.y // 2

    def live(self, shot, half):
        row = half * HALF + lax.broadcasted_iota(jnp.int32, (HALF, 1), 0)
        return row < self.caption_ref[shot]


def stage_text_queries(labels, text_qg, q_all, g_all):
    for u in range(SIDE):
        p, rows = u // 2, slice(u % 2 * HALF, (u % 2 + 1) * HALF)
        q_all[SIDE + p, rows] = text_qg[u][0]
        live = labels.live(labels.query_shot(p), (labels.y ^ u) % 2)
        g_all[SIDE + p, rows] = jnp.where(live, text_qg[u][1], jnp.zeros((HALF, WIDTH), BF16))


class Keys:
    def __init__(self, video_ref, text_ref, text_at):
        self.video_ref, self.text_ref, self.text_rows = video_ref, text_ref, slice(text_at, text_at + HALF)

    def rows(self, is_text, which, c):
        return self.text_ref[which, self.text_rows, c] if is_text else self.video_ref[which, :BLOCK, c]


def near_keys(video_refs, text_refs):
    return [Keys(video, text, 0) for video, text in zip(video_refs, text_refs)]


def far_keys(ref):
    return Keys(ref, ref, BLOCK)


def joined(kv, which, c):
    return jnp.concatenate([block.rows(False, which, c) for block in kv], 0)


def loop(count, step):
    lax.fori_loop(0, count, lambda n, c: (step(n), c)[1], 0)


def chosen(blocks, n):
    return sum(jnp.where(n == m, block, 0) for m, block in enumerate(blocks))


def text_keys(labels, blocks, queries, visit):
    for n, block in enumerate(blocks):
        shot = labels.key_shot(block)
        begin, end = labels.span(shot)

        def step(m, n=n, shot=shot, begin=begin, end=end):
            j = queries[0] if len(queries) == 1 else chosen(queries, m)
            base = labels.query_base(j)

            @pl.when(jnp.logical_and(begin < base + BLOCK, end > base))
            def _():
                row = base + lax.broadcasted_iota(jnp.int32, (1, BLOCK), 1)
                same = jnp.logical_and(row >= begin, row < end)
                visit(n, j, jnp.logical_and(labels.live(shot, labels.y % 2), same))

        loop(len(queries), step)


def own_text(labels, n, visit):
    live = labels.live(labels.key_shot(0), labels.y % 2)
    visit(n, SIDE, jnp.broadcast_to(live, (HALF, BLOCK)))


def text_queries(labels, blocks, visit):
    for n, block in enumerate(blocks):
        base = labels.key_base(block)

        def step(p, n=n, base=base):
            begin, end = labels.span(labels.query_shot(p))

            @pl.when(jnp.logical_and(begin < base + BLOCK, end > base))
            def _():
                row = base + lax.broadcasted_iota(jnp.int32, (BLOCK, 1), 0)
                same = jnp.logical_and(row >= begin, row < end)
                visit(n, SIDE + p, jnp.broadcast_to(same, (BLOCK, BLOCK)))

        loop(2, step)


def head_ds(h):
    return pl.ds(pl.multiple_of(h * HDIM, HDIM), HDIM)


def rows_ds(j):
    return pl.ds(pl.multiple_of(j * BLOCK, BLOCK), BLOCK)


def query_cols(j):
    return slice(j * BLOCK, (j + 1) * BLOCK)


def video_stats(acc, q_all, g_all, kv, queries, fresh):
    def head(h):
        c, row = head_ds(h), pl.ds(h, 1)
        keys, values = joined(kv, 0, c), joined(kv, 1, c)
        for j in queries:
            cols = query_cols(j)
            scores = dot_nt(keys, q_all[j, :, c]) * TO_LOG2
            dprob = dot_nt(values, g_all[j, :, c])
            top = jnp.max(scores, axis=0, keepdims=True)
            if not fresh:
                before = acc[0, row, cols]
                top = jnp.maximum(before, top)
                shrink = jnp.exp2(before - top)
            weight = jnp.exp2(scores - top)
            total = jnp.sum(weight, axis=0, keepdims=True)
            weighted = jnp.sum(weight * dprob, axis=0, keepdims=True)
            if not fresh:
                total += acc[1, row, cols] * shrink
                weighted += acc[2, row, cols] * shrink
            acc[0, row, cols] = top
            acc[1, row, cols] = total
            acc[2, row, cols] = weighted

    loop(HEADS_LOCAL, head)


def visit_stats(acc, q_all, g_all, kv, is_text, n, j, mask):
    cols = rows_ds(j)
    results = []
    for h in range(HEADS_LOCAL):
        c = head_cols(h)
        scores = jnp.where(mask, dot_nt(kv[n].rows(is_text, 0, c), q_all[j, :, c]) * TO_LOG2, LOW)
        dprob = dot_nt(kv[n].rows(is_text, 1, c), g_all[j, :, c])
        before = acc[0, h : h + 1, cols]
        top = jnp.maximum(before, jnp.max(scores, axis=0, keepdims=True))
        floor = jnp.maximum(top, 0.5 * LOW)
        weight = jnp.exp2(scores - floor)
        shrink = jnp.exp2(before - floor)
        results.append(
            (
                top,
                acc[1, h : h + 1, cols] * shrink + jnp.sum(weight, axis=0, keepdims=True),
                acc[2, h : h + 1, cols] * shrink + jnp.sum(weight * dprob, axis=0, keepdims=True),
            )
        )
    for h in range(HEADS_LOCAL):
        for m in range(3):
            acc[m, h : h + 1, cols] = results[h][m]


NEAR = (0, 1, 3)
FAR = 2


def stats_first_kernel(length_ref, caption_ref, place_ref, *refs):
    kv, refs = near_keys(refs[:3], refs[3:6]), refs[6:]
    qg, text_qg, (acc, q_all, g_all) = refs[:3], refs[3 : SIDE + 3], refs[SIDE + 3 :]
    labels = Labels(length_ref, caption_ref, place_ref)
    for j, ref in zip(NEAR, qg):
        q_all[j] = ref[0]
        g_all[j] = ref[1]
    stage_text_queries(labels, text_qg, q_all, g_all)
    acc[0] = jnp.full((HEADS_LOCAL, ROWS), LOW, F32)
    acc[1:3] = jnp.zeros((2, HEADS_LOCAL, ROWS), F32)
    video_stats(acc, q_all, g_all, kv, NEAR, True)
    visit = functools.partial(visit_stats, acc, q_all, g_all, kv)
    text_keys(labels, NEAR, NEAR, functools.partial(visit, True))
    own_text(labels, 0, functools.partial(visit, True))
    text_queries(labels, NEAR, functools.partial(visit, False))


def stats_last_kernel(length_ref, caption_ref, place_ref, *refs):
    kv, far_kv = near_keys(refs[:3], refs[3:6]), [far_keys(refs[6])]
    acc_in, q_in, g_in, far_qg, out_ref, q_all, g_all, acc = refs[7:]
    labels = Labels(length_ref, caption_ref, place_ref)
    for j in range(SIDE + 2):
        q_all[j] = far_qg[0] if j == FAR else q_in[j]
        g_all[j] = far_qg[1] if j == FAR else g_in[j]
    acc[...] = acc_in[...]
    video_stats(acc, q_all, g_all, kv, (FAR,), True)
    video_stats(acc, q_all, g_all, far_kv, range(SIDE), False)
    visit = functools.partial(visit_stats, acc, q_all, g_all)
    text_keys(labels, NEAR, (FAR,), functools.partial(visit, kv, True))
    text_keys(labels, (FAR,), tuple(range(SIDE)), functools.partial(visit, far_kv, True))
    text_queries(labels, (FAR,), functools.partial(visit, far_kv, False))
    total = acc[1]
    some = total > 0.0
    total = jnp.where(some, total, 1.0)
    out_ref[0] = jnp.where(some, acc[0] + jnp.log2(total), LOW)
    out_ref[1] = acc[2] / total


def normalize(stats, norm):
    for j in range(SIDE + 2):
        parts = []
        for e in range(SIDE):
            if j < SIDE:
                parts.append([stats[e][n, :, query_cols(j ^ e)] for n in range(2)])
            else:
                halves = []
                for u in (2 * (j - SIDE), 2 * (j - SIDE) + 1):
                    at = VIDEO_ROWS + (u ^ e) * HALF
                    halves.append([stats[e][n, :, at : at + HALF] for n in range(2)])
                parts.append([jnp.concatenate([halves[0][n], halves[1][n]], 1) for n in range(2)])
        top = functools.reduce(jnp.maximum, [p[0] for p in parts])
        share = [jnp.exp2(p[0] - top) for p in parts]
        total = sum(share)
        delta = sum(p[1] * s for p, s in zip(parts, share)) / total
        norm[0, :, query_cols(j)] = top + jnp.log2(total)
        norm[1, :, query_cols(j)] = delta


def key_grads(labels, blocks, dq_in, q_all, g_all, kv, dkv_out, norm, dq_t, scratch):
    count = len(blocks)
    dk, dv, text_dk, text_dv, p_all, ds_all = scratch
    text_dk[...] = jnp.zeros((count, HEADS_LOCAL, HALF, HDIM), F32)
    text_dv[...] = jnp.zeros((count, HEADS_LOCAL, HALF, HDIM), F32)

    def head(h):
        c, row = head_ds(h), pl.ds(h, 1)
        keys, values = joined(kv, 0, c), joined(kv, 1, c)
        keys_t = jnp.transpose(keys)
        for j in range(SIDE):
            cols = query_cols(j)
            scores = dot_nt(keys, q_all[j, :, c])
            dprob = dot_nt(values, g_all[j, :, c])
            probs = jnp.exp2(scores * TO_LOG2 - norm[0, row, cols])
            dscore = (probs * (dprob - norm[1, row, cols])).astype(BF16)
            p_all[:, cols] = probs.astype(BF16)
            ds_all[:, cols] = dscore
        dv[h] = dot_nn(p_all[...], g_all[:SIDE, :, c].reshape(VIDEO_ROWS, HDIM))
        dk[h] = dot_nn(ds_all[...], q_all[:SIDE, :, c].reshape(VIDEO_ROWS, HDIM))
        part = dot_nn(keys_t, ds_all[...])
        dq_t[h, :, :VIDEO_ROWS] = part if dq_in is None else dq_in[h, :, :VIDEO_ROWS] + part

    loop(HEADS_LOCAL, head)

    def visit(is_text, add, n, j, mask):
        cols = rows_ds(j)
        results = []
        for h in range(HEADS_LOCAL):
            c = head_cols(h)
            keys, queries, grads = kv[n].rows(is_text, 0, c), q_all[j, :, c], g_all[j, :, c]
            scores = dot_nt(keys, queries) * TO_LOG2
            dprob = dot_nt(kv[n].rows(is_text, 1, c), grads)
            probs = jnp.exp2(jnp.where(mask, scores, LOW) - norm[0, h : h + 1, cols])
            low = probs.astype(BF16)
            dscore = (probs * (dprob - norm[1, h : h + 1, cols])).astype(BF16)
            results.append((dot_nn(dscore, queries), dot_nn(low, grads), dot_nn(jnp.transpose(keys), dscore)))
        for h in range(HEADS_LOCAL):
            add(n, h, results[h][0], results[h][1])
            dq_t[h, :, cols] += results[h][2]

    def add_text(n, h, key_part, value_part):
        text_dk[n, h] += key_part
        text_dv[n, h] += value_part

    def add_video(n, h, key_part, value_part):
        dk[h, query_cols(n)] += key_part
        dv[h, query_cols(n)] += value_part

    visit_text = functools.partial(visit, True, add_text)
    text_keys(labels, blocks, tuple(range(SIDE)), visit_text)
    if 0 in blocks:
        own_text(labels, blocks.index(0), visit_text)
    text_queries(labels, blocks, functools.partial(visit, False, add_video))

    for i in range(count):
        for h in range(HEADS_LOCAL):
            c = head_cols(h)
            dkv_out[i][0, :BLOCK, c] = (dk[h, query_cols(i)] * SCALE).astype(BF16)
            dkv_out[i][1, :BLOCK, c] = dv[h, query_cols(i)].astype(BF16)
            dkv_out[i][0, BLOCK:, c] = (text_dk[i, h] * SCALE).astype(BF16)
            dkv_out[i][1, BLOCK:, c] = text_dv[i, h].astype(BF16)


def grads_first_kernel(length_ref, caption_ref, place_ref, *refs):
    q_all, g_all, kv, refs = refs[0], refs[1], near_keys(refs[2:4], refs[4:6]), refs[6:]
    stats, dkv_out, (dq_t, norm, *scratch) = refs[:SIDE], refs[SIDE : SIDE + 2], refs[SIDE + 2 :]
    labels = Labels(length_ref, caption_ref, place_ref)
    normalize(stats, norm)
    dq_t[:, :, VIDEO_ROWS:] = jnp.zeros((HEADS_LOCAL, HDIM, TEXT_ROWS), F32)
    key_grads(labels, (1, 3), None, q_all, g_all, kv, dkv_out, norm, dq_t, scratch)


def grads_last_kernel(length_ref, caption_ref, place_ref, *refs):
    norm, dq_in, q_all, g_all = refs[:4]
    kv, refs = [far_keys(refs[4]), Keys(refs[5], refs[6], 0)], refs[7:]
    dq_out, dkv_out, (dq_t, *scratch) = refs[:SIDE], refs[SIDE : SIDE + 2], refs[SIDE + 2 :]
    labels = Labels(length_ref, caption_ref, place_ref)
    dq_t[:, :, VIDEO_ROWS:] = dq_in[:, :, VIDEO_ROWS:]
    key_grads(labels, (FAR, 0), dq_in, q_all, g_all, kv, dkv_out, norm, dq_t, scratch)
    for n in range(SIDE):
        dq_out[n][:, :, :BLOCK] = (dq_t[:, :, query_cols(n)] * SCALE).astype(BF16)
        dq_out[n][:, :, BLOCK:] = (dq_t[:, :, VIDEO_ROWS + n * HALF : VIDEO_ROWS + (n + 1) * HALF] * SCALE).astype(BF16)


SMEM_SPEC = pl.BlockSpec(memory_space=pltpu.SMEM)
VMEM_SPEC = pl.BlockSpec(memory_space=pltpu.VMEM)
PARAMS = pltpu.CompilerParams(vmem_limit_bytes=VMEM_LIMIT)
SMALL = pltpu.CompilerParams(vmem_limit_bytes=8 * 1024 * 1024)
DQ_T = (HEADS_LOCAL, HDIM, ROWS)
STATS = (3, HEADS_LOCAL, ROWS)
STAGED_QUERIES = jax.ShapeDtypeStruct((SIDE + 2, BLOCK, WIDTH), BF16)
VIDEO_MESSAGE = jax.ShapeDtypeStruct((2, BLOCK, WIDTH), BF16)
KEY_MESSAGE = jax.ShapeDtypeStruct((2, BLOCK + HALF, WIDTH), BF16)


def grads_scratch(count):
    return (
        [pltpu.VMEM((HEADS_LOCAL, count * BLOCK, HDIM), F32)] * 2
        + [pltpu.VMEM((count, HEADS_LOCAL, HALF, HDIM), F32)] * 2
        + [pltpu.VMEM((count * BLOCK, VIDEO_ROWS), BF16)] * 2
    )


def placed(arrays, space=pltpu.VMEM):
    return [pltpu.with_memory_space_constraint(a, space) for a in arrays]


def cost(blocks, matmuls):
    pairs = HEADS_LOCAL * VIDEO_ROWS * BLOCK * blocks
    return pl.CostEstimate(flops=2 * HDIM * matmuls * pairs, bytes_accessed=8 * 1024 * 1024, transcendentals=pairs)


def stats_first_call(scalars, qg, kv, text_qg, text_kv):
    return pl.pallas_call(
        stats_first_kernel,
        in_specs=[SMEM_SPEC] * 3 + [VMEM_SPEC] * (SIDE + 9),
        out_specs=[VMEM_SPEC] * 3,
        out_shape=[jax.ShapeDtypeStruct(STATS, F32), STAGED_QUERIES, STAGED_QUERIES],
        compiler_params=PARAMS,
        cost_estimate=cost(3, 2),
        name="stats_first",
    )(
        *scalars,
        *placed([kv[i] for i in NEAR]),
        *placed([*[text_kv[i] for i in NEAR], *[qg[j] for j in NEAR], *text_qg], pltpu.HBM),
    )


def stats_last_call(scalars, acc, queries, qg, kv, text_kv):
    return pl.pallas_call(
        stats_last_kernel,
        in_specs=[SMEM_SPEC] * 3 + [VMEM_SPEC] * 11,
        out_specs=[VMEM_SPEC] * 3,
        out_shape=[jax.ShapeDtypeStruct((2, HEADS_LOCAL, ROWS), F32), STAGED_QUERIES, STAGED_QUERIES],
        scratch_shapes=[pltpu.VMEM(STATS, F32)],
        compiler_params=PARAMS,
        cost_estimate=cost(2, 2),
        name="stats_last",
    )(
        *scalars,
        *placed([kv[i] for i in NEAR]),
        *placed([text_kv[i] for i in NEAR], pltpu.HBM),
        *placed([kv[FAR], acc, *queries, qg[FAR]]),
    )


def grads_first_call(scalars, queries, kv, text_kv, stats):
    *dkv, dq_t, norm = pl.pallas_call(
        grads_first_kernel,
        in_specs=[SMEM_SPEC] * 3 + [VMEM_SPEC] * (6 + SIDE),
        out_specs=[VMEM_SPEC] * 4,
        out_shape=[KEY_MESSAGE] * 2
        + [jax.ShapeDtypeStruct(DQ_T, F32), jax.ShapeDtypeStruct((2, HEADS_LOCAL, ROWS), F32)],
        scratch_shapes=grads_scratch(2),
        compiler_params=PARAMS,
        cost_estimate=cost(2, 5),
        name="grads_first",
    )(*scalars, *placed([*queries, kv[1], kv[3]]), *placed([text_kv[1], text_kv[3]], pltpu.HBM), *placed(stats))
    return dkv, dq_t, norm


def grads_last_call(scalars, queries, kv, text_kv, dq_t, norm):
    out = pl.pallas_call(
        grads_last_kernel,
        in_specs=[SMEM_SPEC] * 3 + [VMEM_SPEC] * 7,
        out_specs=[VMEM_SPEC] * (SIDE + 2),
        out_shape=[jax.ShapeDtypeStruct((HEADS_LOCAL, HDIM, BLOCK + HALF), BF16)] * SIDE + [KEY_MESSAGE] * 2,
        scratch_shapes=[pltpu.VMEM(DQ_T, F32)] + grads_scratch(2),
        compiler_params=PARAMS,
        cost_estimate=cost(2, 5),
        name="grads_last",
    )(*scalars, *placed([norm]), dq_t, *placed([*queries, kv[FAR], kv[0]]), *placed([text_kv[0]], pltpu.HBM))
    return out[:SIDE], out[SIDE:]


def swap(array, axis, step):
    shift = step if axis == "y" else step * SIDE
    return lax.ppermute(array, "seq", [(i, i ^ shift) for i in range(SIDE * SIDE)])


def gathered(array, axis):
    return [array] + [swap(array, axis, step) for step in range(1, SIDE)]


def on_device(
    video_query,
    video_key,
    video_value,
    video_grad,
    text_query,
    text_key,
    text_value,
    text_grad,
    shot_length,
    caption_length,
):
    place = lax.axis_index("seq").astype(jnp.int32)
    scalars = (shot_length, caption_length, place.reshape(1))
    packed, text_qg, text_kv = pack(
        video_query, video_key, video_value, video_grad, text_query, text_grad, text_key, text_value
    )
    text_qg = gathered(text_qg, "y")
    text_kv = {0: text_kv, 1: swap(text_kv, "z", 1), 3: swap(text_kv, "z", 3)}
    arrived = lax.all_to_all(packed, "head", split_axis=0, concat_axis=0)
    arrived, text_qg, text_kv = lax.optimization_barrier((arrived, text_qg, text_kv))
    qg, kv, far_kv = assemble(arrived, text_kv[0])
    qg1, qg3 = swap(qg, "y", 1), swap(qg, "y", 3)
    kv1, kv3 = swap(kv, "z", 1), swap(kv, "z", 3)
    qg2 = swap(qg, "y", FAR)
    far_kv, qg1, qg3, kv1, kv3 = lax.optimization_barrier((far_kv, qg1, qg3, kv1, kv3))
    qg = [qg, qg1, qg2, qg3]
    kv = [kv, kv1, swap(far_kv, "z", FAR), kv3]

    acc, *queries = stats_first_call(scalars, qg, kv, text_qg, text_kv)
    stats, *queries = stats_last_call(scalars, acc, queries, qg, kv, text_kv)
    stats = gathered(stats, "y")
    (dkv1, dkv3), dq_t, norm = grads_first_call(scalars, queries, kv, text_kv, stats)
    dq, (dkv2, dkv0) = grads_last_call(scalars, queries, kv, text_kv, dq_t, norm)

    dkv1, dkv3 = swap(dkv1, "z", 1), swap(dkv3, "z", 3)
    dq, dkv1, dkv2 = lax.optimization_barrier((dq, dkv1, dkv2))
    dq = [dq[0]] + [swap(dq[step], "y", step) for step in range(1, SIDE)]
    dkv = [dkv0, dkv1, swap(dkv2, "z", 2), dkv3]
    video, *text = sum_terms(dq, dkv)
    video_back = unpack(lax.all_to_all(video, "head", split_axis=0, concat_axis=0))
    return (*video_back, *text)


def solution(mesh):
    video = P(("seq", "head"), None)
    text = P("seq", "head")
    return jax.shard_map(
        on_device,
        mesh=mesh,
        in_specs=(video,) * 4 + (text,) * 4 + (P(), P()),
        out_specs=(video,) * 3 + (text,) * 3,
        check_vma=False,
    )
```

```python
import functools

import jax
import jax.numpy as jnp
from jax import lax
from jax.experimental import pallas as pl
from jax.experimental.pallas import tpu as pltpu
from jax.sharding import PartitionSpec as P

HDIM = 128
CAP = 256
NSHOT = 8
HEADS_LOCAL = 3
WIDTH = HEADS_LOCAL * HDIM
GROUP = 8
SIDE = 4
OWN = 32
BLOCK = GROUP * OWN
HALF = 128
VIDEO_ROWS = SIDE * BLOCK
TEXT_ROWS = SIDE * HALF
ROWS = VIDEO_ROWS + TEXT_ROWS
SCALE = HDIM ** (-0.5)
LOG2E = 1.4426950408889634
TO_LOG2 = SCALE * LOG2E
LOW = -1e30
F32 = jnp.float32
BF16 = jnp.bfloat16
VMEM_LIMIT = 16 * 1024 * 1024


def dot_nt(a, b):
    return lax.dot_general(a, b, (((1,), (1,)), ((), ())), preferred_element_type=F32)


def dot_nn(a, b):
    return lax.dot_general(a, b, (((1,), (0,)), ((), ())), preferred_element_type=F32)


def pack_kernel(q_ref, k_ref, v_ref, g_ref, tq_ref, tg_ref, tk_ref, tv_ref, out_ref, text_qg_ref, text_kv_ref):
    for d in range(GROUP):
        cols = slice(d * WIDTH, (d + 1) * WIDTH)
        for n, ref in enumerate((q_ref, g_ref, k_ref, v_ref)):
            out_ref[d, n] = ref[:, cols]
    text_qg_ref[0] = tq_ref[...]
    text_qg_ref[1] = tg_ref[...]
    text_kv_ref[0] = tk_ref[...]
    text_kv_ref[1] = tv_ref[...]


def pack(*arrays):
    video = jax.ShapeDtypeStruct((GROUP, 4, OWN, WIDTH), BF16)
    text = jax.ShapeDtypeStruct((2, HALF, WIDTH), BF16)
    call = pl.pallas_call(pack_kernel, out_shape=(video, text, text), compiler_params=SMALL, name="pack_inputs")
    return call(*placed(arrays, pltpu.HBM))


def assemble_kernel(in_ref, text_qg_ref, text_kv_ref, qg_ref, kv_ref, far_qg_ref, far_kv_ref):
    for n in range(2):
        for at, text, near, far in ((0, text_qg_ref, qg_ref, far_qg_ref), (2, text_kv_ref, kv_ref, far_kv_ref)):
            rows = in_ref[:, at + n].reshape(BLOCK, WIDTH)
            near[n] = rows
            far[n, :BLOCK] = rows
            far[n, BLOCK:] = text[n]


def assemble(arrived, text_qg, text_kv):
    return pl.pallas_call(
        assemble_kernel,
        out_shape=(VIDEO_MESSAGE, VIDEO_MESSAGE, KEY_MESSAGE, KEY_MESSAGE),
        compiler_params=SMALL,
        name="assemble_blocks",
    )(*placed([arrived]), *placed([text_qg, text_kv], pltpu.HBM))


def unpack_kernel(in_ref, q_ref, k_ref, v_ref):
    for d in range(GROUP):
        cols = slice(d * WIDTH, (d + 1) * WIDTH)
        q_ref[:, cols] = in_ref[d, 0]
        k_ref[:, cols] = in_ref[d, 1]
        v_ref[:, cols] = in_ref[d, 2]


def unpack(arrived):
    shape = jax.ShapeDtypeStruct((OWN, GROUP * WIDTH), BF16)
    return pl.pallas_call(unpack_kernel, out_shape=(shape, shape, shape), compiler_params=SMALL, name="unpack_video")(*placed([arrived]))


def head_cols(h):
    return slice(h * HDIM, (h + 1) * HDIM)


def sum_kernel(*refs):
    dq, dkv = refs[:SIDE], refs[SIDE : 2 * SIDE]
    out, *text_out = refs[2 * SIDE :]
    for h in range(HEADS_LOCAL):
        total = jnp.transpose(sum(r[h].astype(F32) for r in dq).astype(BF16))
        out[:, 0, :, head_cols(h)] = total[:BLOCK].reshape(GROUP, OWN, HDIM)
        text_out[0][:, head_cols(h)] = total[BLOCK:]
    for n in range(2):
        total = sum(r[n].astype(F32) for r in dkv).astype(BF16)
        out[:, 1 + n] = total[:BLOCK].reshape(GROUP, OWN, WIDTH)
        text_out[1 + n][...] = total[BLOCK:]


def sum_terms(dq, dkv):
    return pl.pallas_call(
        sum_kernel,
        out_shape=[jax.ShapeDtypeStruct((GROUP, 3, OWN, WIDTH), BF16)]
        + [jax.ShapeDtypeStruct((HALF, WIDTH), BF16)] * 3,
        compiler_params=SMALL,
        name="sum_terms",
    )(*placed([*dq, *dkv]))


class Labels:
    def __init__(self, length_ref, caption_ref, place_ref):
        place = place_ref[0]
        self.z = place // SIDE
        self.y = place % SIDE
        self.caption_ref = caption_ref
        starts = [jnp.int32(0)]
        for s in range(NSHOT):
            starts.append(starts[-1] + length_ref[s])
        self.starts = starts

    def span(self, shot):
        begin = jnp.int32(0)
        end = jnp.int32(0)
        for s in range(NSHOT):
            begin = jnp.where(shot == s, self.starts[s], begin)
            end = jnp.where(shot == s, self.starts[s + 1], end)
        return begin, end

    def query_base(self, j):
        return (self.z * SIDE + (self.y ^ j)) * BLOCK

    def key_base(self, i):
        return ((self.z ^ i) * SIDE + self.y) * BLOCK

    def query_shot(self, p):
        return self.z * 2 + (self.y ^ (2 * p)) // 2

    def key_shot(self, t):
        return (self.z ^ t) * 2 + self.y // 2

    def live(self, shot, half):
        row = half * HALF + lax.broadcasted_iota(jnp.int32, (HALF, 1), 0)
        return row < self.caption_ref[shot]


def stage_text_queries(labels, p, parts, q_all, g_all):
    shot = labels.query_shot(p)
    for e, (ref, at) in enumerate(parts):
        rows, source = slice(e * HALF, (e + 1) * HALF), slice(at, at + HALF)
        q_all[SIDE + p, rows] = ref[0, source]
        live = labels.live(shot, (labels.y ^ e) % 2)
        g_all[SIDE + p, rows] = jnp.where(live, ref[1, source], jnp.zeros((HALF, WIDTH), BF16))


class Keys:
    def __init__(self, video_ref, text_ref, text_at):
        self.video_ref, self.text_ref, self.text_rows = video_ref, text_ref, slice(text_at, text_at + HALF)

    def rows(self, is_text, which, c):
        return self.text_ref[which, self.text_rows, c] if is_text else self.video_ref[which, :BLOCK, c]


def near_keys(video_refs, text_refs):
    return [Keys(video, text, 0) for video, text in zip(video_refs, text_refs)]


def far_keys(ref):
    return Keys(ref, ref, BLOCK)


def joined(kv, which, c):
    return jnp.concatenate([block.rows(False, which, c) for block in kv], 0)


def loop(count, step):
    lax.fori_loop(0, count, lambda n, c: (step(n), c)[1], 0)


def chosen(blocks, n):
    return sum(jnp.where(n == m, block, 0) for m, block in enumerate(blocks))


def text_keys(labels, blocks, queries, visit):
    for n, block in enumerate(blocks):
        shot = labels.key_shot(block)
        begin, end = labels.span(shot)

        def step(m, n=n, shot=shot, begin=begin, end=end):
            j = queries[0] if len(queries) == 1 else chosen(queries, m)
            base = labels.query_base(j)

            @pl.when(jnp.logical_and(begin < base + BLOCK, end > base))
            def _():
                row = base + lax.broadcasted_iota(jnp.int32, (1, BLOCK), 1)
                same = jnp.logical_and(row >= begin, row < end)
                visit(n, j, jnp.logical_and(labels.live(shot, labels.y % 2), same))

        loop(len(queries), step)


def own_text(labels, n, visit):
    live = labels.live(labels.key_shot(0), labels.y % 2)
    visit(n, SIDE, jnp.broadcast_to(live, (HALF, BLOCK)))


def text_queries(labels, blocks, pairs, visit):
    for n, block in enumerate(blocks):
        base = labels.key_base(block)

        def step(p, n=n, base=base):
            begin, end = labels.span(labels.query_shot(p))

            @pl.when(jnp.logical_and(begin < base + BLOCK, end > base))
            def _():
                row = base + lax.broadcasted_iota(jnp.int32, (BLOCK, 1), 0)
                same = jnp.logical_and(row >= begin, row < end)
                visit(n, SIDE + p, jnp.broadcast_to(same, (BLOCK, BLOCK)))

        for p in pairs:
            step(p)


def head_ds(h):
    return pl.ds(pl.multiple_of(h * HDIM, HDIM), HDIM)


def rows_ds(j):
    return pl.ds(pl.multiple_of(j * BLOCK, BLOCK), BLOCK)


def query_cols(j):
    return slice(j * BLOCK, (j + 1) * BLOCK)


def video_stats(acc, q_all, g_all, kv, queries, fresh):
    def head(h):
        c, row = head_ds(h), pl.ds(h, 1)
        keys, values = joined(kv, 0, c), joined(kv, 1, c)
        for j in queries:
            cols = query_cols(j)
            scores = dot_nt(keys, q_all[j, :, c]) * TO_LOG2
            dprob = dot_nt(values, g_all[j, :, c])
            top = jnp.max(scores, axis=0, keepdims=True)
            if not fresh:
                before = acc[0, row, cols]
                top = jnp.maximum(before, top)
                shrink = jnp.exp2(before - top)
            weight = jnp.exp2(scores - top)
            total = jnp.sum(weight, axis=0, keepdims=True)
            weighted = jnp.sum(weight * dprob, axis=0, keepdims=True)
            if not fresh:
                total += acc[1, row, cols] * shrink
                weighted += acc[2, row, cols] * shrink
            acc[0, row, cols] = top
            acc[1, row, cols] = total
            acc[2, row, cols] = weighted

    loop(HEADS_LOCAL, head)


def visit_stats(acc, q_all, g_all, kv, is_text, n, j, mask):
    cols = rows_ds(j)
    results = []
    for h in range(HEADS_LOCAL):
        c = head_cols(h)
        scores = jnp.where(mask, dot_nt(kv[n].rows(is_text, 0, c), q_all[j, :, c]) * TO_LOG2, LOW)
        dprob = dot_nt(kv[n].rows(is_text, 1, c), g_all[j, :, c])
        before = acc[0, h : h + 1, cols]
        top = jnp.maximum(before, jnp.max(scores, axis=0, keepdims=True))
        floor = jnp.maximum(top, 0.5 * LOW)
        weight = jnp.exp2(scores - floor)
        shrink = jnp.exp2(before - floor)
        results.append(
            (
                top,
                acc[1, h : h + 1, cols] * shrink + jnp.sum(weight, axis=0, keepdims=True),
                acc[2, h : h + 1, cols] * shrink + jnp.sum(weight * dprob, axis=0, keepdims=True),
            )
        )
    for h in range(HEADS_LOCAL):
        for m in range(3):
            acc[m, h : h + 1, cols] = results[h][m]


NEAR = (0, 1, 3)
FAR = 2


def stats_first_kernel(length_ref, caption_ref, place_ref, *refs):
    kv, refs = near_keys(refs[:3], refs[3:6]), refs[6:]
    qg, text_qg, (acc, q_all, g_all) = refs[:3], refs[3:5], refs[5:]
    labels = Labels(length_ref, caption_ref, place_ref)
    for j, ref in zip(NEAR, qg):
        q_all[j] = ref[0]
        g_all[j] = ref[1]
    stage_text_queries(labels, 0, [(ref, 0) for ref in text_qg], q_all, g_all)
    acc[0] = jnp.full((HEADS_LOCAL, ROWS), LOW, F32)
    acc[1:3] = jnp.zeros((2, HEADS_LOCAL, ROWS), F32)
    video_stats(acc, q_all, g_all, kv, NEAR, True)
    visit = functools.partial(visit_stats, acc, q_all, g_all, kv)
    text_keys(labels, NEAR, NEAR, functools.partial(visit, True))
    own_text(labels, 0, functools.partial(visit, True))
    text_queries(labels, NEAR, (0,), functools.partial(visit, False))


def stats_last_kernel(length_ref, caption_ref, place_ref, *refs):
    kv, far_kv = near_keys(refs[:3], refs[3:6]), [far_keys(refs[6])]
    acc_in, q_in, g_in, far_qg, text_qg, out_ref, q_all, g_all, acc = refs[7:]
    labels = Labels(length_ref, caption_ref, place_ref)
    for j in range(SIDE + 1):
        q_all[j] = far_qg[0, :BLOCK] if j == FAR else q_in[j]
        g_all[j] = far_qg[1, :BLOCK] if j == FAR else g_in[j]
    stage_text_queries(labels, 1, [(far_qg, BLOCK), (text_qg, 0)], q_all, g_all)
    acc[...] = acc_in[...]
    video_stats(acc, q_all, g_all, kv, (FAR,), True)
    video_stats(acc, q_all, g_all, far_kv, range(SIDE), False)
    visit = functools.partial(visit_stats, acc, q_all, g_all)
    text_keys(labels, NEAR, (FAR,), functools.partial(visit, kv, True))
    text_keys(labels, (FAR,), tuple(range(SIDE)), functools.partial(visit, far_kv, True))
    text_queries(labels, NEAR, (1,), functools.partial(visit, kv, False))
    text_queries(labels, (FAR,), (0, 1), functools.partial(visit, far_kv, False))
    total = acc[1]
    some = total > 0.0
    total = jnp.where(some, total, 1.0)
    out_ref[0] = jnp.where(some, acc[0] + jnp.log2(total), LOW)
    out_ref[1] = acc[2] / total


def normalize(stats, norm):
    for j in range(SIDE + 2):
        parts = []
        for e in range(SIDE):
            if j < SIDE:
                parts.append([stats[e][n, :, query_cols(j ^ e)] for n in range(2)])
            else:
                halves = []
                for u in (2 * (j - SIDE), 2 * (j - SIDE) + 1):
                    at = VIDEO_ROWS + (u ^ e) * HALF
                    halves.append([stats[e][n, :, at : at + HALF] for n in range(2)])
                parts.append([jnp.concatenate([halves[0][n], halves[1][n]], 1) for n in range(2)])
        top = functools.reduce(jnp.maximum, [p[0] for p in parts])
        share = [jnp.exp2(p[0] - top) for p in parts]
        total = sum(share)
        delta = sum(p[1] * s for p, s in zip(parts, share)) / total
        norm[0, :, query_cols(j)] = top + jnp.log2(total)
        norm[1, :, query_cols(j)] = delta


def key_grads(labels, blocks, dq_in, q_all, g_all, kv, dkv_out, norm, dq_t, scratch):
    count = len(blocks)
    dk, dv, text_dk, text_dv, p_all, ds_all = scratch
    text_dk[...] = jnp.zeros((count, HEADS_LOCAL, HALF, HDIM), F32)
    text_dv[...] = jnp.zeros((count, HEADS_LOCAL, HALF, HDIM), F32)

    def head(h):
        c, row = head_ds(h), pl.ds(h, 1)
        keys, values = joined(kv, 0, c), joined(kv, 1, c)
        keys_t = jnp.transpose(keys)
        for j in range(SIDE):
            cols = query_cols(j)
            scores = dot_nt(keys, q_all[j, :, c])
            dprob = dot_nt(values, g_all[j, :, c])
            probs = jnp.exp2(scores * TO_LOG2 - norm[0, row, cols])
            dscore = (probs * (dprob - norm[1, row, cols])).astype(BF16)
            p_all[:, cols] = probs.astype(BF16)
            ds_all[:, cols] = dscore
        dv[h] = dot_nn(p_all[...], g_all[:SIDE, :, c].reshape(VIDEO_ROWS, HDIM))
        dk[h] = dot_nn(ds_all[...], q_all[:SIDE, :, c].reshape(VIDEO_ROWS, HDIM))
        part = dot_nn(keys_t, ds_all[...])
        dq_t[h, :, :VIDEO_ROWS] = part if dq_in is None else dq_in[h, :, :VIDEO_ROWS] + part

    loop(HEADS_LOCAL, head)

    def visit(is_text, add, n, j, mask):
        cols = rows_ds(j)
        results = []
        for h in range(HEADS_LOCAL):
            c = head_cols(h)
            keys, queries, grads = kv[n].rows(is_text, 0, c), q_all[j, :, c], g_all[j, :, c]
            scores = dot_nt(keys, queries) * TO_LOG2
            dprob = dot_nt(kv[n].rows(is_text, 1, c), grads)
            probs = jnp.exp2(jnp.where(mask, scores, LOW) - norm[0, h : h + 1, cols])
            low = probs.astype(BF16)
            dscore = (probs * (dprob - norm[1, h : h + 1, cols])).astype(BF16)
            results.append((dot_nn(dscore, queries), dot_nn(low, grads), dot_nn(jnp.transpose(keys), dscore)))
        for h in range(HEADS_LOCAL):
            add(n, h, results[h][0], results[h][1])
            dq_t[h, :, cols] += results[h][2]

    def add_text(n, h, key_part, value_part):
        text_dk[n, h] += key_part
        text_dv[n, h] += value_part

    def add_video(n, h, key_part, value_part):
        dk[h, query_cols(n)] += key_part
        dv[h, query_cols(n)] += value_part

    visit_text = functools.partial(visit, True, add_text)
    text_keys(labels, blocks, tuple(range(SIDE)), visit_text)
    if 0 in blocks:
        own_text(labels, blocks.index(0), visit_text)
    text_queries(labels, blocks, (0, 1), functools.partial(visit, False, add_video))

    for i in range(count):
        for h in range(HEADS_LOCAL):
            c = head_cols(h)
            dkv_out[i][0, :BLOCK, c] = (dk[h, query_cols(i)] * SCALE).astype(BF16)
            dkv_out[i][1, :BLOCK, c] = dv[h, query_cols(i)].astype(BF16)
            dkv_out[i][0, BLOCK:, c] = (text_dk[i, h] * SCALE).astype(BF16)
            dkv_out[i][1, BLOCK:, c] = text_dv[i, h].astype(BF16)


def grads_first_kernel(length_ref, caption_ref, place_ref, *refs):
    q_all, g_all, kv, refs = refs[0], refs[1], near_keys(refs[2:4], refs[4:6]), refs[6:]
    stats, dkv_out, (dq_t, norm, *scratch) = refs[:SIDE], refs[SIDE : SIDE + 2], refs[SIDE + 2 :]
    labels = Labels(length_ref, caption_ref, place_ref)
    normalize(stats, norm)
    dq_t[:, :, VIDEO_ROWS:] = jnp.zeros((HEADS_LOCAL, HDIM, TEXT_ROWS), F32)
    key_grads(labels, (1, 3), None, q_all, g_all, kv, dkv_out, norm, dq_t, scratch)


def grads_last_kernel(length_ref, caption_ref, place_ref, *refs):
    norm, dq_in, q_all, g_all = refs[:4]
    kv, refs = [far_keys(refs[4]), Keys(refs[5], refs[6], 0)], refs[7:]
    dq_out, dkv_out, (dq_t, *scratch) = refs[:SIDE], refs[SIDE : SIDE + 2], refs[SIDE + 2 :]
    labels = Labels(length_ref, caption_ref, place_ref)
    dq_t[:, :, VIDEO_ROWS:] = dq_in[:, :, VIDEO_ROWS:]
    key_grads(labels, (FAR, 0), dq_in, q_all, g_all, kv, dkv_out, norm, dq_t, scratch)
    for n in range(SIDE):
        dq_out[n][:, :, :BLOCK] = (dq_t[:, :, query_cols(n)] * SCALE).astype(BF16)
        dq_out[n][:, :, BLOCK:] = (dq_t[:, :, VIDEO_ROWS + n * HALF : VIDEO_ROWS + (n + 1) * HALF] * SCALE).astype(BF16)


SMEM_SPEC = pl.BlockSpec(memory_space=pltpu.SMEM)
VMEM_SPEC = pl.BlockSpec(memory_space=pltpu.VMEM)
PARAMS = pltpu.CompilerParams(vmem_limit_bytes=VMEM_LIMIT)
SMALL = pltpu.CompilerParams(vmem_limit_bytes=8 * 1024 * 1024)
DQ_T = (HEADS_LOCAL, HDIM, ROWS)
STATS = (3, HEADS_LOCAL, ROWS)
STAGED_QUERIES = jax.ShapeDtypeStruct((SIDE + 2, BLOCK, WIDTH), BF16)
VIDEO_MESSAGE = jax.ShapeDtypeStruct((2, BLOCK, WIDTH), BF16)
KEY_MESSAGE = jax.ShapeDtypeStruct((2, BLOCK + HALF, WIDTH), BF16)


def grads_scratch(count):
    return (
        [pltpu.VMEM((HEADS_LOCAL, count * BLOCK, HDIM), F32)] * 2
        + [pltpu.VMEM((count, HEADS_LOCAL, HALF, HDIM), F32)] * 2
        + [pltpu.VMEM((count * BLOCK, VIDEO_ROWS), BF16)] * 2
    )


def placed(arrays, space=pltpu.VMEM):
    return [pltpu.with_memory_space_constraint(a, space) for a in arrays]


def cost(blocks, matmuls):
    pairs = HEADS_LOCAL * VIDEO_ROWS * BLOCK * blocks
    return pl.CostEstimate(flops=2 * HDIM * matmuls * pairs, bytes_accessed=8 * 1024 * 1024, transcendentals=pairs)


def stats_first_call(scalars, qg, kv, text_qg, text_kv):
    return pl.pallas_call(
        stats_first_kernel,
        in_specs=[SMEM_SPEC] * 3 + [VMEM_SPEC] * 11,
        out_specs=[VMEM_SPEC] * 3,
        out_shape=[jax.ShapeDtypeStruct(STATS, F32), STAGED_QUERIES, STAGED_QUERIES],
        compiler_params=PARAMS,
        cost_estimate=cost(3, 2),
        name="stats_first",
    )(
        *scalars,
        *placed([kv[i] for i in NEAR]),
        *placed([*[text_kv[i] for i in NEAR], *[qg[j] for j in NEAR], text_qg[0], text_qg[1]], pltpu.HBM),
    )


def stats_last_call(scalars, acc, queries, qg, kv, text_qg, text_kv):
    return pl.pallas_call(
        stats_last_kernel,
        in_specs=[SMEM_SPEC] * 3 + [VMEM_SPEC] * 12,
        out_specs=[VMEM_SPEC] * 3,
        out_shape=[jax.ShapeDtypeStruct((2, HEADS_LOCAL, ROWS), F32), STAGED_QUERIES, STAGED_QUERIES],
        scratch_shapes=[pltpu.VMEM(STATS, F32)],
        compiler_params=PARAMS,
        cost_estimate=cost(2, 2),
        name="stats_last",
    )(
        *scalars,
        *placed([kv[i] for i in NEAR]),
        *placed([text_kv[i] for i in NEAR], pltpu.HBM),
        *placed([kv[FAR], acc, *queries, qg[FAR]]),
        *placed([text_qg[3]], pltpu.HBM),
    )


def grads_first_call(scalars, queries, kv, text_kv, stats):
    *dkv, dq_t, norm = pl.pallas_call(
        grads_first_kernel,
        in_specs=[SMEM_SPEC] * 3 + [VMEM_SPEC] * (6 + SIDE),
        out_specs=[VMEM_SPEC] * 4,
        out_shape=[KEY_MESSAGE] * 2
        + [jax.ShapeDtypeStruct(DQ_T, F32), jax.ShapeDtypeStruct((2, HEADS_LOCAL, ROWS), F32)],
        scratch_shapes=grads_scratch(2),
        compiler_params=PARAMS,
        cost_estimate=cost(2, 5),
        name="grads_first",
    )(*scalars, *placed([*queries, kv[1], kv[3]]), *placed([text_kv[1], text_kv[3]], pltpu.HBM), *placed(stats))
    return dkv, dq_t, norm


def grads_last_call(scalars, queries, kv, text_kv, dq_t, norm):
    out = pl.pallas_call(
        grads_last_kernel,
        in_specs=[SMEM_SPEC] * 3 + [VMEM_SPEC] * 7,
        out_specs=[VMEM_SPEC] * (SIDE + 2),
        out_shape=[jax.ShapeDtypeStruct((HEADS_LOCAL, HDIM, BLOCK + HALF), BF16)] * SIDE + [KEY_MESSAGE] * 2,
        scratch_shapes=[pltpu.VMEM(DQ_T, F32)] + grads_scratch(2),
        compiler_params=PARAMS,
        cost_estimate=cost(2, 5),
        name="grads_last",
    )(*scalars, *placed([norm]), dq_t, *placed([*queries, kv[FAR], kv[0]]), *placed([text_kv[0]], pltpu.HBM))
    return out[:SIDE], out[SIDE:]


def swap(array, axis, step):
    shift = step if axis == "y" else step * SIDE
    return lax.ppermute(array, "seq", [(i, i ^ shift) for i in range(SIDE * SIDE)])


def gathered(array, axis):
    return [array] + [swap(array, axis, step) for step in range(1, SIDE)]


def on_device(
    video_query,
    video_key,
    video_value,
    video_grad,
    text_query,
    text_key,
    text_value,
    text_grad,
    shot_length,
    caption_length,
):
    place = lax.axis_index("seq").astype(jnp.int32)
    scalars = (shot_length, caption_length, place.reshape(1))
    packed, text_qg, text_kv = pack(
        video_query, video_key, video_value, video_grad, text_query, text_grad, text_key, text_value
    )
    text_qg = {0: text_qg, 1: swap(text_qg, "y", 1), 3: swap(text_qg, "y", 3)}
    text_kv = {0: text_kv, 1: swap(text_kv, "z", 1), 3: swap(text_kv, "z", 3)}
    arrived = lax.all_to_all(packed, "head", split_axis=0, concat_axis=0)
    arrived, text_qg, text_kv = lax.optimization_barrier((arrived, text_qg, text_kv))
    qg, kv, far_qg, far_kv = assemble(arrived, text_qg[0], text_kv[0])
    qg1, qg3 = swap(qg, "y", 1), swap(qg, "y", 3)
    kv1, kv3 = swap(kv, "z", 1), swap(kv, "z", 3)
    far_qg, far_kv, qg1, qg3, kv1, kv3 = lax.optimization_barrier((far_qg, far_kv, qg1, qg3, kv1, kv3))
    qg = [qg, qg1, swap(far_qg, "y", FAR), qg3]
    kv = [kv, kv1, swap(far_kv, "z", FAR), kv3]

    acc, *queries = stats_first_call(scalars, qg, kv, text_qg, text_kv)
    stats, *queries = stats_last_call(scalars, acc, queries, qg, kv, text_qg, text_kv)
    stats = gathered(stats, "y")
    (dkv1, dkv3), dq_t, norm = grads_first_call(scalars, queries, kv, text_kv, stats)
    dq, (dkv2, dkv0) = grads_last_call(scalars, queries, kv, text_kv, dq_t, norm)

    dkv1, dkv3 = swap(dkv1, "z", 1), swap(dkv3, "z", 3)
    dq, dkv1, dkv2 = lax.optimization_barrier((dq, dkv1, dkv2))
    dq = [dq[0]] + [swap(dq[step], "y", step) for step in range(1, SIDE)]
    dkv = [dkv0, dkv1, swap(dkv2, "z", 2), dkv3]
    video, *text = sum_terms(dq, dkv)
    video_back = unpack(lax.all_to_all(video, "head", split_axis=0, concat_axis=0))
    return (*video_back, *text)


def solution(mesh):
    video = P(("seq", "head"), None)
    text = P("seq", "head")
    return jax.shard_map(
        on_device,
        mesh=mesh,
        in_specs=(video,) * 4 + (text,) * 4 + (P(), P()),
        out_specs=(video,) * 3 + (text,) * 3,
        check_vma=False,
    )
```

```python
import functools

import jax
import jax.numpy as jnp
from jax import lax
from jax.experimental import pallas as pl
from jax.experimental.pallas import tpu as pltpu
from jax.sharding import PartitionSpec as P

HDIM = 128
CAP = 256
NSHOT = 8
HEADS_LOCAL = 3
WIDTH = HEADS_LOCAL * HDIM
GROUP = 8
SIDE = 4
OWN = 32
BLOCK = GROUP * OWN
HALF = 128
VIDEO_ROWS = SIDE * BLOCK
TEXT_ROWS = SIDE * HALF
ROWS = VIDEO_ROWS + TEXT_ROWS
SCALE = HDIM ** (-0.5)
LOG2E = 1.4426950408889634
TO_LOG2 = SCALE * LOG2E
LOW = -1e30
F32 = jnp.float32
BF16 = jnp.bfloat16
VMEM_LIMIT = 16 * 1024 * 1024


def dot_nt(a, b):
    return lax.dot_general(a, b, (((1,), (1,)), ((), ())), preferred_element_type=F32)


def dot_nn(a, b):
    return lax.dot_general(a, b, (((1,), (0,)), ((), ())), preferred_element_type=F32)


def pack_kernel(q_ref, k_ref, v_ref, g_ref, tq_ref, tg_ref, tk_ref, tv_ref, out_ref, text_qg_ref, text_kv_ref):
    for d in range(GROUP):
        cols = slice(d * WIDTH, (d + 1) * WIDTH)
        for n, ref in enumerate((q_ref, g_ref, k_ref, v_ref)):
            out_ref[d, n] = ref[:, cols]
    text_qg_ref[0] = tq_ref[...]
    text_qg_ref[1] = tg_ref[...]
    text_kv_ref[0] = tk_ref[...]
    text_kv_ref[1] = tv_ref[...]


def pack(*arrays):
    video = jax.ShapeDtypeStruct((GROUP, 4, OWN, WIDTH), BF16)
    text = jax.ShapeDtypeStruct((2, HALF, WIDTH), BF16)
    call = pl.pallas_call(pack_kernel, out_shape=(video, text, text), compiler_params=SMALL, name="pack_inputs")
    return call(*placed(arrays, pltpu.HBM))


def assemble_kernel(in_ref, qg_ref, kv_ref):
    for n in range(2):
        qg_ref[n] = in_ref[:, n].reshape(BLOCK, WIDTH)
        kv_ref[n] = in_ref[:, 2 + n].reshape(BLOCK, WIDTH)


def assemble(arrived):
    return pl.pallas_call(
        assemble_kernel,
        out_shape=(VIDEO_MESSAGE, VIDEO_MESSAGE),
        compiler_params=SMALL,
        name="assemble_blocks",
    )(*placed([arrived]))


def hand_on_kernel(*refs):
    video, text, outs = refs[:4], refs[4:8], refs[8:]
    for n in range(4):
        outs[n][:BLOCK] = video[n][n % 2]
        outs[n][BLOCK:] = text[n][n % 2]


def hand_on(video, text):
    return pl.pallas_call(
        hand_on_kernel,
        out_shape=[HALF_MESSAGE] * 4,
        compiler_params=SMALL,
        name="hand_on",
    )(*placed(video), *placed(text, pltpu.HBM))


def unpack_kernel(in_ref, q_ref, k_ref, v_ref):
    for d in range(GROUP):
        cols = slice(d * WIDTH, (d + 1) * WIDTH)
        q_ref[:, cols] = in_ref[d, 0]
        k_ref[:, cols] = in_ref[d, 1]
        v_ref[:, cols] = in_ref[d, 2]


def unpack(arrived):
    shape = jax.ShapeDtypeStruct((OWN, GROUP * WIDTH), BF16)
    return pl.pallas_call(unpack_kernel, out_shape=(shape, shape, shape), compiler_params=SMALL, name="unpack_video")(*placed([arrived]))


def head_cols(h):
    return slice(h * HDIM, (h + 1) * HDIM)


def sum_kernel(*refs):
    dq, dkv = refs[:SIDE], refs[SIDE : 2 * SIDE]
    out, *text_out = refs[2 * SIDE :]
    for h in range(HEADS_LOCAL):
        total = jnp.transpose(sum(r[h].astype(F32) for r in dq).astype(BF16))
        out[:, 0, :, head_cols(h)] = total[:BLOCK].reshape(GROUP, OWN, HDIM)
        text_out[0][:, head_cols(h)] = total[BLOCK:]
    for n in range(2):
        total = sum(r[n].astype(F32) for r in dkv).astype(BF16)
        out[:, 1 + n] = total[:BLOCK].reshape(GROUP, OWN, WIDTH)
        text_out[1 + n][...] = total[BLOCK:]


def sum_terms(dq, dkv):
    return pl.pallas_call(
        sum_kernel,
        out_shape=[jax.ShapeDtypeStruct((GROUP, 3, OWN, WIDTH), BF16)]
        + [jax.ShapeDtypeStruct((HALF, WIDTH), BF16)] * 3,
        compiler_params=SMALL,
        name="sum_terms",
    )(*placed([*dq, *dkv]))


class Labels:
    def __init__(self, length_ref, caption_ref, place_ref):
        place = place_ref[0]
        self.z = place // SIDE
        self.y = place % SIDE
        self.caption_ref = caption_ref
        starts = [jnp.int32(0)]
        for s in range(NSHOT):
            starts.append(starts[-1] + length_ref[s])
        self.starts = starts

    def span(self, shot):
        begin = jnp.int32(0)
        end = jnp.int32(0)
        for s in range(NSHOT):
            begin = jnp.where(shot == s, self.starts[s], begin)
            end = jnp.where(shot == s, self.starts[s + 1], end)
        return begin, end

    def query_base(self, j):
        return (self.z * SIDE + (self.y ^ j)) * BLOCK

    def key_base(self, i):
        return ((self.z ^ i) * SIDE + self.y) * BLOCK

    def query_shot(self, p):
        return self.z * 2 + (self.y ^ (2 * p)) // 2

    def key_shot(self, t):
        return (self.z ^ t) * 2 + self.y // 2

    def live(self, shot, half):
        row = half * HALF + lax.broadcasted_iota(jnp.int32, (HALF, 1), 0)
        return row < self.caption_ref[shot]


def stage_text_queries(labels, p, parts, q_all, g_all):
    shot = labels.query_shot(p)
    for e, (queries, grads) in enumerate(parts):
        rows = slice(e * HALF, (e + 1) * HALF)
        q_all[SIDE + p, rows] = queries
        live = labels.live(shot, (labels.y ^ e) % 2)
        g_all[SIDE + p, rows] = jnp.where(live, grads, jnp.zeros((HALF, WIDTH), BF16))


class Keys:
    def __init__(self, video, text, text_at):
        self.video, self.text, self.text_rows = video, text, slice(text_at, text_at + HALF)

    def rows(self, is_text, which, c):
        return self.text[which][self.text_rows, c] if is_text else self.video[which][:BLOCK, c]


def near_keys(video_refs, text_refs):
    return [Keys((v.at[0], v.at[1]), (t.at[0], t.at[1]), 0) for v, t in zip(video_refs, text_refs)]


def far_keys(refs):
    return [Keys(refs, refs, BLOCK)]


def joined(kv, which, c):
    return jnp.concatenate([block.rows(False, which, c) for block in kv], 0)


def loop(count, step):
    lax.fori_loop(0, count, lambda n, c: (step(n), c)[1], 0)


def chosen(blocks, n):
    return sum(jnp.where(n == m, block, 0) for m, block in enumerate(blocks))


def text_keys(labels, blocks, queries, visit):
    for n, block in enumerate(blocks):
        shot = labels.key_shot(block)
        begin, end = labels.span(shot)

        def step(m, n=n, shot=shot, begin=begin, end=end):
            j = queries[0] if len(queries) == 1 else chosen(queries, m)
            base = labels.query_base(j)

            @pl.when(jnp.logical_and(begin < base + BLOCK, end > base))
            def _():
                row = base + lax.broadcasted_iota(jnp.int32, (1, BLOCK), 1)
                same = jnp.logical_and(row >= begin, row < end)
                visit(n, j, jnp.logical_and(labels.live(shot, labels.y % 2), same))

        loop(len(queries), step)


def own_text(labels, n, visit):
    live = labels.live(labels.key_shot(0), labels.y % 2)
    visit(n, SIDE, jnp.broadcast_to(live, (HALF, BLOCK)))


def text_queries(labels, blocks, pairs, visit):
    for n, block in enumerate(blocks):
        base = labels.key_base(block)

        def step(p, n=n, base=base):
            begin, end = labels.span(labels.query_shot(p))

            @pl.when(jnp.logical_and(begin < base + BLOCK, end > base))
            def _():
                row = base + lax.broadcasted_iota(jnp.int32, (BLOCK, 1), 0)
                same = jnp.logical_and(row >= begin, row < end)
                visit(n, SIDE + p, jnp.broadcast_to(same, (BLOCK, BLOCK)))

        for p in pairs:
            step(p)


def head_ds(h):
    return pl.ds(pl.multiple_of(h * HDIM, HDIM), HDIM)


def rows_ds(j):
    return pl.ds(pl.multiple_of(j * BLOCK, BLOCK), BLOCK)


def query_cols(j):
    return slice(j * BLOCK, (j + 1) * BLOCK)


def video_stats(acc, q_all, g_all, kv, queries, fresh):
    def head(h):
        c, row = head_ds(h), pl.ds(h, 1)
        keys, values = joined(kv, 0, c), joined(kv, 1, c)
        for j in queries:
            cols = query_cols(j)
            scores = dot_nt(keys, q_all[j, :, c]) * TO_LOG2
            dprob = dot_nt(values, g_all[j, :, c])
            top = jnp.max(scores, axis=0, keepdims=True)
            if not fresh:
                before = acc[0, row, cols]
                top = jnp.maximum(before, top)
                shrink = jnp.exp2(before - top)
            weight = jnp.exp2(scores - top)
            total = jnp.sum(weight, axis=0, keepdims=True)
            weighted = jnp.sum(weight * dprob, axis=0, keepdims=True)
            if not fresh:
                total += acc[1, row, cols] * shrink
                weighted += acc[2, row, cols] * shrink
            acc[0, row, cols] = top
            acc[1, row, cols] = total
            acc[2, row, cols] = weighted

    loop(HEADS_LOCAL, head)


def visit_stats(acc, q_all, g_all, kv, is_text, n, j, mask):
    cols = rows_ds(j)
    results = []
    for h in range(HEADS_LOCAL):
        c = head_cols(h)
        scores = jnp.where(mask, dot_nt(kv[n].rows(is_text, 0, c), q_all[j, :, c]) * TO_LOG2, LOW)
        dprob = dot_nt(kv[n].rows(is_text, 1, c), g_all[j, :, c])
        before = acc[0, h : h + 1, cols]
        top = jnp.maximum(before, jnp.max(scores, axis=0, keepdims=True))
        floor = jnp.maximum(top, 0.5 * LOW)
        weight = jnp.exp2(scores - floor)
        shrink = jnp.exp2(before - floor)
        results.append(
            (
                top,
                acc[1, h : h + 1, cols] * shrink + jnp.sum(weight, axis=0, keepdims=True),
                acc[2, h : h + 1, cols] * shrink + jnp.sum(weight * dprob, axis=0, keepdims=True),
            )
        )
    for h in range(HEADS_LOCAL):
        for m in range(3):
            acc[m, h : h + 1, cols] = results[h][m]


NEAR = (0, 1, 3)
FAR = 2


def stats_first_kernel(length_ref, caption_ref, place_ref, *refs):
    kv, refs = near_keys(refs[:3], refs[3:6]), refs[6:]
    qg, text_qg, (acc, q_all, g_all) = refs[:3], refs[3:5], refs[5:]
    labels = Labels(length_ref, caption_ref, place_ref)
    for j, ref in zip(NEAR, qg):
        q_all[j] = ref[0]
        g_all[j] = ref[1]
    stage_text_queries(labels, 0, [(ref[0], ref[1]) for ref in text_qg], q_all, g_all)
    acc[0] = jnp.full((HEADS_LOCAL, ROWS), LOW, F32)
    acc[1:3] = jnp.zeros((2, HEADS_LOCAL, ROWS), F32)
    video_stats(acc, q_all, g_all, kv, NEAR, True)
    visit = functools.partial(visit_stats, acc, q_all, g_all, kv)
    text_keys(labels, NEAR, NEAR, functools.partial(visit, True))
    own_text(labels, 0, functools.partial(visit, True))
    text_queries(labels, NEAR, (0,), functools.partial(visit, False))


def stats_last_kernel(length_ref, caption_ref, place_ref, *refs):
    kv, far_kv = near_keys(refs[:3], refs[3:6]), far_keys(refs[6:8])
    acc_in, q_in, g_in, far_q, far_g, text_qg, out_ref, q_all, g_all, acc = refs[8:]
    labels = Labels(length_ref, caption_ref, place_ref)
    for j in range(SIDE + 1):
        q_all[j] = far_q[:BLOCK] if j == FAR else q_in[j]
        g_all[j] = far_g[:BLOCK] if j == FAR else g_in[j]
    stage_text_queries(labels, 1, [(far_q[BLOCK:], far_g[BLOCK:]), (text_qg[0], text_qg[1])], q_all, g_all)
    acc[...] = acc_in[...]
    video_stats(acc, q_all, g_all, kv, (FAR,), True)
    video_stats(acc, q_all, g_all, far_kv, range(SIDE), False)
    visit = functools.partial(visit_stats, acc, q_all, g_all)
    text_keys(labels, NEAR, (FAR,), functools.partial(visit, kv, True))
    text_keys(labels, (FAR,), tuple(range(SIDE)), functools.partial(visit, far_kv, True))
    text_queries(labels, NEAR, (1,), functools.partial(visit, kv, False))
    text_queries(labels, (FAR,), (0, 1), functools.partial(visit, far_kv, False))
    total = acc[1]
    some = total > 0.0
    total = jnp.where(some, total, 1.0)
    out_ref[0] = jnp.where(some, acc[0] + jnp.log2(total), LOW)
    out_ref[1] = acc[2] / total


def normalize(stats, norm):
    for j in range(SIDE + 2):
        parts = []
        for e in range(SIDE):
            if j < SIDE:
                parts.append([stats[e][n, :, query_cols(j ^ e)] for n in range(2)])
            else:
                halves = []
                for u in (2 * (j - SIDE), 2 * (j - SIDE) + 1):
                    at = VIDEO_ROWS + (u ^ e) * HALF
                    halves.append([stats[e][n, :, at : at + HALF] for n in range(2)])
                parts.append([jnp.concatenate([halves[0][n], halves[1][n]], 1) for n in range(2)])
        top = functools.reduce(jnp.maximum, [p[0] for p in parts])
        share = [jnp.exp2(p[0] - top) for p in parts]
        total = sum(share)
        delta = sum(p[1] * s for p, s in zip(parts, share)) / total
        norm[0, :, query_cols(j)] = top + jnp.log2(total)
        norm[1, :, query_cols(j)] = delta


class Terms:
    def __init__(self, refs):
        self.dk, self.dv, self.text_dk, self.text_dv = refs

    def clear(self):
        for ref in (self.dk, self.dv, self.text_dk, self.text_dv):
            ref[...] = jnp.zeros(ref.shape, F32)

    def write(self, n, out):
        rows = query_cols(n)
        for h in range(HEADS_LOCAL):
            c = head_cols(h)
            out[0, :BLOCK, c] = (self.dk[h, rows] * SCALE).astype(BF16)
            out[1, :BLOCK, c] = self.dv[h, rows].astype(BF16)
            out[0, BLOCK:, c] = (self.text_dk[n, h] * SCALE).astype(BF16)
            out[1, BLOCK:, c] = self.text_dv[n, h].astype(BF16)


def key_grads(labels, blocks, queries, pairs, q_all, g_all, kv, norm, dq_in, dq_t, terms, work):
    p_all, ds_all = work

    def head(h):
        c, row = head_ds(h), pl.ds(h, 1)
        keys, values = joined(kv, 0, c), joined(kv, 1, c)
        for n, j in enumerate(queries):
            cols, at = query_cols(j), query_cols(n)
            scores = dot_nt(keys, q_all[j, :, c])
            dprob = dot_nt(values, g_all[j, :, c])
            probs = jnp.exp2(scores * TO_LOG2 - norm[0, row, cols])
            p_all[:, at] = probs.astype(BF16)
            ds_all[:, at] = (probs * (dprob - norm[1, row, cols])).astype(BF16)
        terms.dv[h] += dot_nn(p_all[...], jnp.concatenate([g_all[j, :, c] for j in queries], 0))
        terms.dk[h] += dot_nn(ds_all[...], jnp.concatenate([q_all[j, :, c] for j in queries], 0))
        part = dot_nn(jnp.transpose(keys), ds_all[...])
        for n, j in enumerate(queries):
            cols, piece = query_cols(j), part[:, query_cols(n)]
            dq_t[h, :, cols] = piece if dq_in is None else dq_in[h, :, cols] + piece

    loop(HEADS_LOCAL, head)

    def visit(is_text, n, j, mask):
        cols = rows_ds(j)
        results = []
        for h in range(HEADS_LOCAL):
            c = head_cols(h)
            keys, queries, grads = kv[n].rows(is_text, 0, c), q_all[j, :, c], g_all[j, :, c]
            scores = dot_nt(keys, queries) * TO_LOG2
            dprob = dot_nt(kv[n].rows(is_text, 1, c), grads)
            probs = jnp.exp2(jnp.where(mask, scores, LOW) - norm[0, h : h + 1, cols])
            low = probs.astype(BF16)
            dscore = (probs * (dprob - norm[1, h : h + 1, cols])).astype(BF16)
            results.append((dot_nn(dscore, queries), dot_nn(low, grads), dot_nn(jnp.transpose(keys), dscore)))
        for h in range(HEADS_LOCAL):
            if is_text:
                terms.text_dk[n, h] += results[h][0]
                terms.text_dv[n, h] += results[h][1]
            else:
                terms.dk[h, query_cols(n)] += results[h][0]
                terms.dv[h, query_cols(n)] += results[h][1]
            dq_t[h, :, cols] += results[h][2]

    visit_text = functools.partial(visit, True)
    text_keys(labels, blocks, queries, visit_text)
    if 0 in blocks and 0 in pairs:
        own_text(labels, blocks.index(0), visit_text)
    text_queries(labels, blocks, pairs, functools.partial(visit, False))


def write_queries(dq_t, j, out):
    out[:, :, :BLOCK] = (dq_t[:, :, query_cols(j)] * SCALE).astype(BF16)
    out[:, :, BLOCK:] = (dq_t[:, :, VIDEO_ROWS + j * HALF : VIDEO_ROWS + (j + 1) * HALF] * SCALE).astype(BF16)


ALL = (0, 1, 2, 3)


def grads_far_kernel(length_ref, caption_ref, place_ref, *refs):
    q_all, g_all, kv, stats = refs[0], refs[1], far_keys(refs[2:4]), refs[4 : SIDE + 4]
    dkv_out, dq_t, norm, *scratch = refs[SIDE + 4 :]
    labels = Labels(length_ref, caption_ref, place_ref)
    normalize(stats, norm)
    dq_t[:, :, VIDEO_ROWS:] = jnp.zeros((HEADS_LOCAL, HDIM, TEXT_ROWS), F32)
    terms = Terms(scratch[:4])
    terms.clear()
    key_grads(labels, (FAR,), ALL, (0, 1), q_all, g_all, kv, norm, None, dq_t, terms, scratch[4:])
    terms.write(0, dkv_out)


def grads_near_kernel(length_ref, caption_ref, place_ref, *refs):
    q_all, g_all, dq_in, norm = refs[:4]
    kv, own, refs = near_keys(refs[4:6], refs[6:8]), near_keys(refs[8:9], refs[9:10]), refs[10:]
    dkv_out, (dq_out, dq_t), own_terms, scratch = refs[:2], refs[2:4], Terms(refs[4:8]), refs[8:]
    labels = Labels(length_ref, caption_ref, place_ref)
    dq_t[:, :, VIDEO_ROWS:] = dq_in[:, :, VIDEO_ROWS:]
    terms = Terms(scratch[:4])
    terms.clear()
    own_terms.clear()
    key_grads(labels, (1, 3), ALL, (0, 1), q_all, g_all, kv, norm, dq_in, dq_t, terms, scratch[4:6])
    key_grads(labels, (0,), (FAR,), (1,), q_all, g_all, own, norm, dq_t, dq_t, own_terms, scratch[6:])
    for n in range(2):
        terms.write(n, dkv_out[n])
    write_queries(dq_t, FAR, dq_out)


def grads_own_kernel(length_ref, caption_ref, place_ref, *refs):
    q_all, g_all, dq_in, norm, kv, refs = *refs[:4], near_keys(refs[4:5], refs[5:6]), refs[6:]
    before, dq_out, dkv_out, dq_t, scratch = refs[:4], refs[4:7], refs[7], refs[8], refs[9:]
    labels = Labels(length_ref, caption_ref, place_ref)
    dq_t[:, :, VIDEO_ROWS:] = dq_in[:, :, VIDEO_ROWS:]
    terms = Terms(scratch[:4])
    for ref, source in zip(scratch[:4], before):
        ref[...] = source[...]
    key_grads(labels, (0,), NEAR, (0,), q_all, g_all, kv, norm, dq_in, dq_t, terms, scratch[4:])
    for n, j in enumerate(NEAR):
        write_queries(dq_t, j, dq_out[n])
    terms.write(0, dkv_out)


SMEM_SPEC = pl.BlockSpec(memory_space=pltpu.SMEM)
VMEM_SPEC = pl.BlockSpec(memory_space=pltpu.VMEM)
PARAMS = pltpu.CompilerParams(vmem_limit_bytes=VMEM_LIMIT)
SMALL = pltpu.CompilerParams(vmem_limit_bytes=8 * 1024 * 1024)
DQ_T = (HEADS_LOCAL, HDIM, ROWS)
STATS = (3, HEADS_LOCAL, ROWS)
STAGED_QUERIES = jax.ShapeDtypeStruct((SIDE + 2, BLOCK, WIDTH), BF16)
VIDEO_MESSAGE = jax.ShapeDtypeStruct((2, BLOCK, WIDTH), BF16)
HALF_MESSAGE = jax.ShapeDtypeStruct((BLOCK + HALF, WIDTH), BF16)
KEY_MESSAGE = jax.ShapeDtypeStruct((2, BLOCK + HALF, WIDTH), BF16)


def terms_shapes(count):
    return [(HEADS_LOCAL, count * BLOCK, HDIM)] * 2 + [(count, HEADS_LOCAL, HALF, HDIM)] * 2


def terms_scratch(count):
    return [pltpu.VMEM(shape, F32) for shape in terms_shapes(count)]


def work_scratch(count, queries):
    return [pltpu.VMEM((count * BLOCK, queries * BLOCK), BF16)] * 2


def placed(arrays, space=pltpu.VMEM):
    return [pltpu.with_memory_space_constraint(a, space) for a in arrays]


def cost(blocks, matmuls):
    pairs = HEADS_LOCAL * VIDEO_ROWS * BLOCK * blocks
    return pl.CostEstimate(flops=2 * HDIM * matmuls * pairs, bytes_accessed=8 * 1024 * 1024, transcendentals=pairs)


def stats_first_call(scalars, qg, kv, text_qg, text_kv):
    return pl.pallas_call(
        stats_first_kernel,
        in_specs=[SMEM_SPEC] * 3 + [VMEM_SPEC] * 11,
        out_specs=[VMEM_SPEC] * 3,
        out_shape=[jax.ShapeDtypeStruct(STATS, F32), STAGED_QUERIES, STAGED_QUERIES],
        compiler_params=PARAMS,
        cost_estimate=cost(3, 2),
        name="stats_first",
    )(
        *scalars,
        *placed([kv[i] for i in NEAR]),
        *placed([*[text_kv[i] for i in NEAR], *[qg[j] for j in NEAR], text_qg[0], text_qg[1]], pltpu.HBM),
    )


def stats_last_call(scalars, acc, queries, qg, kv, text_qg, text_kv):
    return pl.pallas_call(
        stats_last_kernel,
        in_specs=[SMEM_SPEC] * 3 + [VMEM_SPEC] * 14,
        out_specs=[VMEM_SPEC] * 3,
        out_shape=[jax.ShapeDtypeStruct((2, HEADS_LOCAL, ROWS), F32), STAGED_QUERIES, STAGED_QUERIES],
        scratch_shapes=[pltpu.VMEM(STATS, F32)],
        compiler_params=PARAMS,
        cost_estimate=cost(2, 2),
        name="stats_last",
    )(
        *scalars,
        *placed([kv[i] for i in NEAR]),
        *placed([text_kv[i] for i in NEAR], pltpu.HBM),
        *placed([*kv[FAR], acc, *queries, *qg[FAR]]),
        *placed([text_qg[3]], pltpu.HBM),
    )


DQ_MESSAGE = jax.ShapeDtypeStruct((HEADS_LOCAL, HDIM, BLOCK + HALF), BF16)


def grads_far_call(scalars, queries, kv, stats):
    return pl.pallas_call(
        grads_far_kernel,
        in_specs=[SMEM_SPEC] * 3 + [VMEM_SPEC] * (4 + SIDE),
        out_specs=[VMEM_SPEC] * 3,
        out_shape=[KEY_MESSAGE, jax.ShapeDtypeStruct(DQ_T, F32), jax.ShapeDtypeStruct((2, HEADS_LOCAL, ROWS), F32)],
        scratch_shapes=terms_scratch(1) + work_scratch(1, SIDE),
        compiler_params=PARAMS,
        cost_estimate=cost(1, 5),
        name="grads_far",
    )(*scalars, *placed([*queries, *kv[FAR], *stats]))


def grads_near_call(scalars, queries, dq_t, norm, kv, text_kv):
    out = pl.pallas_call(
        grads_near_kernel,
        in_specs=[SMEM_SPEC] * 3 + [VMEM_SPEC] * 10,
        out_specs=[VMEM_SPEC] * 8,
        out_shape=[KEY_MESSAGE] * 2
        + [DQ_MESSAGE, jax.ShapeDtypeStruct(DQ_T, F32)]
        + [jax.ShapeDtypeStruct(shape, F32) for shape in terms_shapes(1)],
        scratch_shapes=terms_scratch(2) + work_scratch(2, SIDE) + work_scratch(1, 1),
        compiler_params=PARAMS,
        cost_estimate=cost(2, 5),
        name="grads_near",
    )(
        *scalars,
        *placed(queries),
        dq_t,
        *placed([norm, kv[1], kv[3]]),
        *placed([text_kv[1], text_kv[3]], pltpu.HBM),
        *placed([kv[0]]),
        *placed([text_kv[0]], pltpu.HBM),
    )
    return out[:2], out[2], out[3], out[4:]


def grads_own_call(scalars, queries, dq_t, norm, kv, text_kv, terms):
    out = pl.pallas_call(
        grads_own_kernel,
        in_specs=[SMEM_SPEC] * 3 + [VMEM_SPEC] * 10,
        out_specs=[VMEM_SPEC] * 4,
        out_shape=[DQ_MESSAGE] * 3 + [KEY_MESSAGE],
        scratch_shapes=[pltpu.VMEM(DQ_T, F32)] + terms_scratch(1) + work_scratch(1, 3),
        compiler_params=PARAMS,
        cost_estimate=cost(1, 5),
        name="grads_own",
    )(*scalars, *placed(queries), dq_t, *placed([norm, kv[0]]), *placed([text_kv[0]], pltpu.HBM), *terms)
    return out[:3], out[3]


def swap(array, axis, step):
    shift = step if axis == "y" else step * SIDE
    return lax.ppermute(array, "seq", [(i, i ^ shift) for i in range(SIDE * SIDE)])


def gathered(array, axis):
    return [array] + [swap(array, axis, step) for step in range(1, SIDE)]


def on_device(
    video_query,
    video_key,
    video_value,
    video_grad,
    text_query,
    text_key,
    text_value,
    text_grad,
    shot_length,
    caption_length,
):
    place = lax.axis_index("seq").astype(jnp.int32)
    scalars = (shot_length, caption_length, place.reshape(1))
    packed, text_qg, text_kv = pack(
        video_query, video_key, video_value, video_grad, text_query, text_grad, text_key, text_value
    )
    text_qg = {0: text_qg, 1: swap(text_qg, "y", 1), 3: swap(text_qg, "y", 3)}
    text_kv = {0: text_kv, 1: swap(text_kv, "z", 1), 3: swap(text_kv, "z", 3)}
    arrived = lax.all_to_all(packed, "head", split_axis=0, concat_axis=0)
    arrived, text_qg, text_kv = lax.optimization_barrier((arrived, text_qg, text_kv))
    qg, kv = assemble(arrived)
    qg1, qg3 = swap(qg, "y", 1), swap(qg, "y", 3)
    kv1, kv3 = swap(kv, "z", 1), swap(kv, "z", 3)
    q1, g3, k1, v3 = hand_on([qg1, qg3, kv1, kv3], [text_qg[1], text_qg[3], text_kv[1], text_kv[3]])
    qg = [qg, qg1, (swap(q1, "y", 3), swap(g3, "y", 1)), qg3]
    kv = [kv, kv1, (swap(k1, "z", 3), swap(v3, "z", 1)), kv3]

    acc, *queries = stats_first_call(scalars, qg, kv, text_qg, text_kv)
    stats, *queries = stats_last_call(scalars, acc, queries, qg, kv, text_qg, text_kv)
    stats = gathered(stats, "y")
    dkv2, dq_t, norm = grads_far_call(scalars, queries, kv, stats)
    (dkv1, dkv3), dq2, dq_t, terms = grads_near_call(scalars, queries, dq_t, norm, kv, text_kv)
    (dq0, dq1, dq3), dkv0 = grads_own_call(scalars, queries, dq_t, norm, kv, text_kv, terms)

    dkv2, dq2 = swap(dkv2, "z", FAR), swap(dq2, "y", FAR)
    dq1, dq3, dkv2, dq2 = lax.optimization_barrier((dq1, dq3, dkv2, dq2))
    dq = [dq0, swap(dq1, "y", 1), dq2, swap(dq3, "y", 3)]
    dkv = [dkv0, swap(dkv1, "z", 1), dkv2, swap(dkv3, "z", 3)]
    video, *text = sum_terms(dq, dkv)
    video_back = unpack(lax.all_to_all(video, "head", split_axis=0, concat_axis=0))
    return (*video_back, *text)


def solution(mesh):
    video = P(("seq", "head"), None)
    text = P("seq", "head")
    return jax.shard_map(
        on_device,
        mesh=mesh,
        in_specs=(video,) * 4 + (text,) * 4 + (P(), P()),
        out_specs=(video,) * 3 + (text,) * 3,
        check_vma=False,
    )
```

```python
import functools

import jax
import jax.numpy as jnp
from jax import lax
from jax.experimental import pallas as pl
from jax.experimental.pallas import tpu as pltpu
from jax.sharding import PartitionSpec as P

HDIM = 128
CAP = 256
NSHOT = 8
HEADS_LOCAL = 3
WIDTH = HEADS_LOCAL * HDIM
GROUP = 8
SIDE = 4
OWN = 32
BLOCK = GROUP * OWN
HALF = 128
VIDEO_ROWS = SIDE * BLOCK
TEXT_ROWS = SIDE * HALF
ROWS = VIDEO_ROWS + TEXT_ROWS
SCALE = HDIM ** (-0.5)
LOG2E = 1.4426950408889634
TO_LOG2 = SCALE * LOG2E
LOW = -1e30
F32 = jnp.float32
BF16 = jnp.bfloat16
VMEM_LIMIT = 16 * 1024 * 1024


def dot_nt(a, b):
    return lax.dot_general(a, b, (((1,), (1,)), ((), ())), preferred_element_type=F32)


def dot_nn(a, b):
    return lax.dot_general(a, b, (((1,), (0,)), ((), ())), preferred_element_type=F32)


def pack_kernel(q_ref, k_ref, v_ref, g_ref, tq_ref, tg_ref, tk_ref, tv_ref, out_ref, text_qg_ref, text_kv_ref):
    for d in range(GROUP):
        cols = slice(d * WIDTH, (d + 1) * WIDTH)
        for n, ref in enumerate((q_ref, g_ref, k_ref, v_ref)):
            out_ref[d, n] = ref[:, cols]
    text_qg_ref[0] = tq_ref[...]
    text_qg_ref[1] = tg_ref[...]
    text_kv_ref[0] = tk_ref[...]
    text_kv_ref[1] = tv_ref[...]


def pack(*arrays):
    video = jax.ShapeDtypeStruct((GROUP, 4, OWN, WIDTH), BF16)
    text = jax.ShapeDtypeStruct((2, HALF, WIDTH), BF16)
    call = pl.pallas_call(pack_kernel, out_shape=(video, text, text), compiler_params=SMALL, name="pack_inputs")
    return call(*placed(arrays, pltpu.HBM))


def assemble_kernel(in_ref, qg_ref, kv_ref):
    for n in range(2):
        qg_ref[n] = in_ref[:, n].reshape(BLOCK, WIDTH)
        kv_ref[n] = in_ref[:, 2 + n].reshape(BLOCK, WIDTH)


def assemble(arrived):
    return pl.pallas_call(
        assemble_kernel,
        out_shape=(VIDEO_MESSAGE, VIDEO_MESSAGE),
        compiler_params=SMALL,
        name="assemble_blocks",
    )(*placed([arrived]))


def hand_on_kernel(*refs):
    video, text, outs = refs[:4], refs[4:8], refs[8:]
    for n in range(4):
        outs[n][:BLOCK] = video[n][n % 2]
        outs[n][BLOCK:] = text[n][n % 2]


def hand_on(video, text):
    return pl.pallas_call(
        hand_on_kernel,
        out_shape=[HALF_MESSAGE] * 4,
        compiler_params=SMALL,
        name="hand_on",
    )(*placed(video), *placed(text, pltpu.HBM))


def unpack_kernel(in_ref, q_ref, k_ref, v_ref):
    for d in range(GROUP):
        cols = slice(d * WIDTH, (d + 1) * WIDTH)
        q_ref[:, cols] = in_ref[d, 0]
        k_ref[:, cols] = in_ref[d, 1]
        v_ref[:, cols] = in_ref[d, 2]


def unpack(arrived):
    shape = jax.ShapeDtypeStruct((OWN, GROUP * WIDTH), BF16)
    return pl.pallas_call(unpack_kernel, out_shape=(shape, shape, shape), compiler_params=SMALL, name="unpack_video")(*placed([arrived]))


def head_cols(h):
    return slice(h * HDIM, (h + 1) * HDIM)


def sum_kernel(*refs):
    dq, dkv = refs[:SIDE], refs[SIDE : 2 * SIDE]
    out, *text_out = refs[2 * SIDE :]
    for h in range(HEADS_LOCAL):
        total = jnp.transpose(sum(r[h].astype(F32) for r in dq).astype(BF16))
        out[:, 0, :, head_cols(h)] = total[:BLOCK].reshape(GROUP, OWN, HDIM)
        text_out[0][:, head_cols(h)] = total[BLOCK:]
    for n in range(2):
        total = sum(r[n].astype(F32) for r in dkv).astype(BF16)
        out[:, 1 + n] = total[:BLOCK].reshape(GROUP, OWN, WIDTH)
        text_out[1 + n][...] = total[BLOCK:]


def sum_terms(dq, dkv):
    return pl.pallas_call(
        sum_kernel,
        out_shape=[jax.ShapeDtypeStruct((GROUP, 3, OWN, WIDTH), BF16)]
        + [jax.ShapeDtypeStruct((HALF, WIDTH), BF16)] * 3,
        compiler_params=SMALL,
        name="sum_terms",
    )(*placed([*dq, *dkv]))


class Labels:
    def __init__(self, length_ref, caption_ref, place_ref):
        place = place_ref[0]
        self.z = place // SIDE
        self.y = place % SIDE
        self.caption_ref = caption_ref
        starts = [jnp.int32(0)]
        for s in range(NSHOT):
            starts.append(starts[-1] + length_ref[s])
        self.starts = starts

    def span(self, shot):
        begin = jnp.int32(0)
        end = jnp.int32(0)
        for s in range(NSHOT):
            begin = jnp.where(shot == s, self.starts[s], begin)
            end = jnp.where(shot == s, self.starts[s + 1], end)
        return begin, end

    def query_base(self, j):
        return (self.z * SIDE + (self.y ^ j)) * BLOCK

    def key_base(self, i):
        return ((self.z ^ i) * SIDE + self.y) * BLOCK

    def query_shot(self, p):
        return self.z * 2 + (self.y ^ (2 * p)) // 2

    def key_shot(self, t):
        return (self.z ^ t) * 2 + self.y // 2

    def live(self, shot, half):
        row = half * HALF + lax.broadcasted_iota(jnp.int32, (HALF, 1), 0)
        return row < self.caption_ref[shot]


def stage_text_queries(labels, p, parts, q_all, g_all):
    shot = labels.query_shot(p)
    for e, (queries, grads) in enumerate(parts):
        rows = slice(e * HALF, (e + 1) * HALF)
        q_all[SIDE + p, rows] = queries
        live = labels.live(shot, (labels.y ^ e) % 2)
        g_all[SIDE + p, rows] = jnp.where(live, grads, jnp.zeros((HALF, WIDTH), BF16))


class Keys:
    def __init__(self, video, text, text_at):
        self.video, self.text, self.text_rows = video, text, slice(text_at, text_at + HALF)

    def rows(self, is_text, which, c):
        return self.text[which][self.text_rows, c] if is_text else self.video[which][:BLOCK, c]


def near_keys(video_refs, text_refs):
    return [Keys((v.at[0], v.at[1]), (t.at[0], t.at[1]), 0) for v, t in zip(video_refs, text_refs)]


def far_keys(refs):
    return [Keys(refs, refs, BLOCK)]


def joined(kv, which, c):
    return jnp.concatenate([block.rows(False, which, c) for block in kv], 0)


def loop(count, step):
    lax.fori_loop(0, count, lambda n, c: (step(n), c)[1], 0)


def chosen(blocks, n):
    return sum(jnp.where(n == m, block, 0) for m, block in enumerate(blocks))


def text_keys(labels, blocks, queries, visit):
    for n, block in enumerate(blocks):
        shot = labels.key_shot(block)
        begin, end = labels.span(shot)

        def step(m, n=n, shot=shot, begin=begin, end=end):
            j = queries[0] if len(queries) == 1 else chosen(queries, m)
            base = labels.query_base(j)

            @pl.when(jnp.logical_and(begin < base + BLOCK, end > base))
            def _():
                row = base + lax.broadcasted_iota(jnp.int32, (1, BLOCK), 1)
                same = jnp.logical_and(row >= begin, row < end)
                visit(n, j, jnp.logical_and(labels.live(shot, labels.y % 2), same))

        loop(len(queries), step)


def own_text(labels, n, visit):
    live = labels.live(labels.key_shot(0), labels.y % 2)
    visit(n, SIDE, jnp.broadcast_to(live, (HALF, BLOCK)))


def text_queries(labels, blocks, pairs, visit):
    for n, block in enumerate(blocks):
        base = labels.key_base(block)

        def step(p, n=n, base=base):
            begin, end = labels.span(labels.query_shot(p))

            @pl.when(jnp.logical_and(begin < base + BLOCK, end > base))
            def _():
                row = base + lax.broadcasted_iota(jnp.int32, (BLOCK, 1), 0)
                same = jnp.logical_and(row >= begin, row < end)
                visit(n, SIDE + p, jnp.broadcast_to(same, (BLOCK, BLOCK)))

        for p in pairs:
            step(p)


def head_ds(h):
    return pl.ds(pl.multiple_of(h * HDIM, HDIM), HDIM)


def rows_ds(j):
    return pl.ds(pl.multiple_of(j * BLOCK, BLOCK), BLOCK)


def query_cols(j):
    return slice(j * BLOCK, (j + 1) * BLOCK)


def video_stats(acc, q_all, g_all, kv, queries, fresh):
    def head(h):
        c, row = head_ds(h), pl.ds(h, 1)
        keys, values = joined(kv, 0, c), joined(kv, 1, c)
        for j in queries:
            cols = query_cols(j)
            scores = dot_nt(keys, q_all[j, :, c]) * TO_LOG2
            dprob = dot_nt(values, g_all[j, :, c])
            top = jnp.max(scores, axis=0, keepdims=True)
            if not fresh:
                before = acc[0, row, cols]
                top = jnp.maximum(before, top)
                shrink = jnp.exp2(before - top)
            weight = jnp.exp2(scores - top)
            total = jnp.sum(weight, axis=0, keepdims=True)
            weighted = jnp.sum(weight * dprob, axis=0, keepdims=True)
            if not fresh:
                total += acc[1, row, cols] * shrink
                weighted += acc[2, row, cols] * shrink
            acc[0, row, cols] = top
            acc[1, row, cols] = total
            acc[2, row, cols] = weighted

    loop(HEADS_LOCAL, head)


def visit_stats(acc, q_all, g_all, kv, is_text, n, j, mask):
    cols = rows_ds(j)
    results = []
    for h in range(HEADS_LOCAL):
        c = head_cols(h)
        scores = jnp.where(mask, dot_nt(kv[n].rows(is_text, 0, c), q_all[j, :, c]) * TO_LOG2, LOW)
        dprob = dot_nt(kv[n].rows(is_text, 1, c), g_all[j, :, c])
        before = acc[0, h : h + 1, cols]
        top = jnp.maximum(before, jnp.max(scores, axis=0, keepdims=True))
        floor = jnp.maximum(top, 0.5 * LOW)
        weight = jnp.exp2(scores - floor)
        shrink = jnp.exp2(before - floor)
        results.append(
            (
                top,
                acc[1, h : h + 1, cols] * shrink + jnp.sum(weight, axis=0, keepdims=True),
                acc[2, h : h + 1, cols] * shrink + jnp.sum(weight * dprob, axis=0, keepdims=True),
            )
        )
    for h in range(HEADS_LOCAL):
        for m in range(3):
            acc[m, h : h + 1, cols] = results[h][m]


NEAR = (0, 1, 3)
FAR = 2


def stats_first_kernel(length_ref, caption_ref, place_ref, *refs):
    kv, refs = near_keys(refs[:3], refs[3:6]), refs[6:]
    qg, text_qg, (acc, q_all, g_all) = refs[:3], refs[3:5], refs[5:]
    labels = Labels(length_ref, caption_ref, place_ref)
    for j, ref in zip(NEAR, qg):
        q_all[j] = ref[0]
        g_all[j] = ref[1]
    stage_text_queries(labels, 0, [(ref[0], ref[1]) for ref in text_qg], q_all, g_all)
    acc[0] = jnp.full((HEADS_LOCAL, ROWS), LOW, F32)
    acc[1:3] = jnp.zeros((2, HEADS_LOCAL, ROWS), F32)
    video_stats(acc, q_all, g_all, kv, NEAR, True)
    visit = functools.partial(visit_stats, acc, q_all, g_all, kv)
    text_keys(labels, NEAR, NEAR, functools.partial(visit, True))
    own_text(labels, 0, functools.partial(visit, True))
    text_queries(labels, NEAR, (0,), functools.partial(visit, False))


def stats_last_kernel(length_ref, caption_ref, place_ref, *refs):
    kv, far_kv = near_keys(refs[:3], refs[3:6]), far_keys(refs[6:8])
    acc_in, q_in, g_in, far_q, far_g, text_qg, out_ref, q_all, g_all, acc = refs[8:]
    labels = Labels(length_ref, caption_ref, place_ref)
    for j in range(SIDE + 1):
        q_all[j] = far_q[:BLOCK] if j == FAR else q_in[j]
        g_all[j] = far_g[:BLOCK] if j == FAR else g_in[j]
    stage_text_queries(labels, 1, [(far_q[BLOCK:], far_g[BLOCK:]), (text_qg[0], text_qg[1])], q_all, g_all)
    acc[...] = acc_in[...]
    video_stats(acc, q_all, g_all, kv, (FAR,), True)
    video_stats(acc, q_all, g_all, far_kv, range(SIDE), False)
    visit = functools.partial(visit_stats, acc, q_all, g_all)
    text_keys(labels, NEAR, (FAR,), functools.partial(visit, kv, True))
    text_keys(labels, (FAR,), tuple(range(SIDE)), functools.partial(visit, far_kv, True))
    text_queries(labels, NEAR, (1,), functools.partial(visit, kv, False))
    text_queries(labels, (FAR,), (0, 1), functools.partial(visit, far_kv, False))
    total = acc[1]
    some = total > 0.0
    total = jnp.where(some, total, 1.0)
    out_ref[0] = jnp.where(some, acc[0] + jnp.log2(total), LOW)
    out_ref[1] = acc[2] / total


def normalize(stats, norm):
    for j in range(SIDE + 2):
        parts = []
        for e in range(SIDE):
            if j < SIDE:
                parts.append([stats[e][n, :, query_cols(j ^ e)] for n in range(2)])
            else:
                halves = []
                for u in (2 * (j - SIDE), 2 * (j - SIDE) + 1):
                    at = VIDEO_ROWS + (u ^ e) * HALF
                    halves.append([stats[e][n, :, at : at + HALF] for n in range(2)])
                parts.append([jnp.concatenate([halves[0][n], halves[1][n]], 1) for n in range(2)])
        top = functools.reduce(jnp.maximum, [p[0] for p in parts])
        share = [jnp.exp2(p[0] - top) for p in parts]
        total = sum(share)
        delta = sum(p[1] * s for p, s in zip(parts, share)) / total
        norm[0, :, query_cols(j)] = top + jnp.log2(total)
        norm[1, :, query_cols(j)] = delta


class Terms:
    def __init__(self, refs):
        self.dk, self.dv, self.text_dk, self.text_dv = refs

    def clear(self):
        for ref in (self.dk, self.dv, self.text_dk, self.text_dv):
            ref[...] = jnp.zeros(ref.shape, F32)

    def write(self, n, out):
        rows = query_cols(n)
        for h in range(HEADS_LOCAL):
            c = head_cols(h)
            out[0, :BLOCK, c] = (self.dk[h, rows] * SCALE).astype(BF16)
            out[1, :BLOCK, c] = self.dv[h, rows].astype(BF16)
            out[0, BLOCK:, c] = (self.text_dk[n, h] * SCALE).astype(BF16)
            out[1, BLOCK:, c] = self.text_dv[n, h].astype(BF16)


def key_grads(labels, blocks, queries, pairs, q_all, g_all, kv, norm, dq_in, dq_t, terms, work):
    p_all, ds_all = work

    def head(h):
        c, row = head_ds(h), pl.ds(h, 1)
        keys, values = joined(kv, 0, c), joined(kv, 1, c)
        for n, j in enumerate(queries):
            cols, at = query_cols(j), query_cols(n)
            scores = dot_nt(keys, q_all[j, :, c])
            dprob = dot_nt(values, g_all[j, :, c])
            probs = jnp.exp2(scores * TO_LOG2 - norm[0, row, cols])
            p_all[:, at] = probs.astype(BF16)
            ds_all[:, at] = (probs * (dprob - norm[1, row, cols])).astype(BF16)
        terms.dv[h] += dot_nn(p_all[...], jnp.concatenate([g_all[j, :, c] for j in queries], 0))
        terms.dk[h] += dot_nn(ds_all[...], jnp.concatenate([q_all[j, :, c] for j in queries], 0))
        part = dot_nn(jnp.transpose(keys), ds_all[...])
        for n, j in enumerate(queries):
            cols, piece = query_cols(j), part[:, query_cols(n)]
            dq_t[h, :, cols] = piece if dq_in is None else dq_in[h, :, cols] + piece

    loop(HEADS_LOCAL, head)

    def visit(is_text, n, j, mask):
        cols = rows_ds(j)
        results = []
        for h in range(HEADS_LOCAL):
            c = head_cols(h)
            keys, queries, grads = kv[n].rows(is_text, 0, c), q_all[j, :, c], g_all[j, :, c]
            scores = dot_nt(keys, queries) * TO_LOG2
            dprob = dot_nt(kv[n].rows(is_text, 1, c), grads)
            probs = jnp.exp2(jnp.where(mask, scores, LOW) - norm[0, h : h + 1, cols])
            low = probs.astype(BF16)
            dscore = (probs * (dprob - norm[1, h : h + 1, cols])).astype(BF16)
            results.append((dot_nn(dscore, queries), dot_nn(low, grads), dot_nn(jnp.transpose(keys), dscore)))
        for h in range(HEADS_LOCAL):
            if is_text:
                terms.text_dk[n, h] += results[h][0]
                terms.text_dv[n, h] += results[h][1]
            else:
                terms.dk[h, query_cols(n)] += results[h][0]
                terms.dv[h, query_cols(n)] += results[h][1]
            dq_t[h, :, cols] += results[h][2]

    visit_text = functools.partial(visit, True)
    text_keys(labels, blocks, queries, visit_text)
    if 0 in blocks and 0 in pairs:
        own_text(labels, blocks.index(0), visit_text)
    text_queries(labels, blocks, pairs, functools.partial(visit, False))


def write_queries(dq_t, j, out):
    out[:, :, :BLOCK] = (dq_t[:, :, query_cols(j)] * SCALE).astype(BF16)
    out[:, :, BLOCK:] = (dq_t[:, :, VIDEO_ROWS + j * HALF : VIDEO_ROWS + (j + 1) * HALF] * SCALE).astype(BF16)


ALL = (0, 1, 2, 3)


def grads_far_kernel(length_ref, caption_ref, place_ref, *refs):
    q_all, g_all, kv, stats = refs[0], refs[1], far_keys(refs[2:4]), refs[4 : SIDE + 4]
    dkv_out, dq_t, norm, *scratch = refs[SIDE + 4 :]
    labels = Labels(length_ref, caption_ref, place_ref)
    normalize(stats, norm)
    dq_t[:, :, VIDEO_ROWS:] = jnp.zeros((HEADS_LOCAL, HDIM, TEXT_ROWS), F32)
    terms = Terms(scratch[:4])
    terms.clear()
    key_grads(labels, (FAR,), ALL, (0, 1), q_all, g_all, kv, norm, None, dq_t, terms, scratch[4:])
    terms.write(0, dkv_out)


def grads_near_kernel(length_ref, caption_ref, place_ref, *refs):
    q_all, g_all, dq_in, norm = refs[:4]
    kv, own, refs = near_keys(refs[4:6], refs[6:8]), near_keys(refs[8:9], refs[9:10]), refs[10:]
    dkv_out, (dq_out, dq_t), own_terms, scratch = refs[:2], refs[2:4], Terms(refs[4:8]), refs[8:]
    labels = Labels(length_ref, caption_ref, place_ref)
    dq_t[:, :, VIDEO_ROWS:] = dq_in[:, :, VIDEO_ROWS:]
    terms = Terms(scratch[:4])
    terms.clear()
    own_terms.clear()
    key_grads(labels, (1, 3), ALL, (0, 1), q_all, g_all, kv, norm, dq_in, dq_t, terms, scratch[4:6])
    key_grads(labels, (0,), (FAR,), (1,), q_all, g_all, own, norm, dq_t, dq_t, own_terms, scratch[6:])
    for n in range(2):
        terms.write(n, dkv_out[n])
    write_queries(dq_t, FAR, dq_out)


def grads_own_kernel(length_ref, caption_ref, place_ref, *refs):
    q_all, g_all, dq_in, norm, kv, refs = *refs[:4], near_keys(refs[4:5], refs[5:6]), refs[6:]
    before, dq_out, dkv_out, dq_t, scratch = refs[:4], refs[4:7], refs[7], refs[8], refs[9:]
    labels = Labels(length_ref, caption_ref, place_ref)
    dq_t[:, :, VIDEO_ROWS:] = dq_in[:, :, VIDEO_ROWS:]
    terms = Terms(scratch[:4])
    for ref, source in zip(scratch[:4], before):
        ref[...] = source[...]
    key_grads(labels, (0,), NEAR, (0,), q_all, g_all, kv, norm, dq_in, dq_t, terms, scratch[4:])
    for n, j in enumerate(NEAR):
        write_queries(dq_t, j, dq_out[n])
    terms.write(0, dkv_out)


SMEM_SPEC = pl.BlockSpec(memory_space=pltpu.SMEM)
VMEM_SPEC = pl.BlockSpec(memory_space=pltpu.VMEM)
PARAMS = pltpu.CompilerParams(vmem_limit_bytes=VMEM_LIMIT)
SMALL = pltpu.CompilerParams(vmem_limit_bytes=8 * 1024 * 1024)
DQ_T = (HEADS_LOCAL, HDIM, ROWS)
STATS = (3, HEADS_LOCAL, ROWS)
STAGED_QUERIES = jax.ShapeDtypeStruct((SIDE + 2, BLOCK, WIDTH), BF16)
VIDEO_MESSAGE = jax.ShapeDtypeStruct((2, BLOCK, WIDTH), BF16)
HALF_MESSAGE = jax.ShapeDtypeStruct((BLOCK + HALF, WIDTH), BF16)
KEY_MESSAGE = jax.ShapeDtypeStruct((2, BLOCK + HALF, WIDTH), BF16)


def kept(shapes):
    return [pltpu.VMEM(shape.shape, shape.dtype) for shape in shapes]


def terms_shapes(count):
    return [(HEADS_LOCAL, count * BLOCK, HDIM)] * 2 + [(count, HEADS_LOCAL, HALF, HDIM)] * 2


def terms_scratch(count):
    return [pltpu.VMEM(shape, F32) for shape in terms_shapes(count)]


def work_scratch(count, queries):
    return [pltpu.VMEM((count * BLOCK, queries * BLOCK), BF16)] * 2


def placed(arrays, space=pltpu.VMEM):
    return [pltpu.with_memory_space_constraint(a, space) for a in arrays]


def cost(blocks, matmuls):
    pairs = HEADS_LOCAL * VIDEO_ROWS * BLOCK * blocks
    return pl.CostEstimate(flops=2 * HDIM * matmuls * pairs, bytes_accessed=8 * 1024 * 1024, transcendentals=pairs)


def stats_first_call(scalars, qg, kv, text_qg, text_kv):
    return pl.pallas_call(
        stats_first_kernel,
        in_specs=[SMEM_SPEC] * 3 + [VMEM_SPEC] * 11,
        out_specs=[VMEM_SPEC] * 3,
        out_shape=kept([jax.ShapeDtypeStruct(STATS, F32), STAGED_QUERIES, STAGED_QUERIES]),
        compiler_params=PARAMS,
        cost_estimate=cost(3, 2),
        name="stats_first",
    )(
        *scalars,
        *placed([kv[i] for i in NEAR]),
        *placed([*[text_kv[i] for i in NEAR], *[qg[j] for j in NEAR], text_qg[0], text_qg[1]], pltpu.HBM),
    )


def stats_last_call(scalars, acc, queries, qg, kv, text_qg, text_kv):
    return pl.pallas_call(
        stats_last_kernel,
        in_specs=[SMEM_SPEC] * 3 + [VMEM_SPEC] * 14,
        out_specs=[VMEM_SPEC] * 3,
        out_shape=kept([jax.ShapeDtypeStruct((2, HEADS_LOCAL, ROWS), F32), STAGED_QUERIES, STAGED_QUERIES]),
        scratch_shapes=[pltpu.VMEM(STATS, F32)],
        compiler_params=PARAMS,
        cost_estimate=cost(2, 2),
        name="stats_last",
    )(
        *scalars,
        *placed([kv[i] for i in NEAR]),
        *placed([text_kv[i] for i in NEAR], pltpu.HBM),
        *placed([*kv[FAR], acc, *queries, *qg[FAR]]),
        *placed([text_qg[3]], pltpu.HBM),
    )


DQ_MESSAGE = jax.ShapeDtypeStruct((HEADS_LOCAL, HDIM, BLOCK + HALF), BF16)


def grads_far_call(scalars, queries, kv, stats):
    return pl.pallas_call(
        grads_far_kernel,
        in_specs=[SMEM_SPEC] * 3 + [VMEM_SPEC] * (4 + SIDE),
        out_specs=[VMEM_SPEC] * 3,
        out_shape=kept(
            [KEY_MESSAGE, jax.ShapeDtypeStruct(DQ_T, F32), jax.ShapeDtypeStruct((2, HEADS_LOCAL, ROWS), F32)]
        ),
        scratch_shapes=terms_scratch(1) + work_scratch(1, SIDE),
        compiler_params=PARAMS,
        cost_estimate=cost(1, 5),
        name="grads_far",
    )(*scalars, *placed([*queries, *kv[FAR], *stats]))


def grads_near_call(scalars, queries, dq_t, norm, kv, text_kv):
    out = pl.pallas_call(
        grads_near_kernel,
        in_specs=[SMEM_SPEC] * 3 + [VMEM_SPEC] * 10,
        out_specs=[VMEM_SPEC] * 8,
        out_shape=kept(
            [KEY_MESSAGE] * 2
            + [DQ_MESSAGE, jax.ShapeDtypeStruct(DQ_T, F32)]
            + [jax.ShapeDtypeStruct(shape, F32) for shape in terms_shapes(1)]
        ),
        scratch_shapes=terms_scratch(2) + work_scratch(2, SIDE) + work_scratch(1, 1),
        compiler_params=PARAMS,
        cost_estimate=cost(2, 5),
        name="grads_near",
    )(
        *scalars,
        *placed([*queries, dq_t, norm, kv[1], kv[3]]),
        *placed([text_kv[1], text_kv[3]], pltpu.HBM),
        *placed([kv[0]]),
        *placed([text_kv[0]], pltpu.HBM),
    )
    return out[:2], out[2], out[3], out[4:]


def grads_own_call(scalars, queries, dq_t, norm, kv, text_kv, terms):
    out = pl.pallas_call(
        grads_own_kernel,
        in_specs=[SMEM_SPEC] * 3 + [VMEM_SPEC] * 10,
        out_specs=[VMEM_SPEC] * 4,
        out_shape=kept([DQ_MESSAGE] * 3 + [KEY_MESSAGE]),
        scratch_shapes=[pltpu.VMEM(DQ_T, F32)] + terms_scratch(1) + work_scratch(1, 3),
        compiler_params=PARAMS,
        cost_estimate=cost(1, 5),
        name="grads_own",
    )(*scalars, *placed([*queries, dq_t, norm, kv[0]]), *placed([text_kv[0]], pltpu.HBM), *placed(terms))
    return out[:3], out[3]


def swap(array, axis, step):
    shift = step if axis == "y" else step * SIDE
    return lax.ppermute(array, "seq", [(i, i ^ shift) for i in range(SIDE * SIDE)])


def gathered(array, axis):
    return [array] + [swap(array, axis, step) for step in range(1, SIDE)]


def on_device(
    video_query,
    video_key,
    video_value,
    video_grad,
    text_query,
    text_key,
    text_value,
    text_grad,
    shot_length,
    caption_length,
):
    place = lax.axis_index("seq").astype(jnp.int32)
    scalars = (shot_length, caption_length, place.reshape(1))
    packed, text_qg, text_kv = pack(
        video_query, video_key, video_value, video_grad, text_query, text_grad, text_key, text_value
    )
    text_qg = {0: text_qg, 1: swap(text_qg, "y", 1), 3: swap(text_qg, "y", 3)}
    text_kv = {0: text_kv, 1: swap(text_kv, "z", 1), 3: swap(text_kv, "z", 3)}
    arrived = lax.all_to_all(packed, "head", split_axis=0, concat_axis=0)
    arrived, text_qg, text_kv = lax.optimization_barrier((arrived, text_qg, text_kv))
    qg, kv = assemble(arrived)
    qg1, qg3 = swap(qg, "y", 1), swap(qg, "y", 3)
    kv1, kv3 = swap(kv, "z", 1), swap(kv, "z", 3)
    q1, g3, k1, v3 = hand_on([qg1, qg3, kv1, kv3], [text_qg[1], text_qg[3], text_kv[1], text_kv[3]])
    qg = [qg, qg1, (swap(q1, "y", 3), swap(g3, "y", 1)), qg3]
    kv = [kv, kv1, (swap(k1, "z", 3), swap(v3, "z", 1)), kv3]

    acc, *queries = stats_first_call(scalars, qg, kv, text_qg, text_kv)
    stats, *queries = stats_last_call(scalars, acc, queries, qg, kv, text_qg, text_kv)
    stats = gathered(stats, "y")
    dkv2, dq_t, norm = grads_far_call(scalars, queries, kv, stats)
    (dkv1, dkv3), dq2, dq_t, terms = grads_near_call(scalars, queries, dq_t, norm, kv, text_kv)
    (dq0, dq1, dq3), dkv0 = grads_own_call(scalars, queries, dq_t, norm, kv, text_kv, terms)

    dkv2, dq2 = swap(dkv2, "z", FAR), swap(dq2, "y", FAR)
    dq1, dq3, dkv2, dq2 = lax.optimization_barrier((dq1, dq3, dkv2, dq2))
    dq = [dq0, swap(dq1, "y", 1), dq2, swap(dq3, "y", 3)]
    dkv = [dkv0, swap(dkv1, "z", 1), dkv2, swap(dkv3, "z", 3)]
    video, *text = sum_terms(dq, dkv)
    video_back = unpack(lax.all_to_all(video, "head", split_axis=0, concat_axis=0))
    return (*video_back, *text)


def solution(mesh):
    video = P(("seq", "head"), None)
    text = P("seq", "head")
    return jax.shard_map(
        on_device,
        mesh=mesh,
        in_specs=(video,) * 4 + (text,) * 4 + (P(), P()),
        out_specs=(video,) * 3 + (text,) * 3,
        check_vma=False,
    )
```

```python
import functools

import jax
import jax.numpy as jnp
from jax import lax
from jax.experimental import pallas as pl
from jax.experimental.pallas import tpu as pltpu
from jax.sharding import PartitionSpec as P

HDIM = 128
CAP = 256
NSHOT = 8
HEADS_LOCAL = 3
WIDTH = HEADS_LOCAL * HDIM
GROUP = 8
SIDE = 4
OWN = 32
BLOCK = GROUP * OWN
HALF = 128
VIDEO_ROWS = SIDE * BLOCK
TEXT_ROWS = SIDE * HALF
ROWS = VIDEO_ROWS + TEXT_ROWS
SCALE = HDIM ** (-0.5)
LOG2E = 1.4426950408889634
TO_LOG2 = SCALE * LOG2E
LOW = -1e30
F32 = jnp.float32
BF16 = jnp.bfloat16
VMEM_LIMIT = 16 * 1024 * 1024


def dot_nt(a, b):
    return lax.dot_general(a, b, (((1,), (1,)), ((), ())), preferred_element_type=F32)


def dot_nn(a, b):
    return lax.dot_general(a, b, (((1,), (0,)), ((), ())), preferred_element_type=F32)


def pack_kernel(q_ref, k_ref, v_ref, g_ref, tq_ref, tg_ref, tk_ref, tv_ref, out_ref, text_qg_ref, text_kv_ref):
    for d in range(GROUP):
        cols = slice(d * WIDTH, (d + 1) * WIDTH)
        for n, ref in enumerate((q_ref, g_ref, k_ref, v_ref)):
            out_ref[d, n] = ref[:, cols]
    text_qg_ref[0] = tq_ref[...]
    text_qg_ref[1] = tg_ref[...]
    text_kv_ref[0] = tk_ref[...]
    text_kv_ref[1] = tv_ref[...]


def pack(*arrays):
    video = jax.ShapeDtypeStruct((GROUP, 4, OWN, WIDTH), BF16)
    text = jax.ShapeDtypeStruct((2, HALF, WIDTH), BF16)
    call = pl.pallas_call(pack_kernel, out_shape=(video, text, text), compiler_params=SMALL, name="pack_inputs")
    return call(*placed(arrays, pltpu.HBM))


def assemble_kernel(in_ref, qg_ref, kv_ref):
    for n in range(2):
        qg_ref[n] = in_ref[:, n].reshape(BLOCK, WIDTH)
        kv_ref[n] = in_ref[:, 2 + n].reshape(BLOCK, WIDTH)


def assemble(arrived):
    return pl.pallas_call(
        assemble_kernel,
        out_shape=kept([VIDEO_MESSAGE, VIDEO_MESSAGE]),
        compiler_params=SMALL,
        name="assemble_blocks",
    )(*placed([arrived]))


def hand_on_kernel(*refs):
    video, text, outs = refs[:4], refs[4:8], refs[8:]
    for n in range(4):
        outs[n][:BLOCK] = video[n][n % 2]
        outs[n][BLOCK:] = text[n][n % 2]


def hand_on(video, text):
    return pl.pallas_call(
        hand_on_kernel,
        out_shape=kept([HALF_MESSAGE] * 4),
        compiler_params=SMALL,
        name="hand_on",
    )(*placed(video), *placed(text, pltpu.HBM))


def unpack_kernel(in_ref, q_ref, k_ref, v_ref):
    for d in range(GROUP):
        cols = slice(d * WIDTH, (d + 1) * WIDTH)
        q_ref[:, cols] = in_ref[d, 0]
        k_ref[:, cols] = in_ref[d, 1]
        v_ref[:, cols] = in_ref[d, 2]


def unpack(arrived):
    shape = jax.ShapeDtypeStruct((OWN, GROUP * WIDTH), BF16)
    return pl.pallas_call(unpack_kernel, out_shape=(shape, shape, shape), compiler_params=SMALL, name="unpack_video")(*placed([arrived]))


def head_cols(h):
    return slice(h * HDIM, (h + 1) * HDIM)


def sum_kernel(*refs):
    dq, dkv = refs[:SIDE], refs[SIDE : 2 * SIDE]
    out, *text_out = refs[2 * SIDE :]
    for h in range(HEADS_LOCAL):
        total = jnp.transpose(sum(r[h].astype(F32) for r in dq).astype(BF16))
        out[:, 0, :, head_cols(h)] = total[:BLOCK].reshape(GROUP, OWN, HDIM)
        text_out[0][:, head_cols(h)] = total[BLOCK:]
    for n in range(2):
        total = sum(r[n].astype(F32) for r in dkv).astype(BF16)
        out[:, 1 + n] = total[:BLOCK].reshape(GROUP, OWN, WIDTH)
        text_out[1 + n][...] = total[BLOCK:]


def sum_terms(dq, dkv):
    return pl.pallas_call(
        sum_kernel,
        out_shape=kept([jax.ShapeDtypeStruct((GROUP, 3, OWN, WIDTH), BF16)])
        + [jax.ShapeDtypeStruct((HALF, WIDTH), BF16)] * 3,
        compiler_params=SMALL,
        name="sum_terms",
    )(*placed([*dq, *dkv]))


class Labels:
    def __init__(self, length_ref, caption_ref, place_ref):
        place = place_ref[0]
        self.z = place // SIDE
        self.y = place % SIDE
        self.caption_ref = caption_ref
        starts = [jnp.int32(0)]
        for s in range(NSHOT):
            starts.append(starts[-1] + length_ref[s])
        self.starts = starts

    def span(self, shot):
        begin = jnp.int32(0)
        end = jnp.int32(0)
        for s in range(NSHOT):
            begin = jnp.where(shot == s, self.starts[s], begin)
            end = jnp.where(shot == s, self.starts[s + 1], end)
        return begin, end

    def query_base(self, j):
        return (self.z * SIDE + (self.y ^ j)) * BLOCK

    def key_base(self, i):
        return ((self.z ^ i) * SIDE + self.y) * BLOCK

    def query_shot(self, p):
        return self.z * 2 + (self.y ^ (2 * p)) // 2

    def key_shot(self, t):
        return (self.z ^ t) * 2 + self.y // 2

    def live(self, shot, half):
        row = half * HALF + lax.broadcasted_iota(jnp.int32, (HALF, 1), 0)
        return row < self.caption_ref[shot]


def stage_text_queries(labels, p, parts, q_all, g_all):
    shot = labels.query_shot(p)
    for e, (queries, grads) in enumerate(parts):
        rows = slice(e * HALF, (e + 1) * HALF)
        q_all[SIDE + p, rows] = queries
        live = labels.live(shot, (labels.y ^ e) % 2)
        g_all[SIDE + p, rows] = jnp.where(live, grads, jnp.zeros((HALF, WIDTH), BF16))


class Keys:
    def __init__(self, video, text, text_at):
        self.video, self.text, self.text_rows = video, text, slice(text_at, text_at + HALF)

    def rows(self, is_text, which, c):
        return self.text[which][self.text_rows, c] if is_text else self.video[which][:BLOCK, c]


def near_keys(video_refs, text_refs):
    return [Keys((v.at[0], v.at[1]), (t.at[0], t.at[1]), 0) for v, t in zip(video_refs, text_refs)]


def far_keys(refs):
    return [Keys(refs, refs, BLOCK)]


def joined(kv, which, c):
    return jnp.concatenate([block.rows(False, which, c) for block in kv], 0)


def loop(count, step):
    lax.fori_loop(0, count, lambda n, c: (step(n), c)[1], 0)


def chosen(blocks, n):
    return sum(jnp.where(n == m, block, 0) for m, block in enumerate(blocks))


def text_keys(labels, blocks, queries, visit):
    for n, block in enumerate(blocks):
        shot = labels.key_shot(block)
        begin, end = labels.span(shot)

        def step(m, n=n, shot=shot, begin=begin, end=end):
            j = queries[0] if len(queries) == 1 else chosen(queries, m)
            base = labels.query_base(j)

            @pl.when(jnp.logical_and(begin < base + BLOCK, end > base))
            def _():
                row = base + lax.broadcasted_iota(jnp.int32, (1, BLOCK), 1)
                same = jnp.logical_and(row >= begin, row < end)
                visit(n, j, jnp.logical_and(labels.live(shot, labels.y % 2), same))

        loop(len(queries), step)


def own_text(labels, n, visit):
    live = labels.live(labels.key_shot(0), labels.y % 2)
    visit(n, SIDE, jnp.broadcast_to(live, (HALF, BLOCK)))


def text_queries(labels, blocks, pairs, visit):
    for n, block in enumerate(blocks):
        base = labels.key_base(block)

        def step(p, n=n, base=base):
            begin, end = labels.span(labels.query_shot(p))

            @pl.when(jnp.logical_and(begin < base + BLOCK, end > base))
            def _():
                row = base + lax.broadcasted_iota(jnp.int32, (BLOCK, 1), 0)
                same = jnp.logical_and(row >= begin, row < end)
                visit(n, SIDE + p, jnp.broadcast_to(same, (BLOCK, BLOCK)))

        for p in pairs:
            step(p)


def head_ds(h):
    return pl.ds(pl.multiple_of(h * HDIM, HDIM), HDIM)


def rows_ds(j):
    return pl.ds(pl.multiple_of(j * BLOCK, BLOCK), BLOCK)


def query_cols(j):
    return slice(j * BLOCK, (j + 1) * BLOCK)


def video_stats(acc, q_all, g_all, kv, queries, fresh):
    def head(h):
        c, row = head_ds(h), pl.ds(h, 1)
        keys, values = joined(kv, 0, c), joined(kv, 1, c)
        for j in queries:
            cols = query_cols(j)
            scores = dot_nt(keys, q_all[j, :, c]) * TO_LOG2
            dprob = dot_nt(values, g_all[j, :, c])
            top = jnp.max(scores, axis=0, keepdims=True)
            if not fresh:
                before = acc[0, row, cols]
                top = jnp.maximum(before, top)
                shrink = jnp.exp2(before - top)
            weight = jnp.exp2(scores - top)
            total = jnp.sum(weight, axis=0, keepdims=True)
            weighted = jnp.sum(weight * dprob, axis=0, keepdims=True)
            if not fresh:
                total += acc[1, row, cols] * shrink
                weighted += acc[2, row, cols] * shrink
            acc[0, row, cols] = top
            acc[1, row, cols] = total
            acc[2, row, cols] = weighted

    loop(HEADS_LOCAL, head)


def visit_stats(acc, q_all, g_all, kv, is_text, n, j, mask):
    cols = rows_ds(j)
    results = []
    for h in range(HEADS_LOCAL):
        c = head_cols(h)
        scores = jnp.where(mask, dot_nt(kv[n].rows(is_text, 0, c), q_all[j, :, c]) * TO_LOG2, LOW)
        dprob = dot_nt(kv[n].rows(is_text, 1, c), g_all[j, :, c])
        before = acc[0, h : h + 1, cols]
        top = jnp.maximum(before, jnp.max(scores, axis=0, keepdims=True))
        floor = jnp.maximum(top, 0.5 * LOW)
        weight = jnp.exp2(scores - floor)
        shrink = jnp.exp2(before - floor)
        results.append(
            (
                top,
                acc[1, h : h + 1, cols] * shrink + jnp.sum(weight, axis=0, keepdims=True),
                acc[2, h : h + 1, cols] * shrink + jnp.sum(weight * dprob, axis=0, keepdims=True),
            )
        )
    for h in range(HEADS_LOCAL):
        for m in range(3):
            acc[m, h : h + 1, cols] = results[h][m]


NEAR = (0, 1, 3)
FAR = 2


def stats_first_kernel(length_ref, caption_ref, place_ref, *refs):
    kv, refs = near_keys(refs[:3], refs[3:6]), refs[6:]
    qg, text_qg, (acc, q_all, g_all) = refs[:3], refs[3:5], refs[5:]
    labels = Labels(length_ref, caption_ref, place_ref)
    for j, ref in zip(NEAR, qg):
        q_all[j] = ref[0]
        g_all[j] = ref[1]
    stage_text_queries(labels, 0, [(ref[0], ref[1]) for ref in text_qg], q_all, g_all)
    acc[0] = jnp.full((HEADS_LOCAL, ROWS), LOW, F32)
    acc[1:3] = jnp.zeros((2, HEADS_LOCAL, ROWS), F32)
    video_stats(acc, q_all, g_all, kv, NEAR, True)
    visit = functools.partial(visit_stats, acc, q_all, g_all, kv)
    text_keys(labels, NEAR, NEAR, functools.partial(visit, True))
    own_text(labels, 0, functools.partial(visit, True))
    text_queries(labels, NEAR, (0,), functools.partial(visit, False))


def stats_last_kernel(length_ref, caption_ref, place_ref, *refs):
    kv, far_kv = near_keys(refs[:3], refs[3:6]), far_keys(refs[6:8])
    acc_in, q_in, g_in, far_q, far_g, text_qg, out_ref, q_all, g_all, acc = refs[8:]
    labels = Labels(length_ref, caption_ref, place_ref)
    for j in range(SIDE + 1):
        q_all[j] = far_q[:BLOCK] if j == FAR else q_in[j]
        g_all[j] = far_g[:BLOCK] if j == FAR else g_in[j]
    stage_text_queries(labels, 1, [(far_q[BLOCK:], far_g[BLOCK:]), (text_qg[0], text_qg[1])], q_all, g_all)
    acc[...] = acc_in[...]
    video_stats(acc, q_all, g_all, kv, (FAR,), True)
    video_stats(acc, q_all, g_all, far_kv, range(SIDE), False)
    visit = functools.partial(visit_stats, acc, q_all, g_all)
    text_keys(labels, NEAR, (FAR,), functools.partial(visit, kv, True))
    text_keys(labels, (FAR,), tuple(range(SIDE)), functools.partial(visit, far_kv, True))
    text_queries(labels, NEAR, (1,), functools.partial(visit, kv, False))
    text_queries(labels, (FAR,), (0, 1), functools.partial(visit, far_kv, False))
    total = acc[1]
    some = total > 0.0
    total = jnp.where(some, total, 1.0)
    out_ref[0] = jnp.where(some, acc[0] + jnp.log2(total), LOW)
    out_ref[1] = acc[2] / total


def normalize(stats, norm):
    for j in range(SIDE + 2):
        parts = []
        for e in range(SIDE):
            if j < SIDE:
                parts.append([stats[e][n, :, query_cols(j ^ e)] for n in range(2)])
            else:
                halves = []
                for u in (2 * (j - SIDE), 2 * (j - SIDE) + 1):
                    at = VIDEO_ROWS + (u ^ e) * HALF
                    halves.append([stats[e][n, :, at : at + HALF] for n in range(2)])
                parts.append([jnp.concatenate([halves[0][n], halves[1][n]], 1) for n in range(2)])
        top = functools.reduce(jnp.maximum, [p[0] for p in parts])
        share = [jnp.exp2(p[0] - top) for p in parts]
        total = sum(share)
        delta = sum(p[1] * s for p, s in zip(parts, share)) / total
        norm[0, :, query_cols(j)] = top + jnp.log2(total)
        norm[1, :, query_cols(j)] = delta


class Terms:
    def __init__(self, refs):
        self.dk, self.dv, self.text_dk, self.text_dv = refs

    def clear(self):
        for ref in (self.dk, self.dv, self.text_dk, self.text_dv):
            ref[...] = jnp.zeros(ref.shape, F32)

    def write(self, n, out):
        rows = query_cols(n)
        for h in range(HEADS_LOCAL):
            c = head_cols(h)
            out[0, :BLOCK, c] = (self.dk[h, rows] * SCALE).astype(BF16)
            out[1, :BLOCK, c] = self.dv[h, rows].astype(BF16)
            out[0, BLOCK:, c] = (self.text_dk[n, h] * SCALE).astype(BF16)
            out[1, BLOCK:, c] = self.text_dv[n, h].astype(BF16)


def key_grads(labels, blocks, queries, pairs, q_all, g_all, kv, norm, dq_in, dq_t, terms, work):
    p_all, ds_all = work

    def head(h):
        c, row = head_ds(h), pl.ds(h, 1)
        keys, values = joined(kv, 0, c), joined(kv, 1, c)
        for n, j in enumerate(queries):
            cols, at = query_cols(j), query_cols(n)
            scores = dot_nt(keys, q_all[j, :, c])
            dprob = dot_nt(values, g_all[j, :, c])
            probs = jnp.exp2(scores * TO_LOG2 - norm[0, row, cols])
            p_all[:, at] = probs.astype(BF16)
            ds_all[:, at] = (probs * (dprob - norm[1, row, cols])).astype(BF16)
        terms.dv[h] += dot_nn(p_all[...], jnp.concatenate([g_all[j, :, c] for j in queries], 0))
        terms.dk[h] += dot_nn(ds_all[...], jnp.concatenate([q_all[j, :, c] for j in queries], 0))
        part = dot_nn(jnp.transpose(keys), ds_all[...])
        for n, j in enumerate(queries):
            cols, piece = query_cols(j), part[:, query_cols(n)]
            dq_t[h, :, cols] = piece if dq_in is None else dq_in[h, :, cols] + piece

    loop(HEADS_LOCAL, head)

    def visit(is_text, n, j, mask):
        cols = rows_ds(j)
        results = []
        for h in range(HEADS_LOCAL):
            c = head_cols(h)
            keys, queries, grads = kv[n].rows(is_text, 0, c), q_all[j, :, c], g_all[j, :, c]
            scores = dot_nt(keys, queries) * TO_LOG2
            dprob = dot_nt(kv[n].rows(is_text, 1, c), grads)
            probs = jnp.exp2(jnp.where(mask, scores, LOW) - norm[0, h : h + 1, cols])
            low = probs.astype(BF16)
            dscore = (probs * (dprob - norm[1, h : h + 1, cols])).astype(BF16)
            results.append((dot_nn(dscore, queries), dot_nn(low, grads), dot_nn(jnp.transpose(keys), dscore)))
        for h in range(HEADS_LOCAL):
            if is_text:
                terms.text_dk[n, h] += results[h][0]
                terms.text_dv[n, h] += results[h][1]
            else:
                terms.dk[h, query_cols(n)] += results[h][0]
                terms.dv[h, query_cols(n)] += results[h][1]
            dq_t[h, :, cols] += results[h][2]

    visit_text = functools.partial(visit, True)
    text_keys(labels, blocks, queries, visit_text)
    if 0 in blocks and 0 in pairs:
        own_text(labels, blocks.index(0), visit_text)
    text_queries(labels, blocks, pairs, functools.partial(visit, False))


def write_queries(dq_t, j, out):
    out[:, :, :BLOCK] = (dq_t[:, :, query_cols(j)] * SCALE).astype(BF16)
    out[:, :, BLOCK:] = (dq_t[:, :, VIDEO_ROWS + j * HALF : VIDEO_ROWS + (j + 1) * HALF] * SCALE).astype(BF16)


ALL = (0, 1, 2, 3)


def grads_far_kernel(length_ref, caption_ref, place_ref, *refs):
    q_all, g_all, kv, stats = refs[0], refs[1], far_keys(refs[2:4]), refs[4 : SIDE + 4]
    dkv_out, dq_t, norm, *scratch = refs[SIDE + 4 :]
    labels = Labels(length_ref, caption_ref, place_ref)
    normalize(stats, norm)
    dq_t[:, :, VIDEO_ROWS:] = jnp.zeros((HEADS_LOCAL, HDIM, TEXT_ROWS), F32)
    terms = Terms(scratch[:4])
    terms.clear()
    key_grads(labels, (FAR,), ALL, (0, 1), q_all, g_all, kv, norm, None, dq_t, terms, scratch[4:])
    terms.write(0, dkv_out)


def grads_near_kernel(length_ref, caption_ref, place_ref, *refs):
    q_all, g_all, dq_in, norm = refs[:4]
    kv, own, refs = near_keys(refs[4:6], refs[6:8]), near_keys(refs[8:9], refs[9:10]), refs[10:]
    dkv_out, (dq_out, dq_t), own_terms, scratch = refs[:2], refs[2:4], Terms(refs[4:8]), refs[8:]
    labels = Labels(length_ref, caption_ref, place_ref)
    dq_t[:, :, VIDEO_ROWS:] = dq_in[:, :, VIDEO_ROWS:]
    terms = Terms(scratch[:4])
    terms.clear()
    own_terms.clear()
    key_grads(labels, (1, 3), ALL, (0, 1), q_all, g_all, kv, norm, dq_in, dq_t, terms, scratch[4:6])
    key_grads(labels, (0,), (FAR,), (1,), q_all, g_all, own, norm, dq_t, dq_t, own_terms, scratch[6:])
    for n in range(2):
        terms.write(n, dkv_out[n])
    write_queries(dq_t, FAR, dq_out)


def grads_own_kernel(length_ref, caption_ref, place_ref, *refs):
    q_all, g_all, dq_in, norm, kv, refs = *refs[:4], near_keys(refs[4:5], refs[5:6]), refs[6:]
    before, dq_out, dkv_out, dq_t, scratch = refs[:4], refs[4:7], refs[7], refs[8], refs[9:]
    labels = Labels(length_ref, caption_ref, place_ref)
    dq_t[:, :, VIDEO_ROWS:] = dq_in[:, :, VIDEO_ROWS:]
    terms = Terms(scratch[:4])
    for ref, source in zip(scratch[:4], before):
        ref[...] = source[...]
    key_grads(labels, (0,), NEAR, (0,), q_all, g_all, kv, norm, dq_in, dq_t, terms, scratch[4:])
    for n, j in enumerate(NEAR):
        write_queries(dq_t, j, dq_out[n])
    terms.write(0, dkv_out)


SMEM_SPEC = pl.BlockSpec(memory_space=pltpu.SMEM)
VMEM_SPEC = pl.BlockSpec(memory_space=pltpu.VMEM)
PARAMS = pltpu.CompilerParams(vmem_limit_bytes=VMEM_LIMIT)
SMALL = pltpu.CompilerParams(vmem_limit_bytes=8 * 1024 * 1024)
DQ_T = (HEADS_LOCAL, HDIM, ROWS)
STATS = (3, HEADS_LOCAL, ROWS)
STAGED_QUERIES = jax.ShapeDtypeStruct((SIDE + 2, BLOCK, WIDTH), BF16)
VIDEO_MESSAGE = jax.ShapeDtypeStruct((2, BLOCK, WIDTH), BF16)
HALF_MESSAGE = jax.ShapeDtypeStruct((BLOCK + HALF, WIDTH), BF16)
KEY_MESSAGE = jax.ShapeDtypeStruct((2, BLOCK + HALF, WIDTH), BF16)


def kept(shapes):
    return [pltpu.VMEM(shape.shape, shape.dtype) for shape in shapes]


def terms_shapes(count):
    return [(HEADS_LOCAL, count * BLOCK, HDIM)] * 2 + [(count, HEADS_LOCAL, HALF, HDIM)] * 2


def terms_scratch(count):
    return [pltpu.VMEM(shape, F32) for shape in terms_shapes(count)]


def work_scratch(count, queries):
    return [pltpu.VMEM((count * BLOCK, queries * BLOCK), BF16)] * 2


def placed(arrays, space=pltpu.VMEM):
    return [pltpu.with_memory_space_constraint(a, space) for a in arrays]


def cost(blocks, matmuls):
    pairs = HEADS_LOCAL * VIDEO_ROWS * BLOCK * blocks
    return pl.CostEstimate(flops=2 * HDIM * matmuls * pairs, bytes_accessed=8 * 1024 * 1024, transcendentals=pairs)


def stats_first_call(scalars, qg, kv, text_qg, text_kv):
    return pl.pallas_call(
        stats_first_kernel,
        in_specs=[SMEM_SPEC] * 3 + [VMEM_SPEC] * 11,
        out_specs=[VMEM_SPEC] * 3,
        out_shape=kept([jax.ShapeDtypeStruct(STATS, F32), STAGED_QUERIES, STAGED_QUERIES]),
        compiler_params=PARAMS,
        cost_estimate=cost(3, 2),
        name="stats_first",
    )(
        *scalars,
        *placed([kv[i] for i in NEAR]),
        *placed([*[text_kv[i] for i in NEAR], *[qg[j] for j in NEAR], text_qg[0], text_qg[1]], pltpu.HBM),
    )


def stats_last_call(scalars, acc, queries, qg, kv, text_qg, text_kv):
    return pl.pallas_call(
        stats_last_kernel,
        in_specs=[SMEM_SPEC] * 3 + [VMEM_SPEC] * 14,
        out_specs=[VMEM_SPEC] * 3,
        out_shape=kept([jax.ShapeDtypeStruct((2, HEADS_LOCAL, ROWS), F32), STAGED_QUERIES, STAGED_QUERIES]),
        scratch_shapes=[pltpu.VMEM(STATS, F32)],
        compiler_params=PARAMS,
        cost_estimate=cost(2, 2),
        name="stats_last",
    )(
        *scalars,
        *placed([kv[i] for i in NEAR]),
        *placed([text_kv[i] for i in NEAR], pltpu.HBM),
        *placed([*kv[FAR], acc, *queries, *qg[FAR]]),
        *placed([text_qg[3]], pltpu.HBM),
    )


DQ_MESSAGE = jax.ShapeDtypeStruct((HEADS_LOCAL, HDIM, BLOCK + HALF), BF16)


def grads_far_call(scalars, queries, kv, stats):
    return pl.pallas_call(
        grads_far_kernel,
        in_specs=[SMEM_SPEC] * 3 + [VMEM_SPEC] * (4 + SIDE),
        out_specs=[VMEM_SPEC] * 3,
        out_shape=kept(
            [KEY_MESSAGE, jax.ShapeDtypeStruct(DQ_T, F32), jax.ShapeDtypeStruct((2, HEADS_LOCAL, ROWS), F32)]
        ),
        scratch_shapes=terms_scratch(1) + work_scratch(1, SIDE),
        compiler_params=PARAMS,
        cost_estimate=cost(1, 5),
        name="grads_far",
    )(*scalars, *placed([*queries, *kv[FAR], *stats]))


def grads_near_call(scalars, queries, dq_t, norm, kv, text_kv):
    out = pl.pallas_call(
        grads_near_kernel,
        in_specs=[SMEM_SPEC] * 3 + [VMEM_SPEC] * 10,
        out_specs=[VMEM_SPEC] * 8,
        out_shape=kept(
            [KEY_MESSAGE] * 2
            + [DQ_MESSAGE, jax.ShapeDtypeStruct(DQ_T, F32)]
            + [jax.ShapeDtypeStruct(shape, F32) for shape in terms_shapes(1)]
        ),
        scratch_shapes=terms_scratch(2) + work_scratch(2, SIDE) + work_scratch(1, 1),
        compiler_params=PARAMS,
        cost_estimate=cost(2, 5),
        name="grads_near",
    )(
        *scalars,
        *placed([*queries, dq_t, norm, kv[1], kv[3]]),
        *placed([text_kv[1], text_kv[3]], pltpu.HBM),
        *placed([kv[0]]),
        *placed([text_kv[0]], pltpu.HBM),
    )
    return out[:2], out[2], out[3], out[4:]


def grads_own_call(scalars, queries, dq_t, norm, kv, text_kv, terms):
    out = pl.pallas_call(
        grads_own_kernel,
        in_specs=[SMEM_SPEC] * 3 + [VMEM_SPEC] * 10,
        out_specs=[VMEM_SPEC] * 4,
        out_shape=kept([DQ_MESSAGE] * 3 + [KEY_MESSAGE]),
        scratch_shapes=[pltpu.VMEM(DQ_T, F32)] + terms_scratch(1) + work_scratch(1, 3),
        compiler_params=PARAMS,
        cost_estimate=cost(1, 5),
        name="grads_own",
    )(*scalars, *placed([*queries, dq_t, norm, kv[0]]), *placed([text_kv[0]], pltpu.HBM), *placed(terms))
    return out[:3], out[3]


def swap(array, axis, step):
    shift = step if axis == "y" else step * SIDE
    return lax.ppermute(array, "seq", [(i, i ^ shift) for i in range(SIDE * SIDE)])


def gathered(array, axis):
    return [array] + [swap(array, axis, step) for step in range(1, SIDE)]


def on_device(
    video_query,
    video_key,
    video_value,
    video_grad,
    text_query,
    text_key,
    text_value,
    text_grad,
    shot_length,
    caption_length,
):
    place = lax.axis_index("seq").astype(jnp.int32)
    scalars = (shot_length, caption_length, place.reshape(1))
    packed, text_qg, text_kv = pack(
        video_query, video_key, video_value, video_grad, text_query, text_grad, text_key, text_value
    )
    text_qg = {0: text_qg, 1: swap(text_qg, "y", 1), 3: swap(text_qg, "y", 3)}
    text_kv = {0: text_kv, 1: swap(text_kv, "z", 1), 3: swap(text_kv, "z", 3)}
    arrived = lax.all_to_all(packed, "head", split_axis=0, concat_axis=0)
    arrived, text_qg, text_kv = lax.optimization_barrier((arrived, text_qg, text_kv))
    qg, kv = assemble(arrived)
    qg1, qg3 = swap(qg, "y", 1), swap(qg, "y", 3)
    kv1, kv3 = swap(kv, "z", 1), swap(kv, "z", 3)
    q1, g3, k1, v3 = hand_on([qg1, qg3, kv1, kv3], [text_qg[1], text_qg[3], text_kv[1], text_kv[3]])
    qg = [qg, qg1, (swap(q1, "y", 3), swap(g3, "y", 1)), qg3]
    kv = [kv, kv1, (swap(k1, "z", 3), swap(v3, "z", 1)), kv3]

    acc, *queries = stats_first_call(scalars, qg, kv, text_qg, text_kv)
    stats, *queries = stats_last_call(scalars, acc, queries, qg, kv, text_qg, text_kv)
    stats = gathered(stats, "y")
    dkv2, dq_t, norm = grads_far_call(scalars, queries, kv, stats)
    (dkv1, dkv3), dq2, dq_t, terms = grads_near_call(scalars, queries, dq_t, norm, kv, text_kv)
    (dq0, dq1, dq3), dkv0 = grads_own_call(scalars, queries, dq_t, norm, kv, text_kv, terms)

    dkv2, dq2 = swap(dkv2, "z", FAR), swap(dq2, "y", FAR)
    dq1, dq3, dkv2, dq2 = lax.optimization_barrier((dq1, dq3, dkv2, dq2))
    dq = [dq0, swap(dq1, "y", 1), dq2, swap(dq3, "y", 3)]
    dkv = [dkv0, swap(dkv1, "z", 1), dkv2, swap(dkv3, "z", 3)]
    video, *text = sum_terms(dq, dkv)
    video_back = unpack(lax.all_to_all(video, "head", split_axis=0, concat_axis=0))
    return (*video_back, *text)


def solution(mesh):
    video = P(("seq", "head"), None)
    text = P("seq", "head")
    return jax.shard_map(
        on_device,
        mesh=mesh,
        in_specs=(video,) * 4 + (text,) * 4 + (P(), P()),
        out_specs=(video,) * 3 + (text,) * 3,
        check_vma=False,
    )
```

```python
import functools

import jax
import jax.numpy as jnp
from jax import lax
from jax.experimental import pallas as pl
from jax.experimental.pallas import tpu as pltpu
from jax.sharding import PartitionSpec as P

HDIM = 128
CAP = 256
NSHOT = 8
HEADS_LOCAL = 3
WIDTH = HEADS_LOCAL * HDIM
GROUP = 8
SIDE = 4
OWN = 32
BLOCK = GROUP * OWN
HALF = 128
VIDEO_ROWS = SIDE * BLOCK
TEXT_ROWS = SIDE * HALF
ROWS = VIDEO_ROWS + TEXT_ROWS
SCALE = HDIM ** (-0.5)
LOG2E = 1.4426950408889634
TO_LOG2 = SCALE * LOG2E
LOW = -1e30
F32 = jnp.float32
BF16 = jnp.bfloat16
VMEM_LIMIT = 16 * 1024 * 1024


def dot_nt(a, b):
    return lax.dot_general(a, b, (((1,), (1,)), ((), ())), preferred_element_type=F32)


def dot_nn(a, b):
    return lax.dot_general(a, b, (((1,), (0,)), ((), ())), preferred_element_type=F32)


def pack_kernel(q_ref, k_ref, v_ref, g_ref, tq_ref, tg_ref, tk_ref, tv_ref, out_ref, text_qg_ref, text_kv_ref):
    for d in range(GROUP):
        cols = slice(d * WIDTH, (d + 1) * WIDTH)
        for n, ref in enumerate((q_ref, g_ref, k_ref, v_ref)):
            out_ref[d, n] = ref[:, cols]
    text_qg_ref[0] = tq_ref[...]
    text_qg_ref[1] = tg_ref[...]
    text_kv_ref[0] = tk_ref[...]
    text_kv_ref[1] = tv_ref[...]


def pack(*arrays):
    video = jax.ShapeDtypeStruct((GROUP, 4, OWN, WIDTH), BF16)
    text = jax.ShapeDtypeStruct((2, HALF, WIDTH), BF16)
    call = pl.pallas_call(pack_kernel, out_shape=(video, text, text), compiler_params=SMALL, name="pack_inputs")
    return call(*placed(arrays, pltpu.HBM))


def assemble_kernel(in_ref, qg_ref, kv_ref):
    for n in range(2):
        qg_ref[n] = in_ref[:, n].reshape(BLOCK, WIDTH)
        kv_ref[n] = in_ref[:, 2 + n].reshape(BLOCK, WIDTH)


def assemble(arrived):
    return pl.pallas_call(
        assemble_kernel,
        out_shape=kept([VIDEO_MESSAGE, VIDEO_MESSAGE]),
        compiler_params=SMALL,
        name="assemble_blocks",
    )(*placed([arrived]))


def hand_on_kernel(*refs):
    video, text, outs = refs[:4], refs[4:8], refs[8:]
    for n in range(4):
        outs[n][:BLOCK] = video[n][n % 2]
        outs[n][BLOCK:] = text[n][n % 2]


def hand_on(video, text):
    return pl.pallas_call(
        hand_on_kernel,
        out_shape=kept([HALF_MESSAGE] * 4),
        compiler_params=SMALL,
        name="hand_on",
    )(*placed(video), *placed(text, pltpu.HBM))


def unpack_kernel(in_ref, q_ref, k_ref, v_ref):
    for d in range(GROUP):
        cols = slice(d * WIDTH, (d + 1) * WIDTH)
        q_ref[:, cols] = in_ref[d, 0]
        k_ref[:, cols] = in_ref[d, 1]
        v_ref[:, cols] = in_ref[d, 2]


def unpack(arrived):
    shape = jax.ShapeDtypeStruct((OWN, GROUP * WIDTH), BF16)
    return pl.pallas_call(unpack_kernel, out_shape=(shape, shape, shape), compiler_params=SMALL, name="unpack_video")(*placed([arrived]))


def head_cols(h):
    return slice(h * HDIM, (h + 1) * HDIM)


def sum_kernel(*refs):
    dq, dkv = refs[:SIDE], refs[SIDE : 2 * SIDE]
    out, *text_out = refs[2 * SIDE :]
    for h in range(HEADS_LOCAL):
        total = jnp.transpose(sum(r[h].astype(F32) for r in dq).astype(BF16))
        out[:, 0, :, head_cols(h)] = total[:BLOCK].reshape(GROUP, OWN, HDIM)
        text_out[0][:, head_cols(h)] = total[BLOCK:]
    for n in range(2):
        total = sum(r[n].astype(F32) for r in dkv).astype(BF16)
        out[:, 1 + n] = total[:BLOCK].reshape(GROUP, OWN, WIDTH)
        text_out[1 + n][...] = total[BLOCK:]


def sum_terms(dq, dkv):
    return pl.pallas_call(
        sum_kernel,
        out_shape=kept([jax.ShapeDtypeStruct((GROUP, 3, OWN, WIDTH), BF16)])
        + [jax.ShapeDtypeStruct((HALF, WIDTH), BF16)] * 3,
        compiler_params=SMALL,
        name="sum_terms",
    )(*placed([*dq, *dkv]))


class Labels:
    def __init__(self, length_ref, caption_ref, place_ref):
        place = place_ref[0]
        self.z = place // SIDE
        self.y = place % SIDE
        self.caption_ref = caption_ref
        starts = [jnp.int32(0)]
        for s in range(NSHOT):
            starts.append(starts[-1] + length_ref[s])
        self.starts = starts

    def span(self, shot):
        begin = jnp.int32(0)
        end = jnp.int32(0)
        for s in range(NSHOT):
            begin = jnp.where(shot == s, self.starts[s], begin)
            end = jnp.where(shot == s, self.starts[s + 1], end)
        return begin, end

    def query_base(self, j):
        return (self.z * SIDE + (self.y ^ j)) * BLOCK

    def key_base(self, i):
        return ((self.z ^ i) * SIDE + self.y) * BLOCK

    def query_shot(self, p):
        return self.z * 2 + (self.y ^ (2 * p)) // 2

    def key_shot(self, t):
        return (self.z ^ t) * 2 + self.y // 2

    def live(self, shot, half):
        row = half * HALF + lax.broadcasted_iota(jnp.int32, (HALF, 1), 0)
        return row < self.caption_ref[shot]


def stage_text_queries(labels, p, parts, q_all, g_all):
    shot = labels.query_shot(p)
    for e, (queries, grads) in enumerate(parts):
        rows = slice(e * HALF, (e + 1) * HALF)
        q_all[SIDE + p, rows] = queries
        live = labels.live(shot, (labels.y ^ e) % 2)
        g_all[SIDE + p, rows] = jnp.where(live, grads, jnp.zeros((HALF, WIDTH), BF16))


class Keys:
    def __init__(self, video, text, text_at):
        self.video, self.text, self.text_rows = video, text, slice(text_at, text_at + HALF)

    def rows(self, is_text, which, c):
        return self.text[which][self.text_rows, c] if is_text else self.video[which][:BLOCK, c]


def near_keys(video_refs, text_refs):
    return [Keys((v.at[0], v.at[1]), (t.at[0], t.at[1]), 0) for v, t in zip(video_refs, text_refs)]


def far_keys(refs):
    return [Keys(refs, refs, BLOCK)]


def joined(kv, which, c):
    return jnp.concatenate([block.rows(False, which, c) for block in kv], 0)


def loop(count, step):
    lax.fori_loop(0, count, lambda n, c: (step(n), c)[1], 0)


def chosen(blocks, n):
    return sum(jnp.where(n == m, block, 0) for m, block in enumerate(blocks))


def text_keys(labels, blocks, queries, visit):
    for n, block in enumerate(blocks):
        shot = labels.key_shot(block)
        begin, end = labels.span(shot)

        def step(m, n=n, shot=shot, begin=begin, end=end):
            j = queries[0] if len(queries) == 1 else chosen(queries, m)
            base = labels.query_base(j)

            @pl.when(jnp.logical_and(begin < base + BLOCK, end > base))
            def _():
                row = base + lax.broadcasted_iota(jnp.int32, (1, BLOCK), 1)
                same = jnp.logical_and(row >= begin, row < end)
                visit(n, j, jnp.logical_and(labels.live(shot, labels.y % 2), same))

        loop(len(queries), step)


def own_text(labels, n, visit):
    live = labels.live(labels.key_shot(0), labels.y % 2)
    visit(n, SIDE, jnp.broadcast_to(live, (HALF, BLOCK)))


def text_queries(labels, blocks, pairs, visit):
    for n, block in enumerate(blocks):
        base = labels.key_base(block)

        def step(p, n=n, base=base):
            begin, end = labels.span(labels.query_shot(p))

            @pl.when(jnp.logical_and(begin < base + BLOCK, end > base))
            def _():
                row = base + lax.broadcasted_iota(jnp.int32, (BLOCK, 1), 0)
                same = jnp.logical_and(row >= begin, row < end)
                visit(n, SIDE + p, jnp.broadcast_to(same, (BLOCK, BLOCK)))

        for p in pairs:
            step(p)


def head_ds(h):
    return pl.ds(pl.multiple_of(h * HDIM, HDIM), HDIM)


def rows_ds(j):
    return pl.ds(pl.multiple_of(j * BLOCK, BLOCK), BLOCK)


def query_cols(j):
    return slice(j * BLOCK, (j + 1) * BLOCK)


def video_stats(acc, q_all, g_all, kv, queries, fresh):
    def head(h):
        c, row = head_ds(h), pl.ds(h, 1)
        keys, values = joined(kv, 0, c), joined(kv, 1, c)
        for j in queries:
            cols = query_cols(j)
            scores = dot_nt(keys, q_all[j, :, c]) * TO_LOG2
            dprob = dot_nt(values, g_all[j, :, c])
            top = jnp.max(scores, axis=0, keepdims=True)
            if not fresh:
                before = acc[0, row, cols]
                top = jnp.maximum(before, top)
                shrink = jnp.exp2(before - top)
            weight = jnp.exp2(scores - top)
            total = jnp.sum(weight, axis=0, keepdims=True)
            weighted = jnp.sum(weight * dprob, axis=0, keepdims=True)
            if not fresh:
                total += acc[1, row, cols] * shrink
                weighted += acc[2, row, cols] * shrink
            acc[0, row, cols] = top
            acc[1, row, cols] = total
            acc[2, row, cols] = weighted

    loop(HEADS_LOCAL, head)


def visit_stats(acc, q_all, g_all, kv, is_text, n, j, mask):
    cols = rows_ds(j)
    results = []
    for h in range(HEADS_LOCAL):
        c = head_cols(h)
        scores = jnp.where(mask, dot_nt(kv[n].rows(is_text, 0, c), q_all[j, :, c]) * TO_LOG2, LOW)
        dprob = dot_nt(kv[n].rows(is_text, 1, c), g_all[j, :, c])
        before = acc[0, h : h + 1, cols]
        top = jnp.maximum(before, jnp.max(scores, axis=0, keepdims=True))
        floor = jnp.maximum(top, 0.5 * LOW)
        weight = jnp.exp2(scores - floor)
        shrink = jnp.exp2(before - floor)
        results.append(
            (
                top,
                acc[1, h : h + 1, cols] * shrink + jnp.sum(weight, axis=0, keepdims=True),
                acc[2, h : h + 1, cols] * shrink + jnp.sum(weight * dprob, axis=0, keepdims=True),
            )
        )
    for h in range(HEADS_LOCAL):
        for m in range(3):
            acc[m, h : h + 1, cols] = results[h][m]


NEAR = (0, 1, 3)
FAR = 2


def stats_first_kernel(length_ref, caption_ref, place_ref, *refs):
    kv, refs = near_keys(refs[:3], refs[3:6]), refs[6:]
    qg, text_qg, (acc, q_all, g_all) = refs[:3], refs[3:5], refs[5:]
    labels = Labels(length_ref, caption_ref, place_ref)
    for j, ref in zip(NEAR, qg):
        q_all[j] = ref[0]
        g_all[j] = ref[1]
    stage_text_queries(labels, 0, [(ref[0], ref[1]) for ref in text_qg], q_all, g_all)
    acc[0] = jnp.full((HEADS_LOCAL, ROWS), LOW, F32)
    acc[1:3] = jnp.zeros((2, HEADS_LOCAL, ROWS), F32)
    video_stats(acc, q_all, g_all, kv, NEAR, True)
    visit = functools.partial(visit_stats, acc, q_all, g_all, kv)
    text_keys(labels, NEAR, NEAR, functools.partial(visit, True))
    own_text(labels, 0, functools.partial(visit, True))
    text_queries(labels, NEAR, (0,), functools.partial(visit, False))


def stats_last_kernel(length_ref, caption_ref, place_ref, *refs):
    kv, far_kv = near_keys(refs[:3], refs[3:6]), far_keys(refs[6:8])
    acc_in, q_in, g_in, far_q, far_g, text_qg, out_ref, q_all, g_all, acc = refs[8:]
    labels = Labels(length_ref, caption_ref, place_ref)
    for j in range(SIDE + 1):
        q_all[j] = far_q[:BLOCK] if j == FAR else q_in[j]
        g_all[j] = far_g[:BLOCK] if j == FAR else g_in[j]
    stage_text_queries(labels, 1, [(far_q[BLOCK:], far_g[BLOCK:]), (text_qg[0], text_qg[1])], q_all, g_all)
    acc[...] = acc_in[...]
    video_stats(acc, q_all, g_all, kv, (FAR,), True)
    video_stats(acc, q_all, g_all, far_kv, range(SIDE), False)
    visit = functools.partial(visit_stats, acc, q_all, g_all)
    text_keys(labels, NEAR, (FAR,), functools.partial(visit, kv, True))
    text_keys(labels, (FAR,), tuple(range(SIDE)), functools.partial(visit, far_kv, True))
    text_queries(labels, NEAR, (1,), functools.partial(visit, kv, False))
    text_queries(labels, (FAR,), (0, 1), functools.partial(visit, far_kv, False))
    total = acc[1]
    some = total > 0.0
    total = jnp.where(some, total, 1.0)
    out_ref[0] = jnp.where(some, acc[0] + jnp.log2(total), LOW)
    out_ref[1] = acc[2] / total


def normalize(stats, norm):
    for j in range(SIDE + 2):
        parts = []
        for e in range(SIDE):
            if j < SIDE:
                parts.append([stats[e][n, :, query_cols(j ^ e)] for n in range(2)])
            else:
                halves = []
                for u in (2 * (j - SIDE), 2 * (j - SIDE) + 1):
                    at = VIDEO_ROWS + (u ^ e) * HALF
                    halves.append([stats[e][n, :, at : at + HALF] for n in range(2)])
                parts.append([jnp.concatenate([halves[0][n], halves[1][n]], 1) for n in range(2)])
        top = functools.reduce(jnp.maximum, [p[0] for p in parts])
        share = [jnp.exp2(p[0] - top) for p in parts]
        total = sum(share)
        delta = sum(p[1] * s for p, s in zip(parts, share)) / total
        norm[0, :, query_cols(j)] = top + jnp.log2(total)
        norm[1, :, query_cols(j)] = delta


class Terms:
    def __init__(self, refs):
        self.dk, self.dv, self.text_dk, self.text_dv = refs

    def clear_text(self):
        for ref in (self.text_dk, self.text_dv):
            ref[...] = jnp.zeros(ref.shape, F32)

    def write(self, n, out):
        rows = query_cols(n)
        for h in range(HEADS_LOCAL):
            c = head_cols(h)
            out[0, :BLOCK, c] = (self.dk[h, rows] * SCALE).astype(BF16)
            out[1, :BLOCK, c] = self.dv[h, rows].astype(BF16)
            out[0, BLOCK:, c] = (self.text_dk[n, h] * SCALE).astype(BF16)
            out[1, BLOCK:, c] = self.text_dv[n, h].astype(BF16)


def key_grads(labels, blocks, queries, pairs, q_all, g_all, kv, norm, dq_in, dq_t, terms, work, before=None):
    p_all, ds_all = work

    def head(h):
        c, row = head_ds(h), pl.ds(h, 1)
        keys, values = joined(kv, 0, c), joined(kv, 1, c)
        for n, j in enumerate(queries):
            cols, at = query_cols(j), query_cols(n)
            scores = dot_nt(keys, q_all[j, :, c])
            dprob = dot_nt(values, g_all[j, :, c])
            probs = jnp.exp2(scores * TO_LOG2 - norm[0, row, cols])
            p_all[:, at] = probs.astype(BF16)
            ds_all[:, at] = (probs * (dprob - norm[1, row, cols])).astype(BF16)
        value_part = dot_nn(p_all[...], jnp.concatenate([g_all[j, :, c] for j in queries], 0))
        key_part = dot_nn(ds_all[...], jnp.concatenate([q_all[j, :, c] for j in queries], 0))
        terms.dv[h] = value_part if before is None else before.dv[h] + value_part
        terms.dk[h] = key_part if before is None else before.dk[h] + key_part
        part = dot_nn(jnp.transpose(keys), ds_all[...])
        for n, j in enumerate(queries):
            cols, piece = query_cols(j), part[:, query_cols(n)]
            dq_t[h, :, cols] = piece if dq_in is None else dq_in[h, :, cols] + piece

    loop(HEADS_LOCAL, head)

    def visit(is_text, n, j, mask):
        cols = rows_ds(j)
        results = []
        for h in range(HEADS_LOCAL):
            c = head_cols(h)
            keys, queries, grads = kv[n].rows(is_text, 0, c), q_all[j, :, c], g_all[j, :, c]
            scores = dot_nt(keys, queries) * TO_LOG2
            dprob = dot_nt(kv[n].rows(is_text, 1, c), grads)
            probs = jnp.exp2(jnp.where(mask, scores, LOW) - norm[0, h : h + 1, cols])
            low = probs.astype(BF16)
            dscore = (probs * (dprob - norm[1, h : h + 1, cols])).astype(BF16)
            results.append((dot_nn(dscore, queries), dot_nn(low, grads), dot_nn(jnp.transpose(keys), dscore)))
        for h in range(HEADS_LOCAL):
            if is_text:
                terms.text_dk[n, h] += results[h][0]
                terms.text_dv[n, h] += results[h][1]
            else:
                terms.dk[h, query_cols(n)] += results[h][0]
                terms.dv[h, query_cols(n)] += results[h][1]
            dq_t[h, :, cols] += results[h][2]

    visit_text = functools.partial(visit, True)
    text_keys(labels, blocks, queries, visit_text)
    if 0 in blocks and 0 in pairs:
        own_text(labels, blocks.index(0), visit_text)
    text_queries(labels, blocks, pairs, functools.partial(visit, False))


def write_queries(dq_t, j, out):
    out[:, :, :BLOCK] = (dq_t[:, :, query_cols(j)] * SCALE).astype(BF16)
    out[:, :, BLOCK:] = (dq_t[:, :, VIDEO_ROWS + j * HALF : VIDEO_ROWS + (j + 1) * HALF] * SCALE).astype(BF16)


ALL = (0, 1, 2, 3)


def grads_far_kernel(length_ref, caption_ref, place_ref, *refs):
    q_all, g_all, kv, stats = refs[0], refs[1], far_keys(refs[2:4]), refs[4 : SIDE + 4]
    dkv_out, dq_t, norm, *scratch = refs[SIDE + 4 :]
    labels = Labels(length_ref, caption_ref, place_ref)
    normalize(stats, norm)
    dq_t[:, :, VIDEO_ROWS:] = jnp.zeros((HEADS_LOCAL, HDIM, TEXT_ROWS), F32)
    terms = Terms(scratch[:4])
    terms.clear_text()
    key_grads(labels, (FAR,), ALL, (0, 1), q_all, g_all, kv, norm, None, dq_t, terms, scratch[4:])
    terms.write(0, dkv_out)


def grads_near_kernel(length_ref, caption_ref, place_ref, *refs):
    q_all, g_all, dq_in, norm = refs[:4]
    kv, own, refs = near_keys(refs[4:6], refs[6:8]), near_keys(refs[8:9], refs[9:10]), refs[10:]
    dkv_out, (dq_out, dq_t), own_terms, scratch = refs[:2], refs[2:4], Terms(refs[4:8]), refs[8:]
    labels = Labels(length_ref, caption_ref, place_ref)
    dq_t[:, :, VIDEO_ROWS:] = dq_in[:, :, VIDEO_ROWS:]
    terms = Terms(scratch[:4])
    terms.clear_text()
    own_terms.clear_text()
    key_grads(labels, (1, 3), ALL, (0, 1), q_all, g_all, kv, norm, dq_in, dq_t, terms, scratch[4:6])
    key_grads(labels, (0,), (FAR,), (1,), q_all, g_all, own, norm, dq_t, dq_t, own_terms, scratch[6:])
    for n in range(2):
        terms.write(n, dkv_out[n])
    write_queries(dq_t, FAR, dq_out)


def grads_own_kernel(length_ref, caption_ref, place_ref, *refs):
    q_all, g_all, dq_in, norm, kv, refs = *refs[:4], near_keys(refs[4:5], refs[5:6]), refs[6:]
    before, dq_out, dkv_out, dq_t, scratch = refs[:4], refs[4:7], refs[7], refs[8], refs[9:]
    labels = Labels(length_ref, caption_ref, place_ref)
    dq_t[:, :, VIDEO_ROWS:] = dq_in[:, :, VIDEO_ROWS:]
    terms = Terms(scratch[:4])
    before = Terms(before)
    terms.text_dk[...] = before.text_dk[...]
    terms.text_dv[...] = before.text_dv[...]
    key_grads(labels, (0,), NEAR, (0,), q_all, g_all, kv, norm, dq_in, dq_t, terms, scratch[4:], before)
    for n, j in enumerate(NEAR):
        write_queries(dq_t, j, dq_out[n])
    terms.write(0, dkv_out)


SMEM_SPEC = pl.BlockSpec(memory_space=pltpu.SMEM)
VMEM_SPEC = pl.BlockSpec(memory_space=pltpu.VMEM)
PARAMS = pltpu.CompilerParams(vmem_limit_bytes=VMEM_LIMIT)
SMALL = pltpu.CompilerParams(vmem_limit_bytes=8 * 1024 * 1024)
DQ_T = (HEADS_LOCAL, HDIM, ROWS)
STATS = (3, HEADS_LOCAL, ROWS)
STAGED_QUERIES = jax.ShapeDtypeStruct((SIDE + 2, BLOCK, WIDTH), BF16)
VIDEO_MESSAGE = jax.ShapeDtypeStruct((2, BLOCK, WIDTH), BF16)
HALF_MESSAGE = jax.ShapeDtypeStruct((BLOCK + HALF, WIDTH), BF16)
KEY_MESSAGE = jax.ShapeDtypeStruct((2, BLOCK + HALF, WIDTH), BF16)


def kept(shapes):
    return [pltpu.VMEM(shape.shape, shape.dtype) for shape in shapes]


def terms_shapes(count):
    return [(HEADS_LOCAL, count * BLOCK, HDIM)] * 2 + [(count, HEADS_LOCAL, HALF, HDIM)] * 2


def terms_scratch(count):
    return [pltpu.VMEM(shape, F32) for shape in terms_shapes(count)]


def work_scratch(count, queries):
    return [pltpu.VMEM((count * BLOCK, queries * BLOCK), BF16)] * 2


def placed(arrays, space=pltpu.VMEM):
    return [pltpu.with_memory_space_constraint(a, space) for a in arrays]


def cost(blocks, matmuls):
    pairs = HEADS_LOCAL * VIDEO_ROWS * BLOCK * blocks
    return pl.CostEstimate(flops=2 * HDIM * matmuls * pairs, bytes_accessed=8 * 1024 * 1024, transcendentals=pairs)


def stats_first_call(scalars, qg, kv, text_qg, text_kv):
    return pl.pallas_call(
        stats_first_kernel,
        in_specs=[SMEM_SPEC] * 3 + [VMEM_SPEC] * 11,
        out_specs=[VMEM_SPEC] * 3,
        out_shape=kept([jax.ShapeDtypeStruct(STATS, F32), STAGED_QUERIES, STAGED_QUERIES]),
        compiler_params=PARAMS,
        cost_estimate=cost(3, 2),
        name="stats_first",
    )(
        *scalars,
        *placed([kv[i] for i in NEAR]),
        *placed([*[text_kv[i] for i in NEAR], *[qg[j] for j in NEAR], text_qg[0], text_qg[1]], pltpu.HBM),
    )


def stats_last_call(scalars, acc, queries, qg, kv, text_qg, text_kv):
    return pl.pallas_call(
        stats_last_kernel,
        in_specs=[SMEM_SPEC] * 3 + [VMEM_SPEC] * 14,
        out_specs=[VMEM_SPEC] * 3,
        out_shape=kept([jax.ShapeDtypeStruct((2, HEADS_LOCAL, ROWS), F32), STAGED_QUERIES, STAGED_QUERIES]),
        scratch_shapes=[pltpu.VMEM(STATS, F32)],
        compiler_params=PARAMS,
        cost_estimate=cost(2, 2),
        name="stats_last",
    )(
        *scalars,
        *placed([kv[i] for i in NEAR]),
        *placed([text_kv[i] for i in NEAR], pltpu.HBM),
        *placed([*kv[FAR], acc, *queries, *qg[FAR]]),
        *placed([text_qg[3]], pltpu.HBM),
    )


DQ_MESSAGE = jax.ShapeDtypeStruct((HEADS_LOCAL, HDIM, BLOCK + HALF), BF16)


def grads_far_call(scalars, queries, kv, stats):
    return pl.pallas_call(
        grads_far_kernel,
        in_specs=[SMEM_SPEC] * 3 + [VMEM_SPEC] * (4 + SIDE),
        out_specs=[VMEM_SPEC] * 3,
        out_shape=kept(
            [KEY_MESSAGE, jax.ShapeDtypeStruct(DQ_T, F32), jax.ShapeDtypeStruct((2, HEADS_LOCAL, ROWS), F32)]
        ),
        scratch_shapes=terms_scratch(1) + work_scratch(1, SIDE),
        compiler_params=PARAMS,
        cost_estimate=cost(1, 5),
        name="grads_far",
    )(*scalars, *placed([*queries, *kv[FAR], *stats]))


def grads_near_call(scalars, queries, dq_t, norm, kv, text_kv):
    out = pl.pallas_call(
        grads_near_kernel,
        in_specs=[SMEM_SPEC] * 3 + [VMEM_SPEC] * 10,
        out_specs=[VMEM_SPEC] * 8,
        out_shape=kept(
            [KEY_MESSAGE] * 2
            + [DQ_MESSAGE, jax.ShapeDtypeStruct(DQ_T, F32)]
            + [jax.ShapeDtypeStruct(shape, F32) for shape in terms_shapes(1)]
        ),
        scratch_shapes=terms_scratch(2) + work_scratch(2, SIDE) + work_scratch(1, 1),
        compiler_params=PARAMS,
        cost_estimate=cost(2, 5),
        name="grads_near",
    )(
        *scalars,
        *placed([*queries, dq_t, norm, kv[1], kv[3]]),
        *placed([text_kv[1], text_kv[3]], pltpu.HBM),
        *placed([kv[0]]),
        *placed([text_kv[0]], pltpu.HBM),
    )
    return out[:2], out[2], out[3], out[4:]


def grads_own_call(scalars, queries, dq_t, norm, kv, text_kv, terms):
    out = pl.pallas_call(
        grads_own_kernel,
        in_specs=[SMEM_SPEC] * 3 + [VMEM_SPEC] * 10,
        out_specs=[VMEM_SPEC] * 4,
        out_shape=kept([DQ_MESSAGE] * 3 + [KEY_MESSAGE]),
        scratch_shapes=[pltpu.VMEM(DQ_T, F32)] + terms_scratch(1) + work_scratch(1, 3),
        compiler_params=PARAMS,
        cost_estimate=cost(1, 5),
        name="grads_own",
    )(*scalars, *placed([*queries, dq_t, norm, kv[0]]), *placed([text_kv[0]], pltpu.HBM), *placed(terms))
    return out[:3], out[3]


def swap(array, axis, step):
    shift = step if axis == "y" else step * SIDE
    return lax.ppermute(array, "seq", [(i, i ^ shift) for i in range(SIDE * SIDE)])


def gathered(array, axis):
    return [array] + [swap(array, axis, step) for step in range(1, SIDE)]


def on_device(
    video_query,
    video_key,
    video_value,
    video_grad,
    text_query,
    text_key,
    text_value,
    text_grad,
    shot_length,
    caption_length,
):
    place = lax.axis_index("seq").astype(jnp.int32)
    scalars = (shot_length, caption_length, place.reshape(1))
    packed, text_qg, text_kv = pack(
        video_query, video_key, video_value, video_grad, text_query, text_grad, text_key, text_value
    )
    text_qg = {0: text_qg, 1: swap(text_qg, "y", 1), 3: swap(text_qg, "y", 3)}
    text_kv = {0: text_kv, 1: swap(text_kv, "z", 1), 3: swap(text_kv, "z", 3)}
    arrived = lax.all_to_all(packed, "head", split_axis=0, concat_axis=0)
    arrived, text_qg, text_kv = lax.optimization_barrier((arrived, text_qg, text_kv))
    qg, kv = assemble(arrived)
    qg1, qg3 = swap(qg, "y", 1), swap(qg, "y", 3)
    kv1, kv3 = swap(kv, "z", 1), swap(kv, "z", 3)
    q1, g3, k1, v3 = hand_on([qg1, qg3, kv1, kv3], [text_qg[1], text_qg[3], text_kv[1], text_kv[3]])
    qg = [qg, qg1, (swap(q1, "y", 3), swap(g3, "y", 1)), qg3]
    kv = [kv, kv1, (swap(k1, "z", 3), swap(v3, "z", 1)), kv3]

    acc, *queries = stats_first_call(scalars, qg, kv, text_qg, text_kv)
    stats, *queries = stats_last_call(scalars, acc, queries, qg, kv, text_qg, text_kv)
    stats = gathered(stats, "y")
    dkv2, dq_t, norm = grads_far_call(scalars, queries, kv, stats)
    (dkv1, dkv3), dq2, dq_t, terms = grads_near_call(scalars, queries, dq_t, norm, kv, text_kv)
    (dq0, dq1, dq3), dkv0 = grads_own_call(scalars, queries, dq_t, norm, kv, text_kv, terms)

    dkv2, dq2 = swap(dkv2, "z", FAR), swap(dq2, "y", FAR)
    dq1, dq3, dkv2, dq2 = lax.optimization_barrier((dq1, dq3, dkv2, dq2))
    dq = [dq0, swap(dq1, "y", 1), dq2, swap(dq3, "y", 3)]
    dkv = [dkv0, swap(dkv1, "z", 1), dkv2, swap(dkv3, "z", 3)]
    video, *text = sum_terms(dq, dkv)
    video_back = unpack(lax.all_to_all(video, "head", split_axis=0, concat_axis=0))
    return (*video_back, *text)


def solution(mesh):
    video = P(("seq", "head"), None)
    text = P("seq", "head")
    return jax.shard_map(
        on_device,
        mesh=mesh,
        in_specs=(video,) * 4 + (text,) * 4 + (P(), P()),
        out_specs=(video,) * 3 + (text,) * 3,
        check_vma=False,
    )
```
